256 devices in a mesh: db: 16 (over y, x), head: 16 (over z, core).
Axes of the slice: x: 4, y: 4, z: 8, core: 2. Of those that a mesh axis runs over, the one named last changes fastest.
Arguments:
- tokens: bfloat16 [16384, 4096], P('db', 'head'), may hold values from -6 to 6
- query_weight: bfloat16 [4096, 4096], P(None, 'head'), may hold values from -0.09375 to 0.09375
- key_weight: bfloat16 [896, 4096], P(None, 'head'), may hold values from -0.1875 to 0.1875
- value_weight: bfloat16 [896, 4096], P(None, 'head'), may hold values from -0.1875 to 0.1875
- out_weight: bfloat16 [4096, 4096], P('head'), may hold values from -0.09375 to 0.09375
- codes: bfloat16 [128, 128, 896], P('db'), may hold values from -6 to 6
- scales: float32 [128, 7], P('db'), may hold values from 0.25 to 4
- block_len: int32 [128], P('db'), may hold values from 32 to 128
- nbr_owner: int32 [256, 2], P('db'), may hold values from 0 to 15, all different within a row; in each aligned block of 16 rows (0 to 15, 16 to 31, ...) at most 2 rows name the same one
- nbr_block: int32 [256, 2], P('db'), may hold values from 0 to 7
Outputs:
- cross_out: bfloat16 [16384, 4096], P('db', 'head')
The draws below stay inside these ranges and needn't reach their ends.
Inputs may be any that keep to these rules, and one draw needn't show every extreme that they name: `nbr_owner`: the 2 neighbours of a span lie on different shards; among the spans of one index of db at most 2 neighbours lie on any one shard, and in some index of db exactly 2 do.
All inputs are finite; a program needn't handle non-finite values.
Results may differ from the reference program's by a relative error of at most 0.011.
Values may be sent and summed in bfloat16 or wider, within the bound.
No kernel may reach another device: no remote copies, remote signals or barrier semaphores. Data moves between devices by JAX's collectives and lax.ppermute only.
A program may use at most 128 MiB of HBM per device.

```python
import math
import jax
import jax.numpy as jnp
import numpy as np
from jax import lax

D = 4096
HEADS = 32
HD = 128
ENC = 896
GROUP = 128
SPAN = 64
NBR_LEN = 128
NBRS = 2
NB_DEV = 8
C_DEV = 16
CAP = 2
TOKENS = 16384
SPANS = 256
NBLK = 128
N_DB = 16


def plant(values, stream_key, least, largest):
    longest = values.shape.index(max(values.shape))
    spots = []
    for shift in (0, 1):
        where = [jax.random.randint(jax.random.fold_in(stream_key, axis), (), 0, length) for axis, length in enumerate(values.shape)]
        where[longest] = (where[longest] + shift) % values.shape[longest]
        spots.append(tuple(where))
    return values.at[spots[0]].set(least).at[spots[1]].set(largest)


def level_of(stream_key, extent, shards, smallest, largest):
    def one(dim, parts):
        draws = jax.random.uniform(jax.random.fold_in(jax.random.fold_in(stream_key, 6), dim), (parts,), jnp.float32, smallest / len(shards), largest / len(shards))
        return jnp.repeat(jnp.exp(draws), extent[dim] // parts).reshape((-1,) + (1,) * (len(extent) - dim - 1))

    level = one(*shards[0])
    for cut in shards[1:]:
        level = level * one(*cut)
    return level


def routed_block(stream_key, own, number, rows, amount, top, most, slope):
    sequence = jax.random.permutation(stream_key, amount)
    packed, ordinary = load_shares(amount, rows * top, most, slope, True), load_shares(amount, rows * top, most, slope, False)
    places = jnp.arange(amount)

    def named(lengths, rotation):
        used = int((lengths > 0).sum())
        fixed = max(1, used // 4)
        moved = fixed + (places - fixed + rotation * (used - fixed)) % max(1, amount - fixed)
        return jnp.zeros((amount,), jnp.int32).at[sequence[jnp.where(places < fixed, places, moved)]].set(jnp.asarray(lengths, jnp.int32))

    lengths = jnp.where(number % 4 == 0, named(packed, number // 4), named(ordinary, number - number // 4 - 1))
    mixed = jax.random.permutation(jax.random.fold_in(own, 3), amount)
    donor, receiver = mixed[0:amount // 2 * 2:2], mixed[1:amount // 2 * 2:2]
    room = jnp.minimum(lengths[donor] - 1, most - lengths[receiver]) // 2
    room = jnp.where((donor == sequence[0]) | (receiver == sequence[0]) | (lengths[receiver] == 0), 0, jnp.maximum(room, 0))
    moved = jax.random.randint(jax.random.fold_in(own, 4), (amount // 2,), 0, 1 << 20) % (room + 1)
    lengths = lengths.at[donor].add(-moved).at[receiver].add(moved)
    labels = jnp.searchsorted(jnp.cumsum(lengths), jnp.arange(rows * top), side="right").astype(jnp.int32)
    grid = labels.reshape(top, rows).T
    grid = grid[jax.random.permutation(jax.random.fold_in(own, 1), rows)]
    rotation = jax.random.randint(jax.random.fold_in(own, 2), (rows, 1), 0, top)
    return jnp.take_along_axis(grid, (jnp.arange(top)[None, :] + rotation) % top, axis=1)


def load_shares(number_of, total, most, lean, full):
    portions = [(1 << 20) // math.isqrt(rank ** lean) + 1 for rank in range(1, number_of + 1)]
    largest = most if full else min(most, max(-(-total // number_of), total * portions[0] // sum(portions)))
    least = 1 if total - largest >= number_of - 1 else 0
    given, rest = [largest] + [least] * (number_of - 1), total - largest - least * (number_of - 1)
    while rest > 0:
        movable = [i for i in range(1, number_of) if given[i] < largest] or [i for i in range(1, number_of) if given[i] < most]
        whole, budget = sum([portions[i] for i in movable]), rest
        for i in movable:
            extra = min(most - given[i], max(1, budget * portions[i] // whole), rest)
            given[i] = given[i] + extra
            rest = rest - extra
    return np.array(given)


def gaussian(key, dims, width, bound, pieces=(), kind=jnp.bfloat16):
    array = width * jax.random.normal(key, dims, jnp.float32)
    if pieces:
        array = array * level_of(key, dims, pieces, -0.22, 0.18)
    return jnp.clip(array, -bound, bound).astype(kind)


def setup_inputs(seed: int = 0) -> dict:
    seeds = jax.random.split(jax.random.key(seed), 11)
    tokens = gaussian(seeds[0], (TOKENS, D), 1.0, 6.0, ((0, 16), (1, 16)))
    query_weight = gaussian(seeds[1], (D, D), D ** -0.5, 0.09375, ((1, 16),))
    key_weight = gaussian(seeds[2], (ENC, D), ENC ** -0.5, 0.1875, ((1, 16),))
    value_weight = gaussian(seeds[3], (ENC, D), ENC ** -0.5, 0.1875, ((1, 16),))
    out_weight = gaussian(seeds[4], (D, D), D ** -0.5, 0.09375, ((0, 16),))
    codes = gaussian(seeds[5], (NBLK, NBR_LEN, ENC), 1.0, 6.0, ((0, 16),))
    scales = jnp.clip(jnp.exp(math.log(4.0) - 2.7725887 * jax.random.uniform(seeds[6], (NBLK, ENC // GROUP), jnp.float32) ** level_of(seeds[6], (NBLK, ENC // GROUP), ((0, 16),), -0.2, 0.2)), 0.25, 4.0)
    block_len = plant(jax.random.randint(seeds[7], (NBLK,), NBR_LEN // 4, NBR_LEN + 1), jax.random.fold_in(seeds[7], 1), NBR_LEN // 4, NBR_LEN).astype(jnp.int32)
    nbr_owner_keys = jax.random.split(jax.random.fold_in(seeds[8], 1), SPANS // C_DEV)
    nbr_owner_turns = jax.random.permutation(jax.random.fold_in(seeds[8], 3), SPANS // C_DEV)
    nbr_owner = jax.vmap(lambda own, number: routed_block(jax.random.fold_in(seeds[8], 2), own, number, C_DEV, N_DB, NBRS, CAP, 2))(nbr_owner_keys, nbr_owner_turns).reshape((SPANS, NBRS))
    nbr_block = plant(jax.random.randint(seeds[9], (SPANS, NBRS), 0, NB_DEV), jax.random.fold_in(seeds[9], 1), 0, NB_DEV - 1).astype(jnp.int32)
    return dict(tokens=tokens, query_weight=query_weight, key_weight=key_weight, value_weight=value_weight, out_weight=out_weight, codes=codes, scales=scales, block_len=block_len, nbr_owner=nbr_owner, nbr_block=nbr_block)


def normalize(values):
    return values * lax.rsqrt(lax.optimization_barrier(jnp.mean(values * values, axis=-1, keepdims=True)) + 1e-06)

def reference(tokens, query_weight, key_weight, value_weight, out_weight, codes, scales, block_len, nbr_owner, nbr_block):
    groups = ENC // GROUP
    grouped = codes.astype(jnp.float32).reshape(NBLK, NBR_LEN, groups, GROUP)
    encoded = (grouped * scales[:, None, :, None]).reshape(NBLK * NBR_LEN, ENC).astype(jnp.bfloat16)
    key_proj = jnp.dot(encoded, key_weight, preferred_element_type=jnp.float32)
    key_rows = normalize(key_proj.reshape(NBLK, NBR_LEN, HEADS, HD)).astype(jnp.bfloat16)
    value_rows = jnp.dot(encoded, value_weight, preferred_element_type=jnp.float32).astype(jnp.bfloat16)
    value_rows = value_rows.reshape(NBLK, NBR_LEN, HEADS, HD)
    query_proj = jnp.dot(tokens, query_weight, preferred_element_type=jnp.float32)
    queries = normalize(query_proj.reshape(SPANS, SPAN, HEADS, HD)).astype(jnp.bfloat16)
    block_ids = (nbr_owner * NB_DEV + nbr_block).astype(jnp.int32)
    positions = jnp.arange(NBR_LEN, dtype=jnp.int32)
    factor = 2.0 / math.sqrt(HD)

    def attend(span_id):
        chosen = block_ids[span_id]
        keys_here = key_rows[chosen].reshape(NBRS * NBR_LEN, HEADS, HD).astype(jnp.float32)
        values_here = value_rows[chosen].reshape(NBRS * NBR_LEN, HEADS, HD).astype(jnp.float32)
        valid_keys = (positions[None, :] < block_len[chosen][:, None]).reshape(NBRS * NBR_LEN)
        scores = jnp.einsum('thd,khd->htk', queries[span_id].astype(jnp.float32), keys_here) * factor
        raised = jnp.where(valid_keys[None, None, :], jnp.exp(scores), 0.0)
        attn_weights = (raised / lax.optimization_barrier(jnp.sum(raised, axis=-1, keepdims=True))).astype(jnp.bfloat16)
        attended = jnp.einsum('htk,khd->thd', attn_weights.astype(jnp.float32), values_here)
        return attended.astype(jnp.bfloat16).reshape(SPAN, D)
    attended_all = lax.map(attend, jnp.arange(SPANS, dtype=jnp.int32)).reshape(TOKENS, D)
    return jnp.dot(attended_all, out_weight, preferred_element_type=jnp.float32).astype(jnp.bfloat16)
```

```python
import math

import jax
import jax.numpy as jnp
from jax import lax
from jax.experimental import pallas as pl
from jax.experimental.pallas import tpu as pltpu
from jax.sharding import Mesh
from jax.sharding import PartitionSpec as P

HD = 128
ENC = 896
GROUP = 128
SPAN = 64
NBR_LEN = 128
NBRS = 2
DB = ("y", "x")
F32 = jnp.float32
BF16 = jnp.bfloat16
VMEM = pl.BlockSpec(memory_space=pltpu.VMEM)
SMEM = pl.BlockSpec(memory_space=pltpu.SMEM)
ANY = pl.BlockSpec(memory_space=pl.ANY)


def unit(values):
    return values * lax.rsqrt(jnp.mean(values * values, axis=-1, keepdims=True) + 1e-06)


def project_kernel(scales_ref, codes_ref, key_ref, value_ref, out_ref, enc_ref):
    step = pl.program_id(0)
    blocks = codes_ref.shape[0]
    for b in range(blocks):
        for g in range(ENC // GROUP):
            cols = slice(g * GROUP, (g + 1) * GROUP)
            scaled = codes_ref[b, :, cols].astype(F32) * scales_ref[step * blocks + b, g]
            enc_ref[b * NBR_LEN : (b + 1) * NBR_LEN, cols] = scaled.astype(BF16)
    enc = enc_ref[...]
    keys = jnp.dot(enc, key_ref[...], preferred_element_type=F32)
    values = jnp.dot(enc, value_ref[...], preferred_element_type=F32).astype(BF16)
    width = key_ref.shape[1]
    for b in range(blocks):
        rows = slice(b * NBR_LEN, (b + 1) * NBR_LEN)
        for h in range(width // HD):
            cols = slice(h * HD, (h + 1) * HD)
            out_ref[b, :, cols] = unit(keys[rows, cols]).astype(BF16)
        out_ref[b, :, width : 2 * width] = values[rows]


def project_blocks(codes, scales, key_weight, value_weight):
    count, width, per = codes.shape[0], key_weight.shape[1], 2
    return pl.pallas_call(
        project_kernel,
        grid=(count // per,),
        out_shape=jax.ShapeDtypeStruct((count, NBR_LEN, 2 * width), BF16),
        in_specs=[
            SMEM,
            pl.BlockSpec((per, NBR_LEN, ENC), lambda i: (i, 0, 0)),
            pl.BlockSpec((ENC, width), lambda i: (0, 0)),
            pl.BlockSpec((ENC, width), lambda i: (0, 0)),
        ],
        out_specs=pl.BlockSpec((per, NBR_LEN, 2 * width), lambda i: (i, 0, 0)),
        scratch_shapes=[pltpu.VMEM((per * NBR_LEN, ENC), BF16)],
        cost_estimate=pl.CostEstimate(
            flops=2 * count * NBR_LEN * ENC * 2 * width, bytes_accessed=5 << 20, transcendentals=0
        ),
        name="project_blocks",
    )(scales, codes, key_weight, value_weight)


def select_kernel(wanted_ref, rows_ref, out_ref, sems):
    shards, items = wanted_ref.shape
    copies = []
    for e in range(shards):
        for s in range(items):
            copy = pltpu.make_async_copy(
                rows_ref.at[wanted_ref[e, s]], out_ref.at[e, s], sems.at[e, s]
            )
            copy.start()
            copies.append(copy)
    for copy in copies:
        copy.wait()


def select_blocks(wanted, rows):
    shards, items = wanted.shape
    return pl.pallas_call(
        select_kernel,
        out_shape=jax.ShapeDtypeStruct((shards, items) + rows.shape[1:], BF16),
        in_specs=[SMEM, VMEM],
        out_specs=ANY,
        scratch_shapes=[pltpu.SemaphoreType.DMA((shards, items))],
        cost_estimate=pl.CostEstimate(flops=0, bytes_accessed=9 << 20, transcendentals=0),
        name="select_blocks",
    )(wanted, rows)


def query_kernel(tokens_ref, weight_ref, out_ref):
    projected = jnp.dot(tokens_ref[...], weight_ref[...], preferred_element_type=F32)
    for h in range(weight_ref.shape[1] // HD):
        cols = slice(h * HD, (h + 1) * HD)
        out_ref[:, cols] = unit(projected[:, cols]).astype(BF16)


def project_queries(tokens, weight):
    rows, depth = tokens.shape
    width, tile = weight.shape[1], 128
    return pl.pallas_call(
        query_kernel,
        grid=(rows // tile,),
        out_shape=jax.ShapeDtypeStruct((rows, width), BF16),
        in_specs=[
            pl.BlockSpec((tile, depth), lambda i: (i, 0)),
            pl.BlockSpec((depth, width), lambda i: (0, 0)),
        ],
        out_specs=pl.BlockSpec((tile, width), lambda i: (i, 0)),
        compiler_params=pltpu.CompilerParams(vmem_limit_bytes=24 << 20),
        cost_estimate=pl.CostEstimate(
            flops=2 * rows * depth * width, bytes_accessed=11 << 20, transcendentals=0
        ),
        name="project_queries",
    )(tokens, weight)


def attend_kernel(slot_ref, length_ref, query_ref, rows_ref, out_ref, held_ref, sems):
    requests = held_ref.shape[0]
    width = query_ref.shape[1]
    factor = 2.0 / math.sqrt(HD)
    copies = []
    for r in range(requests):
        copy = pltpu.make_async_copy(rows_ref.at[slot_ref[r]], held_ref.at[r], sems.at[r])
        copy.start()
        copies.append(copy)
    places = lax.broadcasted_iota(jnp.int32, (SPAN, NBR_LEN), 1)
    for c in range(requests // NBRS):
        for n in range(NBRS):
            copies[c * NBRS + n].wait()
        spans = slice(c * SPAN, (c + 1) * SPAN)
        for h in range(width // HD):
            cols = slice(h * HD, (h + 1) * HD)
            query = query_ref[spans, cols]
            raised = []
            for n in range(NBRS):
                scores = lax.dot_general(
                    query,
                    held_ref[c * NBRS + n, :, cols],
                    (((1,), (1,)), ((), ())),
                    preferred_element_type=F32,
                )
                raised.append(
                    jnp.where(
                        places < length_ref[c * NBRS + n], jnp.exp(scores * factor), 0.0
                    )
                )
            total = sum(jnp.sum(part, axis=-1, keepdims=True) for part in raised)
            scale = 1.0 / total
            result = jnp.zeros((SPAN, HD), F32)
            for n in range(NBRS):
                result += jnp.dot(
                    (raised[n] * scale).astype(BF16),
                    held_ref[c * NBRS + n, :, width + h * HD : width + (h + 1) * HD],
                    preferred_element_type=F32,
                )
            out_ref[spans, cols] = result.astype(BF16)


def attend(slot_index, lengths, queries, rows):
    requests = slot_index.shape[0]
    return pl.pallas_call(
        attend_kernel,
        out_shape=jax.ShapeDtypeStruct(queries.shape, BF16),
        in_specs=[SMEM, SMEM, VMEM, ANY],
        out_specs=VMEM,
        scratch_shapes=[
            pltpu.VMEM((requests,) + rows.shape[1:], BF16),
            pltpu.SemaphoreType.DMA((requests,)),
        ],
        compiler_params=pltpu.CompilerParams(vmem_limit_bytes=24 << 20),
        cost_estimate=pl.CostEstimate(
            flops=4 * queries.shape[0] * NBRS * NBR_LEN * queries.shape[1],
            bytes_accessed=6 << 20,
            transcendentals=0,
        ),
        name="attend",
    )(slot_index, lengths, queries, rows)


def reduce_ring(attended, own_weight, partner_attended, partner_weight, ring):
    rows = attended.shape[0] // 2
    stacked = jnp.concatenate([attended, partner_attended], axis=1)
    up = [(i, (i + 1) % ring) for i in range(ring)]
    down = [(i, (i - 1) % ring) for i in range(ring)]
    weight = jnp.concatenate([own_weight, partner_weight], axis=0)

    def share(half, step):
        return jnp.dot(
            stacked[half * rows : (half + 1) * rows],
            weight[:, step % ring],
            preferred_element_type=F32,
        )

    far = ring // 2
    chains = [(0, 1, far), (1, -1, far), (1, 1, far - 1), (0, -1, far - 1)]
    held = {}
    for distance in range(far, 0, -1):
        for half, way, first in chains:
            if distance > first:
                continue
            part = share(half, way * distance)
            if distance < first:
                part = part + held[half, way].astype(F32)
            held[half, way] = lax.ppermute(part.astype(BF16), "z", up if way == 1 else down)
    out = [
        (share(half, 0) + held[half, 1].astype(F32) + held[half, -1].astype(F32)).astype(BF16)
        for half in range(2)
    ]
    return jnp.concatenate(out, axis=0)


def local(
    tokens,
    query_weight,
    key_weight,
    value_weight,
    out_weight,
    codes,
    scales,
    block_len,
    nbr_owner,
    nbr_block,
):
    width = query_weight.shape[1]
    ring = lax.axis_size("z")
    cores = lax.axis_size("c")
    shards = lax.axis_size(DB)
    here, core = lax.axis_index("z"), lax.axis_index("c")
    swap = [(i, (i + 1) % cores) for i in range(cores)]

    gathered = lax.all_gather(tokens, ("z", "c"), axis=1, tiled=True)

    owners = nbr_owner.reshape(-1)
    wanted_blocks = nbr_block.reshape(-1)
    order = jnp.arange(owners.shape[0], dtype=jnp.int32)
    earlier = jnp.sum(
        ((owners[:, None] == owners[None, :]) & (order[:, None] > order[None, :])).astype(jnp.int32),
        axis=1,
    )
    slot_index = owners * NBRS + earlier
    slots = jnp.arange(shards * NBRS, dtype=jnp.int32)
    request_table = jnp.sum(
        jnp.where(slot_index[:, None] == slots[None, :], wanted_blocks[:, None], 0), axis=0
    ).reshape(shards, NBRS)
    notes = jnp.concatenate(
        [request_table, jnp.broadcast_to(block_len[None, :], (shards, block_len.shape[0]))], axis=1
    )
    heard = lax.all_to_all(notes, DB, split_axis=0, concat_axis=0, tiled=True)
    wanted = heard[:, :NBRS]
    all_lengths = heard[:, NBRS:].reshape(-1)
    block_ids = owners * block_len.shape[0] + wanted_blocks
    ids = jnp.arange(all_lengths.shape[0], dtype=jnp.int32)
    lengths = jnp.sum(
        jnp.where(block_ids[:, None] == ids[None, :], all_lengths[None, :], 0), axis=1
    )

    projected = project_blocks(codes, scales, key_weight, value_weight)
    sent = select_blocks(wanted, projected)
    rows = lax.all_to_all(sent, DB, split_axis=0, concat_axis=0, tiled=True)
    rows = rows.reshape(shards * NBRS, NBR_LEN, 2 * width)

    by_core = out_weight.reshape(width, ring, cores, width)
    own_weight = lax.dynamic_index_in_dim(by_core, core, 2, keepdims=False)
    lent_weight = lax.dynamic_index_in_dim(by_core, 1 - core, 2, keepdims=False)
    partner_weight = lax.ppermute(lent_weight, "c", swap)
    twice = jnp.concatenate([own_weight, own_weight], axis=1)
    own_weight = lax.dynamic_slice_in_dim(twice, here, ring, 1)
    twice = jnp.concatenate([partner_weight, partner_weight], axis=1)
    partner_weight = lax.dynamic_slice_in_dim(twice, here, ring, 1)

    queries = project_queries(gathered, query_weight)
    attended = attend(slot_index, lengths, queries, rows)
    partner_attended = lax.ppermute(attended, "c", swap)
    return reduce_ring(attended, own_weight, partner_attended, partner_weight, ring)


def solution(mesh):
    grid = Mesh(mesh.devices.reshape(4, 4, 8, 2), ("y", "x", "z", "c"))
    head = ("z", "c")
    placed = (
        P(DB, head),
        P(None, head),
        P(None, head),
        P(None, head),
        P(head, None),
        P(DB, None, None),
        P(DB, None),
        P(DB),
        P(DB, None),
        P(DB, None),
    )
    return jax.shard_map(
        local, mesh=grid, in_specs=placed, out_specs=P(DB, head), check_vma=False
    )
```

```python
import functools
import math

import jax
import jax.numpy as jnp
from jax import lax
from jax.experimental import pallas as pl
from jax.experimental.pallas import tpu as pltpu
from jax.sharding import Mesh
from jax.sharding import PartitionSpec as P

HD = 128
ENC = 896
GROUP = 128
SPAN = 64
NBR_LEN = 128
NBRS = 2
DB = ("y", "x")
F32 = jnp.float32
BF16 = jnp.bfloat16
VMEM = pl.BlockSpec(memory_space=pltpu.VMEM)
SMEM = pl.BlockSpec(memory_space=pltpu.SMEM)
ANY = pl.BlockSpec(memory_space=pl.ANY)


def unit(values):
    return values * lax.rsqrt(jnp.mean(values * values, axis=-1, keepdims=True) + 1e-06)


def project_kernel(scales_ref, codes_ref, key_ref, value_ref, out_ref, enc_ref):
    step = pl.program_id(0)
    blocks = codes_ref.shape[0]
    for b in range(blocks):
        for g in range(ENC // GROUP):
            cols = slice(g * GROUP, (g + 1) * GROUP)
            scaled = codes_ref[b, :, cols].astype(F32) * scales_ref[step * blocks + b, g]
            enc_ref[b * NBR_LEN : (b + 1) * NBR_LEN, cols] = scaled.astype(BF16)
    enc = enc_ref[...]
    keys = jnp.dot(enc, key_ref[...], preferred_element_type=F32)
    values = jnp.dot(enc, value_ref[...], preferred_element_type=F32).astype(BF16)
    width = key_ref.shape[1]
    for b in range(blocks):
        rows = slice(b * NBR_LEN, (b + 1) * NBR_LEN)
        for h in range(width // HD):
            cols = slice(h * HD, (h + 1) * HD)
            out_ref[b, :, cols] = unit(keys[rows, cols]).astype(BF16)
        out_ref[b, :, width : 2 * width] = values[rows]


def project_blocks(codes, scales, key_weight, value_weight):
    count, width, per = codes.shape[0], key_weight.shape[1], 2
    return pl.pallas_call(
        project_kernel,
        grid=(count // per,),
        out_shape=jax.ShapeDtypeStruct((count, NBR_LEN, 2 * width), BF16),
        in_specs=[
            SMEM,
            pl.BlockSpec((per, NBR_LEN, ENC), lambda i: (i, 0, 0)),
            pl.BlockSpec((ENC, width), lambda i: (0, 0)),
            pl.BlockSpec((ENC, width), lambda i: (0, 0)),
        ],
        out_specs=pl.BlockSpec((per, NBR_LEN, 2 * width), lambda i: (i, 0, 0)),
        scratch_shapes=[pltpu.VMEM((per * NBR_LEN, ENC), BF16)],
        cost_estimate=pl.CostEstimate(
            flops=2 * count * NBR_LEN * ENC * 2 * width, bytes_accessed=5 << 20, transcendentals=0
        ),
        name="project_blocks",
    )(scales, codes, key_weight, value_weight)


def select_kernel(place_ref, heard_ref, rows_ref, out_ref, sems):
    shards, requests = out_ref.shape[0], out_ref.shape[0] * NBRS
    here = place_ref[0]
    copies = []
    for e in range(shards):
        first, last = jnp.int32(-1), jnp.int32(0)
        for r in range(requests):
            mine = heard_ref[e, r] == here
            block = heard_ref[e, requests + r]
            first = jnp.where(mine & (first < 0), block, first)
            last = jnp.where(mine, block, last)
        for s, block in enumerate((jnp.maximum(first, 0), last)):
            copy = pltpu.make_async_copy(rows_ref.at[block], out_ref.at[e, s], sems.at[e, s])
            copy.start()
            copies.append(copy)
    for copy in copies:
        copy.wait()


def select_blocks(place, heard, rows):
    shards = heard.shape[0]
    return pl.pallas_call(
        select_kernel,
        out_shape=jax.ShapeDtypeStruct((shards, NBRS) + rows.shape[1:], BF16),
        in_specs=[SMEM, SMEM, VMEM],
        out_specs=ANY,
        scratch_shapes=[pltpu.SemaphoreType.DMA((shards, NBRS))],
        cost_estimate=pl.CostEstimate(flops=0, bytes_accessed=9 << 20, transcendentals=0),
        name="select_blocks",
    )(place, heard, rows)


def query_kernel(tokens_ref, weight_ref, out_ref):
    projected = jnp.dot(tokens_ref[...], weight_ref[...], preferred_element_type=F32)
    for h in range(weight_ref.shape[1] // HD):
        cols = slice(h * HD, (h + 1) * HD)
        out_ref[:, cols] = unit(projected[:, cols]).astype(BF16)


def project_queries(tokens, weight):
    rows, depth = tokens.shape
    width, tile = weight.shape[1], 128
    return pl.pallas_call(
        query_kernel,
        grid=(rows // tile,),
        out_shape=jax.ShapeDtypeStruct((rows, width), BF16),
        in_specs=[
            pl.BlockSpec((tile, depth), lambda i: (i, 0)),
            pl.BlockSpec((depth, width), lambda i: (0, 0)),
        ],
        out_specs=pl.BlockSpec((tile, width), lambda i: (i, 0)),
        compiler_params=pltpu.CompilerParams(vmem_limit_bytes=24 << 20),
        cost_estimate=pl.CostEstimate(
            flops=2 * rows * depth * width, bytes_accessed=11 << 20, transcendentals=0
        ),
        name="project_queries",
    )(tokens, weight)


def attend_kernel(first, slot_ref, length_ref, query_ref, rows_ref, out_ref, held_ref, sems):
    spans = slot_ref.shape[0] // NBRS
    count = sems.shape[0] // NBRS
    width = query_ref.shape[1]
    keys = NBRS * NBR_LEN
    factor = 2.0 / math.sqrt(HD)
    copies = []
    for c in range(count):
        for n in range(NBRS):
            copy = pltpu.make_async_copy(
                rows_ref.at[slot_ref[n * spans + first + c]],
                held_ref.at[pl.ds((c * NBRS + n) * NBR_LEN, NBR_LEN)],
                sems.at[c * NBRS + n],
            )
            copy.start()
            copies.append(copy)
    places = lax.broadcasted_iota(jnp.int32, (SPAN, keys), 1)
    group = 4
    for start in range(0, count, group):
        members = [(c, h) for c in range(start, start + group) for h in range(width // HD)]
        for copy in copies[start * NBRS : (start + group) * NBRS]:
            copy.wait()
        raised = []
        for c, h in members:
            scores = lax.dot_general(
                query_ref[c * SPAN : (c + 1) * SPAN, h * HD : (h + 1) * HD],
                held_ref[c * keys : (c + 1) * keys, h * HD : (h + 1) * HD],
                (((1,), (1,)), ((), ())),
                preferred_element_type=F32,
            )
            ends = [length_ref[n * spans + first + c] + n * NBR_LEN for n in range(NBRS)]
            valid = (places < ends[0]) | ((places >= NBR_LEN) & (places < ends[1]))
            raised.append(jnp.where(valid, jnp.exp(scores * factor), 0.0))
        weights = [
            (part * (1.0 / jnp.sum(part, axis=-1, keepdims=True))).astype(BF16) for part in raised
        ]
        for (c, h), part in zip(members, weights):
            cols = slice(width + h * HD, width + (h + 1) * HD)
            result = jnp.dot(
                part, held_ref[c * keys : (c + 1) * keys, cols], preferred_element_type=F32
            )
            out_ref[c * SPAN : (c + 1) * SPAN, h * HD : (h + 1) * HD] = result.astype(BF16)


def attend(part, parts, slot_index, lengths, queries, rows):
    tokens, width = queries.shape[0] // parts, queries.shape[1]
    count = tokens // SPAN
    requests = count * NBRS
    return pl.pallas_call(
        functools.partial(attend_kernel, part * count),
        grid=(1,),
        out_shape=jax.ShapeDtypeStruct((tokens, width), BF16),
        in_specs=[SMEM, SMEM, pl.BlockSpec((tokens, width), lambda i: (part, 0)), ANY],
        out_specs=pl.BlockSpec((tokens, width), lambda i: (0, 0)),
        scratch_shapes=[
            pltpu.VMEM((requests * NBR_LEN, rows.shape[2]), BF16),
            pltpu.SemaphoreType.DMA((requests,)),
        ],
        compiler_params=pltpu.CompilerParams(vmem_limit_bytes=24 << 20),
        cost_estimate=pl.CostEstimate(
            flops=4 * tokens * NBRS * NBR_LEN * width, bytes_accessed=3 << 20, transcendentals=0
        ),
        name="attend",
    )(slot_index, lengths, queries, rows)


def relay_kernel(place_ref, weight_ref, own_ref, lent_ref, sems):
    here, core = place_ref[0], place_ref[1]
    ring, _, width = own_ref.shape
    copies = []
    for k in range(ring):
        chip = lax.rem(here + k, ring)
        for i, (ref, which) in enumerate(((own_ref, core), (lent_ref, 1 - core))):
            cols = pl.ds(pl.multiple_of((chip * 2 + which) * width, width), width)
            copy = pltpu.make_async_copy(weight_ref.at[:, cols], ref.at[k], sems.at[i, k])
            copy.start()
            copies.append(copy)
    for copy in copies:
        copy.wait()


def relay(place, weight, ring):
    depth = weight.shape[0]
    shape = jax.ShapeDtypeStruct((ring, depth, weight.shape[1] // (2 * ring)), BF16)
    return pl.pallas_call(
        relay_kernel,
        out_shape=(shape, shape),
        in_specs=[SMEM, ANY],
        out_specs=(ANY, ANY),
        scratch_shapes=[pltpu.SemaphoreType.DMA((2, ring))],
        cost_estimate=pl.CostEstimate(flops=0, bytes_accessed=4 << 20, transcendentals=0),
        name="relay",
    )(place, weight)


def reduce_ring(attended, partner_attended, own_weight, partner_weight, ring):
    up = [(i, (i + 1) % ring) for i in range(ring)]
    down = [(i, (i - 1) % ring) for i in range(ring)]

    def share(half, step):
        return jnp.dot(
            attended[half], own_weight[step % ring], preferred_element_type=F32
        ) + jnp.dot(partner_attended[half], partner_weight[step % ring], preferred_element_type=F32)

    far = ring // 2
    chains = [(0, 1, far), (1, -1, far), (0, -1, far - 1), (1, 1, far - 1)]
    held = {}
    for distance in range(far, 0, -1):
        for half, way, first in chains:
            if distance > first:
                continue
            part = share(half, way * distance)
            if distance < first:
                part = part + held[half, way].astype(F32)
            held[half, way] = lax.ppermute(part.astype(BF16), "z", up if way == 1 else down)
    out = [
        (share(half, 0) + held[half, 1].astype(F32) + held[half, -1].astype(F32)).astype(BF16)
        for half in range(2)
    ]
    return jnp.concatenate(out, axis=0)


def local(
    tokens,
    query_weight,
    key_weight,
    value_weight,
    out_weight,
    codes,
    scales,
    block_len,
    nbr_owner,
    nbr_block,
):
    width = query_weight.shape[1]
    ring = lax.axis_size("z")
    cores = lax.axis_size("c")
    shards = lax.axis_size(DB)
    here, core = lax.axis_index("z"), lax.axis_index("c")
    swap = [(i, (i + 1) % cores) for i in range(cores)]

    gathered = lax.all_gather(tokens, ("z", "c"), axis=1, tiled=True)

    owners = nbr_owner.T.reshape(-1)
    wanted_blocks = nbr_block.T.reshape(-1)
    notes = jnp.concatenate([owners, wanted_blocks, block_len])
    notes = jnp.broadcast_to(notes[None, :], (shards, notes.shape[0]))
    heard = lax.all_to_all(notes, DB, split_axis=0, concat_axis=0, tiled=True)
    projected = project_blocks(codes, scales, key_weight, value_weight)
    sent = select_blocks(lax.axis_index(DB).astype(jnp.int32).reshape(1), heard, projected)
    rows = lax.all_to_all(sent, DB, split_axis=0, concat_axis=0, tiled=True)
    rows = rows.reshape(shards * NBRS, NBR_LEN, 2 * width)

    order = jnp.arange(owners.shape[0], dtype=jnp.int32)
    earlier = jnp.sum(
        ((owners[:, None] == owners[None, :]) & (order[:, None] > order[None, :])).astype(jnp.int32),
        axis=1,
    )
    slot_index = owners * NBRS + earlier
    all_lengths = heard[:, 2 * owners.shape[0] :].reshape(-1)
    block_ids = owners * block_len.shape[0] + wanted_blocks
    ids = jnp.arange(all_lengths.shape[0], dtype=jnp.int32)
    lengths = jnp.sum(
        jnp.where(block_ids[:, None] == ids[None, :], all_lengths[None, :], 0), axis=1
    )

    own_weight, lent_weight = relay(jnp.stack([here, core]).astype(jnp.int32), out_weight, ring)
    partner_weight = lax.ppermute(lent_weight, "c", swap)

    queries = project_queries(gathered, query_weight)
    attended = [attend(part, 2, slot_index, lengths, queries, rows) for part in range(2)]
    partner_attended = [lax.ppermute(part, "c", swap) for part in attended]
    return reduce_ring(attended, partner_attended, own_weight, partner_weight, ring)


def solution(mesh):
    grid = Mesh(mesh.devices.reshape(4, 4, 8, 2), ("y", "x", "z", "c"))
    head = ("z", "c")
    placed = (
        P(DB, head),
        P(None, head),
        P(None, head),
        P(None, head),
        P(head, None),
        P(DB, None, None),
        P(DB, None),
        P(DB),
        P(DB, None),
        P(DB, None),
    )
    return jax.shard_map(
        local, mesh=grid, in_specs=placed, out_specs=P(DB, head), check_vma=False
    )
```

```python
import functools
import math

import jax
import jax.numpy as jnp
from jax import lax
from jax.experimental import pallas as pl
from jax.experimental.pallas import tpu as pltpu
from jax.sharding import Mesh
from jax.sharding import PartitionSpec as P

HD = 128
ENC = 896
GROUP = 128
SPAN = 64
NBR_LEN = 128
NBRS = 2
DB = ("y", "x")
F32 = jnp.float32
BF16 = jnp.bfloat16
VMEM = pl.BlockSpec(memory_space=pltpu.VMEM)
SMEM = pl.BlockSpec(memory_space=pltpu.SMEM)
ANY = pl.BlockSpec(memory_space=pl.ANY)


def unit(values):
    return values * lax.rsqrt(jnp.mean(values * values, axis=-1, keepdims=True) + 1e-06)


def project_kernel(scales_ref, codes_ref, key_ref, value_ref, out_ref, enc_ref):
    step = pl.program_id(0)
    blocks = codes_ref.shape[0]
    for b in range(blocks):
        for g in range(ENC // GROUP):
            cols = slice(g * GROUP, (g + 1) * GROUP)
            scaled = codes_ref[b, :, cols].astype(F32) * scales_ref[step * blocks + b, g]
            enc_ref[b * NBR_LEN : (b + 1) * NBR_LEN, cols] = scaled.astype(BF16)
    enc = enc_ref[...]
    keys = jnp.dot(enc, key_ref[...], preferred_element_type=F32)
    values = jnp.dot(enc, value_ref[...], preferred_element_type=F32).astype(BF16)
    width = key_ref.shape[1]
    for b in range(blocks):
        rows = slice(b * NBR_LEN, (b + 1) * NBR_LEN)
        for h in range(width // HD):
            cols = slice(h * HD, (h + 1) * HD)
            out_ref[b, :, cols] = unit(keys[rows, cols]).astype(BF16)
        out_ref[b, :, width : 2 * width] = values[rows]


def project_blocks(codes, scales, key_weight, value_weight):
    count, width, per = codes.shape[0], key_weight.shape[1], 2
    return pl.pallas_call(
        project_kernel,
        grid=(count // per,),
        out_shape=jax.ShapeDtypeStruct((count, NBR_LEN, 2 * width), BF16),
        in_specs=[
            SMEM,
            pl.BlockSpec((per, NBR_LEN, ENC), lambda i: (i, 0, 0)),
            pl.BlockSpec((ENC, width), lambda i: (0, 0)),
            pl.BlockSpec((ENC, width), lambda i: (0, 0)),
        ],
        out_specs=pl.BlockSpec((per, NBR_LEN, 2 * width), lambda i: (i, 0, 0)),
        scratch_shapes=[pltpu.VMEM((per * NBR_LEN, ENC), BF16)],
        cost_estimate=pl.CostEstimate(
            flops=2 * count * NBR_LEN * ENC * 2 * width, bytes_accessed=5 << 20, transcendentals=0
        ),
        name="project_blocks",
    )(scales, codes, key_weight, value_weight)


def select_kernel(place_ref, heard_ref, rows_ref, out_ref, sems):
    shards, requests = out_ref.shape[0], out_ref.shape[0] * NBRS
    here = place_ref[0]
    copies = []
    for e in range(shards):
        first, last = jnp.int32(-1), jnp.int32(0)
        for r in range(requests):
            mine = heard_ref[e, r] == here
            block = heard_ref[e, requests + r]
            first = jnp.where(mine & (first < 0), block, first)
            last = jnp.where(mine, block, last)
        for s, block in enumerate((jnp.maximum(first, 0), last)):
            copy = pltpu.make_async_copy(rows_ref.at[block], out_ref.at[e, s], sems.at[e, s])
            copy.start()
            copies.append(copy)
    for copy in copies:
        copy.wait()


def select_blocks(place, heard, rows):
    shards = heard.shape[0]
    return pl.pallas_call(
        select_kernel,
        out_shape=jax.ShapeDtypeStruct((shards, NBRS) + rows.shape[1:], BF16),
        in_specs=[SMEM, SMEM, VMEM],
        out_specs=ANY,
        scratch_shapes=[pltpu.SemaphoreType.DMA((shards, NBRS))],
        cost_estimate=pl.CostEstimate(flops=0, bytes_accessed=9 << 20, transcendentals=0),
        name="select_blocks",
    )(place, heard, rows)


def query_kernel(tokens_ref, weight_ref, out_ref):
    projected = jnp.dot(tokens_ref[...], weight_ref[...], preferred_element_type=F32)
    for h in range(weight_ref.shape[1] // HD):
        cols = slice(h * HD, (h + 1) * HD)
        out_ref[:, cols] = unit(projected[:, cols]).astype(BF16)


def project_queries(tokens, weight):
    rows, depth = tokens.shape
    width, tile = weight.shape[1], 128
    return pl.pallas_call(
        query_kernel,
        grid=(rows // tile,),
        out_shape=jax.ShapeDtypeStruct((rows, width), BF16),
        in_specs=[
            pl.BlockSpec((tile, depth), lambda i: (i, 0)),
            pl.BlockSpec((depth, width), lambda i: (0, 0)),
        ],
        out_specs=pl.BlockSpec((tile, width), lambda i: (i, 0)),
        compiler_params=pltpu.CompilerParams(vmem_limit_bytes=24 << 20),
        cost_estimate=pl.CostEstimate(
            flops=2 * rows * depth * width, bytes_accessed=11 << 20, transcendentals=0
        ),
        name="project_queries",
    )(tokens, weight)


def attend_kernel(first, slot_ref, length_ref, query_ref, rows_ref, out_ref, held_ref, sems):
    spans = slot_ref.shape[0] // NBRS
    count = sems.shape[0] // NBRS
    width = query_ref.shape[1]
    keys = NBRS * NBR_LEN
    factor = 2.0 / math.sqrt(HD)
    copies = []
    for c in range(count):
        for n in range(NBRS):
            copy = pltpu.make_async_copy(
                rows_ref.at[slot_ref[n * spans + first + c]],
                held_ref.at[pl.ds((c * NBRS + n) * NBR_LEN, NBR_LEN)],
                sems.at[c * NBRS + n],
            )
            copy.start()
            copies.append(copy)
    places = lax.broadcasted_iota(jnp.int32, (SPAN, keys), 1)
    group = 4
    for start in range(0, count, group):
        members = [(c, h) for c in range(start, start + group) for h in range(width // HD)]
        for copy in copies[start * NBRS : (start + group) * NBRS]:
            copy.wait()
        raised = []
        for c, h in members:
            scores = lax.dot_general(
                query_ref[c * SPAN : (c + 1) * SPAN, h * HD : (h + 1) * HD],
                held_ref[c * keys : (c + 1) * keys, h * HD : (h + 1) * HD],
                (((1,), (1,)), ((), ())),
                preferred_element_type=F32,
            )
            ends = [length_ref[n * spans + first + c] + n * NBR_LEN for n in range(NBRS)]
            valid = (places < ends[0]) | ((places >= NBR_LEN) & (places < ends[1]))
            raised.append(jnp.where(valid, jnp.exp(scores * factor), 0.0))
        weights = [
            (part * (1.0 / jnp.sum(part, axis=-1, keepdims=True))).astype(BF16) for part in raised
        ]
        for (c, h), part in zip(members, weights):
            cols = slice(width + h * HD, width + (h + 1) * HD)
            result = jnp.dot(
                part, held_ref[c * keys : (c + 1) * keys, cols], preferred_element_type=F32
            )
            out_ref[c * SPAN : (c + 1) * SPAN, h * HD : (h + 1) * HD] = result.astype(BF16)


def attend(part, parts, slot_index, lengths, queries, rows):
    tokens, width = queries.shape[0] // parts, queries.shape[1]
    count = tokens // SPAN
    requests = count * NBRS
    return pl.pallas_call(
        functools.partial(attend_kernel, part * count),
        grid=(1,),
        out_shape=jax.ShapeDtypeStruct((tokens, width), BF16),
        in_specs=[SMEM, SMEM, pl.BlockSpec((tokens, width), lambda i: (part, 0)), ANY],
        out_specs=pl.BlockSpec((tokens, width), lambda i: (0, 0)),
        scratch_shapes=[
            pltpu.VMEM((requests * NBR_LEN, rows.shape[2]), BF16),
            pltpu.SemaphoreType.DMA((requests,)),
        ],
        compiler_params=pltpu.CompilerParams(vmem_limit_bytes=24 << 20),
        cost_estimate=pl.CostEstimate(
            flops=4 * tokens * NBRS * NBR_LEN * width, bytes_accessed=3 << 20, transcendentals=0
        ),
        name="attend",
    )(slot_index, lengths, queries, rows)


def relay_kernel(place_ref, weight_ref, own_ref, lent_ref):
    here, core = place_ref[0], place_ref[1]
    ring, _, width = own_ref.shape
    for k in range(ring):
        chip = lax.rem(here + k, ring)
        for ref, which in ((own_ref, core), (lent_ref, 1 - core)):
            cols = pl.ds(pl.multiple_of((chip * 2 + which) * width, width), width)
            ref[k] = weight_ref[:, cols]


def relay(place, weight, ring):
    depth = weight.shape[0]
    shape = jax.ShapeDtypeStruct((ring, depth, weight.shape[1] // (2 * ring)), BF16)
    return pl.pallas_call(
        relay_kernel,
        out_shape=(shape, shape),
        in_specs=[SMEM, VMEM],
        out_specs=(VMEM, VMEM),
        compiler_params=pltpu.CompilerParams(vmem_limit_bytes=16 << 20),
        cost_estimate=pl.CostEstimate(flops=0, bytes_accessed=4 << 20, transcendentals=0),
        name="relay",
    )(place, weight)


def share_kernel(steps, own_ref, partner_ref, own_w_ref, partner_w_ref, *out_refs):
    for step, ref in zip(steps, out_refs):
        ref[...] = (
            jnp.dot(own_ref[...], own_w_ref[step], preferred_element_type=F32)
            + jnp.dot(partner_ref[...], partner_w_ref[step], preferred_element_type=F32)
        ).astype(ref.dtype)


def shares(starts, rest, own, partner, own_weight, partner_weight):
    rows, width = own.shape
    steps = starts + rest
    outs = [
        jax.ShapeDtypeStruct((rows, width), BF16 if i < len(starts) else F32)
        for i in range(len(steps))
    ]
    return pl.pallas_call(
        functools.partial(share_kernel, steps),
        out_shape=outs,
        in_specs=[VMEM] * 4,
        out_specs=[VMEM] * len(outs),
        compiler_params=pltpu.CompilerParams(vmem_limit_bytes=24 << 20),
        cost_estimate=pl.CostEstimate(
            flops=4 * rows * width * width * len(steps), bytes_accessed=6 << 20, transcendentals=0
        ),
        name="shares",
    )(own, partner, own_weight, partner_weight)


def reduce_ring(attended, partner_attended, own_weight, partner_weight, ring):
    up = [(i, (i + 1) % ring) for i in range(ring)]
    down = [(i, (i - 1) % ring) for i in range(ring)]
    far = ring // 2
    chains = [(0, 1, far), (1, -1, far), (0, -1, far - 1), (1, 1, far - 1)]
    held, part = {}, {}
    for half in range(2):
        mine = [(way, first) for rows, way, first in chains if rows == half]
        starts = [way * first % ring for way, first in mine]
        rest = [k for k in range(ring) if k not in starts]
        made = shares(
            starts, rest, attended[half], partner_attended[half], own_weight, partner_weight
        )
        for i, (way, _) in enumerate(mine):
            held[half, way] = made[i]
        part.update({(half, k): made[len(starts) + i] for i, k in enumerate(rest)})
    for distance in range(far, 0, -1):
        for half, way, first in chains:
            if distance > first:
                continue
            if distance < first:
                total = held[half, way].astype(F32) + part[half, way * distance % ring]
                held[half, way] = total.astype(BF16)
            held[half, way] = lax.ppermute(held[half, way], "z", up if way == 1 else down)
    out = [
        (part[half, 0] + held[half, 1].astype(F32) + held[half, -1].astype(F32)).astype(BF16)
        for half in range(2)
    ]
    return jnp.concatenate(out, axis=0)


def local(
    tokens,
    query_weight,
    key_weight,
    value_weight,
    out_weight,
    codes,
    scales,
    block_len,
    nbr_owner,
    nbr_block,
):
    width = query_weight.shape[1]
    ring = lax.axis_size("z")
    cores = lax.axis_size("c")
    shards = lax.axis_size(DB)
    here, core = lax.axis_index("z"), lax.axis_index("c")
    swap = [(i, (i + 1) % cores) for i in range(cores)]

    gathered = lax.all_gather(tokens, ("z", "c"), axis=1, tiled=True)

    owners = nbr_owner.T.reshape(-1)
    wanted_blocks = nbr_block.T.reshape(-1)
    notes = jnp.concatenate([owners, wanted_blocks, block_len])
    notes = jnp.broadcast_to(notes[None, :], (shards, notes.shape[0]))
    heard = lax.all_to_all(notes, DB, split_axis=0, concat_axis=0, tiled=True)
    projected = project_blocks(codes, scales, key_weight, value_weight)
    sent = select_blocks(lax.axis_index(DB).astype(jnp.int32).reshape(1), heard, projected)
    rows = lax.all_to_all(sent, DB, split_axis=0, concat_axis=0, tiled=True)
    rows = rows.reshape(shards * NBRS, NBR_LEN, 2 * width)

    order = jnp.arange(owners.shape[0], dtype=jnp.int32)
    earlier = jnp.sum(
        ((owners[:, None] == owners[None, :]) & (order[:, None] > order[None, :])).astype(jnp.int32),
        axis=1,
    )
    slot_index = owners * NBRS + earlier
    all_lengths = heard[:, 2 * owners.shape[0] :].reshape(-1)
    block_ids = owners * block_len.shape[0] + wanted_blocks
    ids = jnp.arange(all_lengths.shape[0], dtype=jnp.int32)
    lengths = jnp.sum(
        jnp.where(block_ids[:, None] == ids[None, :], all_lengths[None, :], 0), axis=1
    )

    own_weight, lent_weight = relay(jnp.stack([here, core]).astype(jnp.int32), out_weight, ring)
    partner_weight = lax.ppermute(lent_weight, "c", swap)

    queries = project_queries(gathered, query_weight)
    attended = [attend(part, 2, slot_index, lengths, queries, rows) for part in range(2)]
    partner_attended = [lax.ppermute(part, "c", swap) for part in attended]
    return reduce_ring(attended, partner_attended, own_weight, partner_weight, ring)


def solution(mesh):
    grid = Mesh(mesh.devices.reshape(4, 4, 8, 2), ("y", "x", "z", "c"))
    head = ("z", "c")
    placed = (
        P(DB, head),
        P(None, head),
        P(None, head),
        P(None, head),
        P(head, None),
        P(DB, None, None),
        P(DB, None),
        P(DB),
        P(DB, None),
        P(DB, None),
    )
    return jax.shard_map(
        local, mesh=grid, in_specs=placed, out_specs=P(DB, head), check_vma=False
    )
```

```python
import functools
import math

import jax
import jax.numpy as jnp
from jax import lax
from jax.experimental import pallas as pl
from jax.experimental.pallas import tpu as pltpu
from jax.sharding import Mesh
from jax.sharding import PartitionSpec as P

HD = 128
ENC = 896
GROUP = 128
SPAN = 64
NBR_LEN = 128
NBRS = 2
DB = ("y", "x")
F32 = jnp.float32
BF16 = jnp.bfloat16
VMEM = pl.BlockSpec(memory_space=pltpu.VMEM)
SMEM = pl.BlockSpec(memory_space=pltpu.SMEM)
ANY = pl.BlockSpec(memory_space=pl.ANY)


def unit(values):
    return values * lax.rsqrt(jnp.mean(values * values, axis=-1, keepdims=True) + 1e-06)


def project_kernel(scales_ref, codes_ref, key_ref, value_ref, out_ref, enc_ref):
    step = pl.program_id(0)
    blocks = codes_ref.shape[0]
    for b in range(blocks):
        for g in range(ENC // GROUP):
            cols = slice(g * GROUP, (g + 1) * GROUP)
            scaled = codes_ref[b, :, cols].astype(F32) * scales_ref[step * blocks + b, g]
            enc_ref[b * NBR_LEN : (b + 1) * NBR_LEN, cols] = scaled.astype(BF16)
    enc = enc_ref[...]
    keys = jnp.dot(enc, key_ref[...], preferred_element_type=F32)
    values = jnp.dot(enc, value_ref[...], preferred_element_type=F32).astype(BF16)
    width = key_ref.shape[1]
    for b in range(blocks):
        rows = slice(b * NBR_LEN, (b + 1) * NBR_LEN)
        for h in range(width // HD):
            cols = slice(h * HD, (h + 1) * HD)
            out_ref[b, :, cols] = unit(keys[rows, cols]).astype(BF16)
        out_ref[b, :, width : 2 * width] = values[rows]


def project_blocks(codes, scales, key_weight, value_weight):
    count, width, per = codes.shape[0], key_weight.shape[1], 2
    return pl.pallas_call(
        project_kernel,
        grid=(count // per,),
        out_shape=jax.ShapeDtypeStruct((count, NBR_LEN, 2 * width), BF16),
        in_specs=[
            SMEM,
            pl.BlockSpec((per, NBR_LEN, ENC), lambda i: (i, 0, 0)),
            pl.BlockSpec((ENC, width), lambda i: (0, 0)),
            pl.BlockSpec((ENC, width), lambda i: (0, 0)),
        ],
        out_specs=pl.BlockSpec((per, NBR_LEN, 2 * width), lambda i: (i, 0, 0)),
        scratch_shapes=[pltpu.VMEM((per * NBR_LEN, ENC), BF16)],
        cost_estimate=pl.CostEstimate(
            flops=2 * count * NBR_LEN * ENC * 2 * width, bytes_accessed=5 << 20, transcendentals=0
        ),
        name="project_blocks",
    )(scales, codes, key_weight, value_weight)


def select_kernel(place_ref, heard_ref, rows_ref, out_ref, sems):
    shards, requests = out_ref.shape[0], out_ref.shape[0] * NBRS
    here = place_ref[0]
    copies = []
    for e in range(shards):
        first, last = jnp.int32(-1), jnp.int32(0)
        for r in range(requests):
            mine = heard_ref[e, r] == here
            block = heard_ref[e, requests + r]
            first = jnp.where(mine & (first < 0), block, first)
            last = jnp.where(mine, block, last)
        for s, block in enumerate((jnp.maximum(first, 0), last)):
            copy = pltpu.make_async_copy(rows_ref.at[block], out_ref.at[e, s], sems.at[e, s])
            copy.start()
            copies.append(copy)
    for copy in copies:
        copy.wait()


def select_blocks(place, heard, rows):
    shards = heard.shape[0]
    return pl.pallas_call(
        select_kernel,
        out_shape=jax.ShapeDtypeStruct((shards, NBRS) + rows.shape[1:], BF16),
        in_specs=[SMEM, SMEM, VMEM],
        out_specs=ANY,
        scratch_shapes=[pltpu.SemaphoreType.DMA((shards, NBRS))],
        cost_estimate=pl.CostEstimate(flops=0, bytes_accessed=9 << 20, transcendentals=0),
        name="select_blocks",
    )(place, heard, rows)


def query_kernel(place_ref, *refs):
    ring = len(refs) - 4
    weight_ref, partner_ref, own_ref, lent_ref = refs[ring:]
    here, core = place_ref[0], place_ref[1]
    own, lent = None, None
    for k in range(ring):
        chip = lax.rem(here + ring - k, ring)
        part = jnp.dot(refs[k][...], weight_ref[chip, core], preferred_element_type=F32)
        own = part if own is None else own + part
        part = jnp.dot(refs[k][...], partner_ref[chip], preferred_element_type=F32)
        lent = part if lent is None else lent + part
    own_ref[...] = own
    lent_ref[...] = lent


def project_queries(place, pieces, weight, partner_weight):
    rows, depth = pieces[0].shape
    width, tile = weight.shape[-1], 256
    out = jax.ShapeDtypeStruct((rows, width), F32)
    return pl.pallas_call(
        query_kernel,
        grid=(rows // tile,),
        out_shape=(out, out),
        in_specs=[SMEM]
        + [pl.BlockSpec((tile, depth), lambda i: (i, 0)) for _ in pieces]
        + [
            pl.BlockSpec(weight.shape, lambda i: (0, 0, 0, 0)),
            pl.BlockSpec(partner_weight.shape, lambda i: (0, 0, 0)),
        ],
        out_specs=[pl.BlockSpec((tile, width), lambda i: (i, 0))] * 2,
        compiler_params=pltpu.CompilerParams(vmem_limit_bytes=24 << 20),
        cost_estimate=pl.CostEstimate(
            flops=4 * rows * depth * width * len(pieces), bytes_accessed=9 << 20, transcendentals=0
        ),
        name="project_queries",
    )(place, *pieces, weight, partner_weight)


def attend_kernel(
    first, slot_ref, length_ref, own_ref, lent_ref, rows_ref, out_ref, query_ref, held_ref, sems
):
    spans = slot_ref.shape[0] // NBRS
    count = sems.shape[0] // NBRS
    width = out_ref.shape[1]
    keys = NBRS * NBR_LEN
    factor = 2.0 / math.sqrt(HD)
    copies = []
    for c in range(count):
        for n in range(NBRS):
            copy = pltpu.make_async_copy(
                rows_ref.at[slot_ref[n * spans + first + c]],
                held_ref.at[pl.ds((c * NBRS + n) * NBR_LEN, NBR_LEN)],
                sems.at[c * NBRS + n],
            )
            copy.start()
            copies.append(copy)
    for h in range(width // HD):
        cols = slice(h * HD, (h + 1) * HD)
        query_ref[:, cols] = unit(own_ref[:, cols] + lent_ref[:, cols]).astype(BF16)
    places = lax.broadcasted_iota(jnp.int32, (SPAN, keys), 1)
    group = 4
    for start in range(0, count, group):
        members = [(c, h) for c in range(start, start + group) for h in range(width // HD)]
        for copy in copies[start * NBRS : (start + group) * NBRS]:
            copy.wait()
        raised = []
        for c, h in members:
            scores = lax.dot_general(
                query_ref[c * SPAN : (c + 1) * SPAN, h * HD : (h + 1) * HD],
                held_ref[c * keys : (c + 1) * keys, h * HD : (h + 1) * HD],
                (((1,), (1,)), ((), ())),
                preferred_element_type=F32,
            )
            ends = [length_ref[n * spans + first + c] + n * NBR_LEN for n in range(NBRS)]
            valid = (places < ends[0]) | ((places >= NBR_LEN) & (places < ends[1]))
            raised.append(jnp.where(valid, jnp.exp(scores * factor), 0.0))
        weights = [
            (part * (1.0 / jnp.sum(part, axis=-1, keepdims=True))).astype(BF16) for part in raised
        ]
        for (c, h), part in zip(members, weights):
            cols = slice(width + h * HD, width + (h + 1) * HD)
            result = jnp.dot(
                part, held_ref[c * keys : (c + 1) * keys, cols], preferred_element_type=F32
            )
            out_ref[c * SPAN : (c + 1) * SPAN, h * HD : (h + 1) * HD] = result.astype(BF16)


def attend(part, parts, slot_index, lengths, own, lent, rows):
    tokens, width = own.shape[0] // parts, own.shape[1]
    count = tokens // SPAN
    requests = count * NBRS
    return pl.pallas_call(
        functools.partial(attend_kernel, part * count),
        grid=(1,),
        out_shape=jax.ShapeDtypeStruct((tokens, width), BF16),
        in_specs=[SMEM, SMEM] + [pl.BlockSpec((tokens, width), lambda i: (part, 0))] * 2 + [ANY],
        out_specs=pl.BlockSpec((tokens, width), lambda i: (0, 0)),
        scratch_shapes=[
            pltpu.VMEM((tokens, width), BF16),
            pltpu.VMEM((requests * NBR_LEN, rows.shape[2]), BF16),
            pltpu.SemaphoreType.DMA((requests,)),
        ],
        compiler_params=pltpu.CompilerParams(vmem_limit_bytes=24 << 20),
        cost_estimate=pl.CostEstimate(
            flops=4 * tokens * NBRS * NBR_LEN * width, bytes_accessed=3 << 20, transcendentals=0
        ),
        name="attend",
    )(slot_index, lengths, own, lent, rows)


def relay_kernel(place_ref, weight_ref, own_ref, lent_ref):
    here, core = place_ref[0], place_ref[1]
    ring, _, width = own_ref.shape
    for k in range(ring):
        chip = lax.rem(here + k, ring)
        for ref, which in ((own_ref, core), (lent_ref, 1 - core)):
            cols = pl.ds(pl.multiple_of((chip * 2 + which) * width, width), width)
            ref[k] = weight_ref[:, cols]


def relay(place, weight, ring):
    depth = weight.shape[0]
    shape = jax.ShapeDtypeStruct((ring, depth, weight.shape[1] // (2 * ring)), BF16)
    return pl.pallas_call(
        relay_kernel,
        out_shape=(shape, shape),
        in_specs=[SMEM, VMEM],
        out_specs=(VMEM, VMEM),
        compiler_params=pltpu.CompilerParams(vmem_limit_bytes=16 << 20),
        cost_estimate=pl.CostEstimate(flops=0, bytes_accessed=4 << 20, transcendentals=0),
        name="relay",
    )(place, weight)


def share_kernel(steps, own_ref, partner_ref, own_w_ref, partner_w_ref, *out_refs):
    for step, ref in zip(steps, out_refs):
        ref[...] = (
            jnp.dot(own_ref[...], own_w_ref[step], preferred_element_type=F32)
            + jnp.dot(partner_ref[...], partner_w_ref[step], preferred_element_type=F32)
        ).astype(ref.dtype)


def shares(starts, rest, own, partner, own_weight, partner_weight):
    rows, width = own.shape
    steps = starts + rest
    outs = [
        jax.ShapeDtypeStruct((rows, width), BF16 if i < len(starts) else F32)
        for i in range(len(steps))
    ]
    return pl.pallas_call(
        functools.partial(share_kernel, steps),
        out_shape=outs,
        in_specs=[VMEM] * 4,
        out_specs=[VMEM] * len(outs),
        compiler_params=pltpu.CompilerParams(vmem_limit_bytes=24 << 20),
        cost_estimate=pl.CostEstimate(
            flops=4 * rows * width * width * len(steps), bytes_accessed=6 << 20, transcendentals=0
        ),
        name="shares",
    )(own, partner, own_weight, partner_weight)


def reduce_ring(attended, partner_attended, own_weight, partner_weight, ring):
    up = [(i, (i + 1) % ring) for i in range(ring)]
    down = [(i, (i - 1) % ring) for i in range(ring)]
    far = ring // 2
    chains = [(0, 1, far), (1, -1, far), (0, -1, far - 1), (1, 1, far - 1)]
    held, part = {}, {}
    for half in range(2):
        mine = [(way, first) for rows, way, first in chains if rows == half]
        starts = [way * first % ring for way, first in mine]
        rest = [k for k in range(ring) if k not in starts]
        made = shares(
            starts, rest, attended[half], partner_attended[half], own_weight, partner_weight
        )
        for i, (way, _) in enumerate(mine):
            held[half, way] = made[i]
        part.update({(half, k): made[len(starts) + i] for i, k in enumerate(rest)})
    for distance in range(far, 0, -1):
        for half, way, first in chains:
            if distance > first:
                continue
            if distance < first:
                total = held[half, way].astype(F32) + part[half, way * distance % ring]
                held[half, way] = total.astype(BF16)
            held[half, way] = lax.ppermute(held[half, way], "z", up if way == 1 else down)
    out = [
        (part[half, 0] + held[half, 1].astype(F32) + held[half, -1].astype(F32)).astype(BF16)
        for half in range(2)
    ]
    return jnp.concatenate(out, axis=0)


def local(
    tokens,
    query_weight,
    key_weight,
    value_weight,
    out_weight,
    codes,
    scales,
    block_len,
    nbr_owner,
    nbr_block,
):
    width = query_weight.shape[1]
    ring = lax.axis_size("z")
    cores = lax.axis_size("c")
    shards = lax.axis_size(DB)
    here, core = lax.axis_index("z"), lax.axis_index("c")
    swap = [(i, (i + 1) % cores) for i in range(cores)]

    place = jnp.stack([here, core]).astype(jnp.int32)
    owners = nbr_owner.T.reshape(-1)
    wanted_blocks = nbr_block.T.reshape(-1)
    notes = jnp.concatenate([owners, wanted_blocks, block_len])
    notes = jnp.broadcast_to(notes[None, :], (shards, notes.shape[0]))
    heard = lax.all_to_all(notes, DB, split_axis=0, concat_axis=0, tiled=True)
    projected = project_blocks(codes, scales, key_weight, value_weight)
    sent = select_blocks(lax.axis_index(DB).astype(jnp.int32).reshape(1), heard, projected)
    up = [(i, (i + 1) % ring) for i in range(ring)]
    down = [(i, (i - 1) % ring) for i in range(ring)]
    pieces = {0: tokens, 1: lax.ppermute(tokens, "z", up)}
    pieces[ring - 1] = lax.ppermute(tokens, "z", down)
    sent, pieces[1], pieces[ring - 1] = lax.optimization_barrier(
        (sent, pieces[1], pieces[ring - 1])
    )
    rows = lax.all_to_all(sent, DB, split_axis=0, concat_axis=0, tiled=True)
    rows = rows.reshape(shards * NBRS, NBR_LEN, 2 * width)

    order = jnp.arange(owners.shape[0], dtype=jnp.int32)
    earlier = jnp.sum(
        ((owners[:, None] == owners[None, :]) & (order[:, None] > order[None, :])).astype(jnp.int32),
        axis=1,
    )
    slot_index = owners * NBRS + earlier
    all_lengths = heard[:, 2 * owners.shape[0] :].reshape(-1)
    block_ids = owners * block_len.shape[0] + wanted_blocks
    ids = jnp.arange(all_lengths.shape[0], dtype=jnp.int32)
    lengths = jnp.sum(
        jnp.where(block_ids[:, None] == ids[None, :], all_lengths[None, :], 0), axis=1
    )

    for k in range(2, ring // 2 + 1):
        pieces[k] = lax.ppermute(pieces[k - 1], "z", up)
        if k < ring // 2:
            pieces[ring - k] = lax.ppermute(pieces[ring - k + 1], "z", down)
    by_core = query_weight.reshape(ring, cores, width, width)
    lent_rows = lax.dynamic_index_in_dim(by_core, 1 - core, 1, keepdims=False)
    partner_rows = lax.ppermute(lent_rows, "c", swap)

    own_weight, lent_weight = relay(place, out_weight, ring)
    partner_weight = lax.ppermute(lent_weight, "c", swap)

    own, lent = project_queries(place, [pieces[k] for k in range(ring)], by_core, partner_rows)
    lent = lax.ppermute(lent, "c", swap)
    attended = [attend(part, 2, slot_index, lengths, own, lent, rows) for part in range(2)]
    partner_attended = [lax.ppermute(part, "c", swap) for part in attended]
    return reduce_ring(attended, partner_attended, own_weight, partner_weight, ring)


def solution(mesh):
    grid = Mesh(mesh.devices.reshape(4, 4, 8, 2), ("y", "x", "z", "c"))
    head = ("z", "c")
    placed = (
        P(DB, head),
        P(None, head),
        P(None, head),
        P(None, head),
        P(head, None),
        P(DB, None, None),
        P(DB, None),
        P(DB),
        P(DB, None),
        P(DB, None),
    )
    return jax.shard_map(
        local, mesh=grid, in_specs=placed, out_specs=P(DB, head), check_vma=False
    )
```

```python
import functools
import math

import jax
import jax.numpy as jnp
from jax import lax
from jax.experimental import pallas as pl
from jax.experimental.pallas import tpu as pltpu
from jax.sharding import Mesh
from jax.sharding import PartitionSpec as P

HD = 128
ENC = 896
GROUP = 128
SPAN = 64
NBR_LEN = 128
NBRS = 2
DB = ("y", "x")
F32 = jnp.float32
BF16 = jnp.bfloat16
VMEM = pl.BlockSpec(memory_space=pltpu.VMEM)
SMEM = pl.BlockSpec(memory_space=pltpu.SMEM)
ANY = pl.BlockSpec(memory_space=pl.ANY)


def unit(values):
    return values * lax.rsqrt(jnp.mean(values * values, axis=-1, keepdims=True) + 1e-06)


def project_kernel(scales_ref, codes_ref, key_ref, value_ref, out_ref, enc_ref):
    step = pl.program_id(0)
    blocks = codes_ref.shape[0]
    for b in range(blocks):
        for g in range(ENC // GROUP):
            cols = slice(g * GROUP, (g + 1) * GROUP)
            scaled = codes_ref[b, :, cols].astype(F32) * scales_ref[step * blocks + b, g]
            enc_ref[b * NBR_LEN : (b + 1) * NBR_LEN, cols] = scaled.astype(BF16)
    enc = enc_ref[...]
    keys = jnp.dot(enc, key_ref[...], preferred_element_type=F32)
    values = jnp.dot(enc, value_ref[...], preferred_element_type=F32).astype(BF16)
    width = key_ref.shape[1]
    for b in range(blocks):
        rows = slice(b * NBR_LEN, (b + 1) * NBR_LEN)
        for h in range(width // HD):
            cols = slice(h * HD, (h + 1) * HD)
            out_ref[b, :, cols] = unit(keys[rows, cols]).astype(BF16)
        out_ref[b, :, width : 2 * width] = values[rows]


def project_blocks(codes, scales, key_weight, value_weight):
    count, width, per = codes.shape[0], key_weight.shape[1], 2
    return pl.pallas_call(
        project_kernel,
        grid=(count // per,),
        out_shape=jax.ShapeDtypeStruct((count, NBR_LEN, 2 * width), BF16),
        in_specs=[
            SMEM,
            pl.BlockSpec((per, NBR_LEN, ENC), lambda i: (i, 0, 0)),
            pl.BlockSpec((ENC, width), lambda i: (0, 0)),
            pl.BlockSpec((ENC, width), lambda i: (0, 0)),
        ],
        out_specs=pl.BlockSpec((per, NBR_LEN, 2 * width), lambda i: (i, 0, 0)),
        scratch_shapes=[pltpu.VMEM((per * NBR_LEN, ENC), BF16)],
        cost_estimate=pl.CostEstimate(
            flops=2 * count * NBR_LEN * ENC * 2 * width, bytes_accessed=5 << 20, transcendentals=0
        ),
        name="project_blocks",
    )(scales, codes, key_weight, value_weight)


def select_kernel(place_ref, heard_ref, rows_ref, out_ref, sems):
    shards, spans, blocks = out_ref.shape[0], heard_ref.shape[2], rows_ref.shape[0]
    lowest = place_ref[0] * blocks
    copies = []
    for e in range(shards):
        first, last = jnp.int32(-1), jnp.int32(0)
        for n in range(NBRS):
            for c in range(spans):
                block = heard_ref[e, n, c] - lowest
                mine = (block >= 0) & (block < blocks)
                first = jnp.where(mine & (first < 0), block, first)
                last = jnp.where(mine, block, last)
        for s, block in enumerate((jnp.maximum(first, 0), last)):
            copy = pltpu.make_async_copy(rows_ref.at[block], out_ref.at[e, s], sems.at[e, s])
            copy.start()
            copies.append(copy)
    for copy in copies:
        copy.wait()


def select_blocks(place, heard, rows):
    shards = heard.shape[0]
    return pl.pallas_call(
        select_kernel,
        out_shape=jax.ShapeDtypeStruct((shards, NBRS) + rows.shape[1:], BF16),
        in_specs=[SMEM, SMEM, VMEM],
        out_specs=ANY,
        scratch_shapes=[pltpu.SemaphoreType.DMA((shards, NBRS))],
        cost_estimate=pl.CostEstimate(flops=0, bytes_accessed=9 << 20, transcendentals=0),
        name="select_blocks",
    )(place, heard, rows)


def query_kernel(steps, place_ref, *refs):
    pieces, (weight_ref, partner_ref), sums = refs[: len(steps)], refs[len(steps) :][:2], refs[len(steps) + 2 :]
    ring = weight_ref.shape[0]
    for matrix_ref, old_ref, new_ref in zip((weight_ref, partner_ref), sums[:2], sums[-2:]):
        total = old_ref[...] if len(sums) > 2 else None
        for step, piece in zip(steps, pieces):
            chip = lax.rem(place_ref[0] + ring - step, ring)
            part = jnp.dot(piece[...], matrix_ref[chip], preferred_element_type=F32)
            total = part if total is None else total + part
        new_ref[...] = total


def add_queries(place, steps, pieces, weight, partner_weight, sums):
    rows, depth = pieces[0].shape
    width = weight.shape[-1]
    out = jax.ShapeDtypeStruct((rows, width), F32)
    held = 3 + len(steps)
    return pl.pallas_call(
        functools.partial(query_kernel, steps),
        out_shape=(out, out),
        in_specs=[SMEM] + [VMEM] * (len(steps) + 2 + len(sums)),
        out_specs=(VMEM, VMEM),
        input_output_aliases={held + i: i for i in range(len(sums))},
        compiler_params=pltpu.CompilerParams(vmem_limit_bytes=12 << 20),
        cost_estimate=pl.CostEstimate(
            flops=4 * rows * depth * width * len(steps), bytes_accessed=4 << 20, transcendentals=0
        ),
        name="add_queries",
    )(place, *pieces, weight, partner_weight, *sums)


def attend_kernel(
    first, slot_ref, length_ref, own_ref, lent_ref, rows_ref, out_ref, query_ref, held_ref, sems
):
    spans = slot_ref.shape[0] // NBRS
    count = sems.shape[0] // NBRS
    width = out_ref.shape[1]
    keys = NBRS * NBR_LEN
    factor = 2.0 / math.sqrt(HD)
    copies = []
    for c in range(count):
        for n in range(NBRS):
            copy = pltpu.make_async_copy(
                rows_ref.at[slot_ref[n * spans + first + c]],
                held_ref.at[pl.ds((c * NBRS + n) * NBR_LEN, NBR_LEN)],
                sems.at[c * NBRS + n],
            )
            copy.start()
            copies.append(copy)
    for h in range(width // HD):
        cols = slice(h * HD, (h + 1) * HD)
        query_ref[:, cols] = unit(own_ref[:, cols] + lent_ref[:, cols]).astype(BF16)
    places = lax.broadcasted_iota(jnp.int32, (SPAN, keys), 1)
    group = 4
    for start in range(0, count, group):
        members = [(c, h) for c in range(start, start + group) for h in range(width // HD)]
        for copy in copies[start * NBRS : (start + group) * NBRS]:
            copy.wait()
        raised = []
        for c, h in members:
            scores = lax.dot_general(
                query_ref[c * SPAN : (c + 1) * SPAN, h * HD : (h + 1) * HD],
                held_ref[c * keys : (c + 1) * keys, h * HD : (h + 1) * HD],
                (((1,), (1,)), ((), ())),
                preferred_element_type=F32,
            )
            ends = [length_ref[n * spans + first + c] + n * NBR_LEN for n in range(NBRS)]
            valid = (places < ends[0]) | ((places >= NBR_LEN) & (places < ends[1]))
            raised.append(jnp.where(valid, jnp.exp(scores * factor), 0.0))
        weights = [
            (part * (1.0 / jnp.sum(part, axis=-1, keepdims=True))).astype(BF16) for part in raised
        ]
        for (c, h), part in zip(members, weights):
            cols = slice(width + h * HD, width + (h + 1) * HD)
            result = jnp.dot(
                part, held_ref[c * keys : (c + 1) * keys, cols], preferred_element_type=F32
            )
            out_ref[c * SPAN : (c + 1) * SPAN, h * HD : (h + 1) * HD] = result.astype(BF16)


def attend(part, slot_index, lengths, own, lent, rows):
    tokens, width = own.shape
    count = tokens // SPAN
    requests = count * NBRS
    return pl.pallas_call(
        functools.partial(attend_kernel, part * count),
        out_shape=jax.ShapeDtypeStruct((tokens, width), BF16),
        in_specs=[SMEM, SMEM, VMEM, VMEM, ANY],
        out_specs=VMEM,
        scratch_shapes=[
            pltpu.VMEM((tokens, width), BF16),
            pltpu.VMEM((requests * NBR_LEN, rows.shape[2]), BF16),
            pltpu.SemaphoreType.DMA((requests,)),
        ],
        compiler_params=pltpu.CompilerParams(vmem_limit_bytes=12 << 20),
        cost_estimate=pl.CostEstimate(
            flops=4 * tokens * NBRS * NBR_LEN * width, bytes_accessed=3 << 20, transcendentals=0
        ),
        name="attend",
    )(slot_index, lengths, own, lent, rows)


def relay_kernel(place_ref, weight_ref, own_ref, lent_ref):
    here, core = place_ref[0], place_ref[1]
    ring, _, width = own_ref.shape
    for k in range(ring):
        chip = lax.rem(here + k, ring)
        for ref, which in ((own_ref, core), (lent_ref, 1 - core)):
            cols = pl.ds(pl.multiple_of((chip * 2 + which) * width, width), width)
            ref[k] = weight_ref[:, cols]


def relay(place, weight, ring):
    depth = weight.shape[0]
    shape = jax.ShapeDtypeStruct((ring, depth, weight.shape[1] // (2 * ring)), BF16)
    return pl.pallas_call(
        relay_kernel,
        out_shape=(shape, shape),
        in_specs=[SMEM, VMEM],
        out_specs=(VMEM, VMEM),
        compiler_params=pltpu.CompilerParams(vmem_limit_bytes=16 << 20),
        cost_estimate=pl.CostEstimate(flops=0, bytes_accessed=4 << 20, transcendentals=0),
        name="relay",
    )(place, weight)


def share_kernel(steps, own_ref, partner_ref, own_w_ref, partner_w_ref, *out_refs):
    for step, ref in zip(steps, out_refs):
        ref[...] = (
            jnp.dot(own_ref[...], own_w_ref[step], preferred_element_type=F32)
            + jnp.dot(partner_ref[...], partner_w_ref[step], preferred_element_type=F32)
        ).astype(ref.dtype)


def shares(starts, rest, own, partner, own_weight, partner_weight):
    rows, width = own.shape
    steps = starts + rest
    outs = [
        jax.ShapeDtypeStruct((rows, width), BF16 if i < len(starts) else F32)
        for i in range(len(steps))
    ]
    return pl.pallas_call(
        functools.partial(share_kernel, steps),
        out_shape=outs,
        in_specs=[VMEM] * 4,
        out_specs=[VMEM] * len(outs),
        compiler_params=pltpu.CompilerParams(vmem_limit_bytes=12 << 20),
        cost_estimate=pl.CostEstimate(
            flops=4 * rows * width * width * len(steps), bytes_accessed=6 << 20, transcendentals=0
        ),
        name="shares",
    )(own, partner, own_weight, partner_weight)


def reduce_ring(attended, partner_attended, own_weight, partner_weight, ring):
    up = [(i, (i + 1) % ring) for i in range(ring)]
    down = [(i, (i - 1) % ring) for i in range(ring)]
    far = ring // 2
    chains = [(0, 1, far), (1, -1, far), (0, -1, far - 1), (1, 1, far - 1)]
    held, part = {}, {}
    for half in range(2):
        mine = [(way, first) for rows, way, first in chains if rows == half]
        starts = [way * first % ring for way, first in mine]
        rest = [k for k in range(ring) if k not in starts]
        made = shares(
            starts, rest, attended[half], partner_attended[half], own_weight, partner_weight
        )
        for i, (way, _) in enumerate(mine):
            held[half, way] = made[i]
        part.update({(half, k): made[len(starts) + i] for i, k in enumerate(rest)})
    for distance in range(far, 0, -1):
        for half, way, first in chains:
            if distance > first:
                continue
            if distance < first:
                total = held[half, way].astype(F32) + part[half, way * distance % ring]
                held[half, way] = total.astype(BF16)
            held[half, way] = lax.ppermute(held[half, way], "z", up if way == 1 else down)
    out = [
        (part[half, 0] + held[half, 1].astype(F32) + held[half, -1].astype(F32)).astype(BF16)
        for half in range(2)
    ]
    return jnp.concatenate(out, axis=0)


def local(
    tokens,
    query_weight,
    key_weight,
    value_weight,
    out_weight,
    codes,
    scales,
    block_len,
    nbr_owner,
    nbr_block,
):
    width = query_weight.shape[1]
    ring = lax.axis_size("z")
    cores = lax.axis_size("c")
    shards = lax.axis_size(DB)
    here, core = lax.axis_index("z"), lax.axis_index("c")
    swap = [(i, (i + 1) % cores) for i in range(cores)]

    place = jnp.stack([here, core]).astype(jnp.int32)
    spans, blocks = nbr_owner.shape[0], block_len.shape[0]

    block_ids = nbr_owner.T * blocks + nbr_block.T
    notes = jnp.concatenate([block_ids, jnp.pad(block_len, (0, spans - blocks))[None, :]], axis=0)
    notes = jnp.broadcast_to(notes[None], (shards,) + notes.shape)
    heard = lax.all_to_all(notes, DB, split_axis=0, concat_axis=0, tiled=True)
    projected = project_blocks(codes, scales, key_weight, value_weight)

    own_weight, lent_weight = relay(place, out_weight, ring)
    by_core = query_weight.reshape(ring, cores, width, width)
    own_rows = lax.dynamic_index_in_dim(by_core, core, 1, keepdims=False)
    lent_rows = lax.dynamic_index_in_dim(by_core, 1 - core, 1, keepdims=False)
    projected, own_weight, lent_weight, own_rows, lent_rows = lax.optimization_barrier(
        (projected, own_weight, lent_weight, own_rows, lent_rows)
    )
    sent = select_blocks(lax.axis_index(DB).astype(jnp.int32).reshape(1), heard, projected)
    _, tokens, lent_weight, lent_rows = lax.optimization_barrier(
        (sent, tokens, lent_weight, lent_rows)
    )
    rows = lax.all_to_all(sent, DB, split_axis=0, concat_axis=0, tiled=True)
    rows = rows.reshape(shards * NBRS, NBR_LEN, 2 * width)

    owners = nbr_owner.T.reshape(-1)
    block_ids = block_ids.reshape(-1)
    order = jnp.arange(owners.shape[0], dtype=jnp.int32)
    earlier = jnp.sum(
        ((owners[:, None] == owners[None, :]) & (order[:, None] > order[None, :])).astype(jnp.int32),
        axis=1,
    )
    slot_index = owners * NBRS + earlier
    all_lengths = heard[:, NBRS, :blocks].reshape(-1)
    ids = jnp.arange(all_lengths.shape[0], dtype=jnp.int32)
    lengths = jnp.sum(
        jnp.where(block_ids[:, None] == ids[None, :], all_lengths[None, :], 0), axis=1
    )

    up = [(i, (i + 1) % ring) for i in range(ring)]
    down = [(i, (i - 1) % ring) for i in range(ring)]
    far = ring // 2
    partner_rows = lax.ppermute(lent_rows, "c", swap)
    partner_weight = lax.ppermute(lent_weight, "c", swap)
    pieces = [{0: half} for half in jnp.split(tokens, 2)]
    sums = [(), ()]

    def add(half, steps):
        parts = [pieces[half][i] for i in steps]
        sums[half] = add_queries(place, steps, parts, own_rows, partner_rows, sums[half])

    for k in range(1, far + 1):
        for half in range(2):
            part = pieces[half]
            if k > 1:
                before, after = k - 1, ring - k + 1
                part[before], part[after], sums[half] = lax.optimization_barrier(
                    (part[before], part[after], sums[half])
                )
            if k < far or half == 0:
                part[k] = lax.ppermute(part[k - 1], "z", up)
            if k < far or half == 1:
                part[ring - k] = lax.ppermute(part[(ring - k + 1) % ring], "z", down)
            if k > 1:
                add(half, ([0] if k == 2 else []) + [before, after])
    for half in range(2):
        add(half, [far])
    attended = []
    for half in range(2):
        own, lent = sums[half]
        lent = lax.ppermute(lent, "c", swap)
        attended.append(attend(half, slot_index, lengths, own, lent, rows))
    partner_attended = [lax.ppermute(part, "c", swap) for part in attended]
    return reduce_ring(attended, partner_attended, own_weight, partner_weight, ring)


def solution(mesh):
    grid = Mesh(mesh.devices.reshape(4, 4, 8, 2), ("y", "x", "z", "c"))
    head = ("z", "c")
    placed = (
        P(DB, head),
        P(None, head),
        P(None, head),
        P(None, head),
        P(head, None),
        P(DB, None, None),
        P(DB, None),
        P(DB),
        P(DB, None),
        P(DB, None),
    )
    return jax.shard_map(
        local, mesh=grid, in_specs=placed, out_specs=P(DB, head), check_vma=False
    )
```

```python
import functools
import math

import jax
import jax.numpy as jnp
from jax import lax
from jax.experimental import pallas as pl
from jax.experimental.pallas import tpu as pltpu
from jax.sharding import Mesh
from jax.sharding import PartitionSpec as P

HD = 128
ENC = 896
GROUP = 128
SPAN = 64
NBR_LEN = 128
NBRS = 2
DB = ("y", "x")
F32 = jnp.float32
BF16 = jnp.bfloat16
VMEM = pl.BlockSpec(memory_space=pltpu.VMEM)
SMEM = pl.BlockSpec(memory_space=pltpu.SMEM)
ANY = pl.BlockSpec(memory_space=pl.ANY)


def unit(values):
    return values * lax.rsqrt(jnp.mean(values * values, axis=-1, keepdims=True) + 1e-06)


def project_kernel(scales_ref, codes_ref, key_ref, value_ref, out_ref, enc_ref):
    step = pl.program_id(0)
    blocks = codes_ref.shape[0]
    for b in range(blocks):
        for g in range(ENC // GROUP):
            cols = slice(g * GROUP, (g + 1) * GROUP)
            scaled = codes_ref[b, :, cols].astype(F32) * scales_ref[step * blocks + b, g]
            enc_ref[b * NBR_LEN : (b + 1) * NBR_LEN, cols] = scaled.astype(BF16)
    enc = enc_ref[...]
    keys = jnp.dot(enc, key_ref[...], preferred_element_type=F32)
    values = jnp.dot(enc, value_ref[...], preferred_element_type=F32).astype(BF16)
    width = key_ref.shape[1]
    for b in range(blocks):
        rows = slice(b * NBR_LEN, (b + 1) * NBR_LEN)
        for h in range(width // HD):
            cols = slice(h * HD, (h + 1) * HD)
            out_ref[b, :, cols] = unit(keys[rows, cols]).astype(BF16)
        out_ref[b, :, width : 2 * width] = values[rows]


def project_blocks(codes, scales, key_weight, value_weight):
    count, width, per = codes.shape[0], key_weight.shape[1], 2
    return pl.pallas_call(
        project_kernel,
        grid=(count // per,),
        out_shape=jax.ShapeDtypeStruct((count, NBR_LEN, 2 * width), BF16),
        in_specs=[
            SMEM,
            pl.BlockSpec((per, NBR_LEN, ENC), lambda i: (i, 0, 0)),
            pl.BlockSpec((ENC, width), lambda i: (0, 0)),
            pl.BlockSpec((ENC, width), lambda i: (0, 0)),
        ],
        out_specs=pl.BlockSpec((per, NBR_LEN, 2 * width), lambda i: (i, 0, 0)),
        scratch_shapes=[pltpu.VMEM((per * NBR_LEN, ENC), BF16)],
        cost_estimate=pl.CostEstimate(
            flops=2 * count * NBR_LEN * ENC * 2 * width, bytes_accessed=5 << 20, transcendentals=0
        ),
        name="project_blocks",
    )(scales, codes, key_weight, value_weight)


def select_kernel(place_ref, heard_ref, rows_ref, out_ref, sems):
    shards, spans, blocks = out_ref.shape[0], heard_ref.shape[2], rows_ref.shape[0]
    lowest = place_ref[0] * blocks
    copies = []
    for e in range(shards):
        named = [heard_ref[e, n, c] - lowest for n in range(NBRS) for c in range(spans)]
        first, last = jnp.int32(0), jnp.int32(0)
        for up, down in zip(named, reversed(named)):
            last = jnp.where((up >= 0) & (up < blocks), up, last)
            first = jnp.where((down >= 0) & (down < blocks), down, first)
        for s, block in enumerate((first, last)):
            copy = pltpu.make_async_copy(rows_ref.at[block], out_ref.at[e, s], sems.at[e, s])
            copy.start()
            copies.append(copy)
    for copy in copies:
        copy.wait()


def select_blocks(place, heard, rows):
    shards = heard.shape[0]
    return pl.pallas_call(
        select_kernel,
        out_shape=jax.ShapeDtypeStruct((shards, NBRS) + rows.shape[1:], BF16),
        in_specs=[SMEM, SMEM, VMEM],
        out_specs=ANY,
        scratch_shapes=[pltpu.SemaphoreType.DMA((shards, NBRS))],
        cost_estimate=pl.CostEstimate(flops=0, bytes_accessed=9 << 20, transcendentals=0),
        name="select_blocks",
    )(place, heard, rows)


def query_kernel(tokens_ref, weight_ref, out_ref):
    projected = jnp.dot(tokens_ref[...], weight_ref[...], preferred_element_type=F32)
    for h in range(weight_ref.shape[1] // HD):
        cols = slice(h * HD, (h + 1) * HD)
        out_ref[:, cols] = unit(projected[:, cols]).astype(BF16)


def project_queries(tokens, weight):
    rows, depth = tokens.shape
    width, tile = weight.shape[1], 128
    return pl.pallas_call(
        query_kernel,
        grid=(rows // tile,),
        out_shape=jax.ShapeDtypeStruct((rows, width), BF16),
        in_specs=[
            pl.BlockSpec((tile, depth), lambda i: (i, 0)),
            pl.BlockSpec((depth, width), lambda i: (0, 0)),
        ],
        out_specs=pl.BlockSpec((tile, width), lambda i: (i, 0)),
        compiler_params=pltpu.CompilerParams(vmem_limit_bytes=48 << 20),
        cost_estimate=pl.CostEstimate(
            flops=2 * rows * depth * width, bytes_accessed=11 << 20, transcendentals=0
        ),
        name="project_queries",
    )(tokens, weight)


def attend_kernel(first, slot_ref, length_ref, query_ref, rows_ref, out_ref, held_ref, sems):
    spans = slot_ref.shape[0] // NBRS
    count = sems.shape[0] // NBRS
    width = query_ref.shape[1]
    keys = NBRS * NBR_LEN
    factor = 2.0 / math.sqrt(HD)
    copies = []
    for c in range(count):
        for n in range(NBRS):
            copy = pltpu.make_async_copy(
                rows_ref.at[slot_ref[n * spans + first + c]],
                held_ref.at[pl.ds((c * NBRS + n) * NBR_LEN, NBR_LEN)],
                sems.at[c * NBRS + n],
            )
            copy.start()
            copies.append(copy)
    places = lax.broadcasted_iota(jnp.int32, (SPAN, keys), 1)
    group = 4
    for start in range(0, count, group):
        members = [(c, h) for c in range(start, start + group) for h in range(width // HD)]
        for copy in copies[start * NBRS : (start + group) * NBRS]:
            copy.wait()
        raised = []
        for c, h in members:
            scores = lax.dot_general(
                query_ref[c * SPAN : (c + 1) * SPAN, h * HD : (h + 1) * HD],
                held_ref[c * keys : (c + 1) * keys, h * HD : (h + 1) * HD],
                (((1,), (1,)), ((), ())),
                preferred_element_type=F32,
            )
            ends = [length_ref[n * spans + first + c] + n * NBR_LEN for n in range(NBRS)]
            valid = (places < ends[0]) | ((places >= NBR_LEN) & (places < ends[1]))
            raised.append(jnp.where(valid, jnp.exp(scores * factor), 0.0))
        weights = [
            (part * (1.0 / jnp.sum(part, axis=-1, keepdims=True))).astype(BF16) for part in raised
        ]
        for (c, h), part in zip(members, weights):
            cols = slice(width + h * HD, width + (h + 1) * HD)
            result = jnp.dot(
                part, held_ref[c * keys : (c + 1) * keys, cols], preferred_element_type=F32
            )
            out_ref[c * SPAN : (c + 1) * SPAN, h * HD : (h + 1) * HD] = result.astype(BF16)


def attend(part, parts, slot_index, lengths, queries, rows):
    tokens, width = queries.shape[0] // parts, queries.shape[1]
    count = tokens // SPAN
    requests = count * NBRS
    return pl.pallas_call(
        functools.partial(attend_kernel, part * count),
        grid=(1,),
        out_shape=jax.ShapeDtypeStruct((tokens, width), BF16),
        in_specs=[SMEM, SMEM, pl.BlockSpec((tokens, width), lambda i: (part, 0)), ANY],
        out_specs=pl.BlockSpec((tokens, width), lambda i: (0, 0)),
        scratch_shapes=[
            pltpu.VMEM((requests * NBR_LEN, rows.shape[2]), BF16),
            pltpu.SemaphoreType.DMA((requests,)),
        ],
        compiler_params=pltpu.CompilerParams(vmem_limit_bytes=12 << 20),
        cost_estimate=pl.CostEstimate(
            flops=4 * tokens * NBRS * NBR_LEN * width, bytes_accessed=3 << 20, transcendentals=0
        ),
        name="attend",
    )(slot_index, lengths, queries, rows)


def relay_kernel(place_ref, weight_ref, lent_ref):
    here, core = place_ref[0], place_ref[1]
    ring, _, width = lent_ref.shape
    for k in range(ring):
        chip = lax.rem(here + k, ring)
        cols = pl.ds(pl.multiple_of((chip * 2 + 1 - core) * width, width), width)
        lent_ref[k] = weight_ref[:, cols]


def relay(place, weight, ring):
    depth = weight.shape[0]
    return pl.pallas_call(
        relay_kernel,
        out_shape=jax.ShapeDtypeStruct((ring, depth, weight.shape[1] // (2 * ring)), BF16),
        in_specs=[SMEM, VMEM],
        out_specs=VMEM,
        compiler_params=pltpu.CompilerParams(vmem_limit_bytes=8 << 20),
        cost_estimate=pl.CostEstimate(flops=0, bytes_accessed=3 << 20, transcendentals=0),
        name="relay",
    )(place, weight)


def share_kernel(steps, place_ref, own_ref, partner_ref, weight_ref, partner_w_ref, *out_refs):
    here, core = place_ref[0], place_ref[1]
    ring, _, width = partner_w_ref.shape
    for step, ref in zip(steps, out_refs):
        chip = lax.rem(here + step, ring)
        cols = pl.ds(pl.multiple_of((chip * 2 + core) * width, width), width)
        ref[...] = (
            jnp.dot(own_ref[...], weight_ref[:, cols], preferred_element_type=F32)
            + jnp.dot(partner_ref[...], partner_w_ref[step], preferred_element_type=F32)
        ).astype(ref.dtype)


def shares(place, steps, dtype, own, partner, weight, partner_weight):
    rows, width = own.shape
    return pl.pallas_call(
        functools.partial(share_kernel, steps),
        out_shape=[jax.ShapeDtypeStruct((rows, width), dtype)] * len(steps),
        in_specs=[SMEM] + [VMEM] * 4,
        out_specs=[VMEM] * len(steps),
        compiler_params=pltpu.CompilerParams(vmem_limit_bytes=12 << 20),
        cost_estimate=pl.CostEstimate(
            flops=4 * rows * width * width * len(steps), bytes_accessed=4 << 20, transcendentals=0
        ),
        name="shares",
    )(place, own, partner, weight, partner_weight)


def reduce_ring(place, attended, partner_attended, weight, partner_weight, ring):
    up = [(i, (i + 1) % ring) for i in range(ring)]
    down = [(i, (i - 1) % ring) for i in range(ring)]
    far = ring // 2
    chains = [(0, 1, far), (1, -1, far), (0, -1, far - 1), (1, 1, far - 1)]
    held, part = {}, {}
    for half in range(2):
        mine = [(way, first) for rows, way, first in chains if rows == half]
        starts = [way * first % ring for way, first in mine]
        rest = [k for k in range(ring) if k not in starts]
        operands = (attended[half], partner_attended[half], weight, partner_weight)
        begun = shares(place, starts, BF16, *operands)
        held.update({(half, way): begun[i] for i, (way, _) in enumerate(mine)})
        others = shares(place, rest, F32, *operands)
        part.update({(half, k): others[i] for i, k in enumerate(rest)})
    for distance in range(far, 0, -1):
        for half, way, first in chains:
            if distance > first:
                continue
            if distance < first:
                total = held[half, way].astype(F32) + part[half, way * distance % ring]
                held[half, way] = total.astype(BF16)
            held[half, way] = lax.ppermute(held[half, way], "z", up if way == 1 else down)
    out = [
        (part[half, 0] + held[half, 1].astype(F32) + held[half, -1].astype(F32)).astype(BF16)
        for half in range(2)
    ]
    return jnp.concatenate(out, axis=0)


def local(
    tokens,
    query_weight,
    key_weight,
    value_weight,
    out_weight,
    codes,
    scales,
    block_len,
    nbr_owner,
    nbr_block,
):
    width = query_weight.shape[1]
    ring = lax.axis_size("z")
    cores = lax.axis_size("c")
    shards = lax.axis_size(DB)
    here, core = lax.axis_index("z"), lax.axis_index("c")
    swap = [(i, (i + 1) % cores) for i in range(cores)]

    place = jnp.stack([here, core]).astype(jnp.int32)
    spans, blocks = nbr_owner.shape[0], block_len.shape[0]

    block_ids = nbr_owner.T * blocks + nbr_block.T
    notes = jnp.concatenate([block_ids, jnp.pad(block_len, (0, spans - blocks))[None, :]], axis=0)
    notes = jnp.broadcast_to(notes[None], (shards,) + notes.shape)
    notes, tokens = lax.optimization_barrier((notes, tokens))
    heard = lax.all_to_all(notes, DB, split_axis=0, concat_axis=0, tiled=True)
    projected = project_blocks(codes, scales, key_weight, value_weight)

    gathered = lax.all_gather(tokens, ("z", "c"), axis=1, tiled=True)
    sent = select_blocks(lax.axis_index(DB).astype(jnp.int32).reshape(1), heard, projected)
    rows = lax.all_to_all(sent, DB, split_axis=0, concat_axis=0, tiled=True)
    rows = rows.reshape(shards * NBRS, NBR_LEN, 2 * width)

    owners = nbr_owner.T.reshape(-1)
    block_ids = block_ids.reshape(-1)
    order = jnp.arange(owners.shape[0], dtype=jnp.int32)
    earlier = jnp.sum(
        ((owners[:, None] == owners[None, :]) & (order[:, None] > order[None, :])).astype(jnp.int32),
        axis=1,
    )
    slot_index = owners * NBRS + earlier
    all_lengths = heard[:, NBRS, :blocks].reshape(-1)
    ids = jnp.arange(all_lengths.shape[0], dtype=jnp.int32)
    lengths = jnp.sum(
        jnp.where(block_ids[:, None] == ids[None, :], all_lengths[None, :], 0), axis=1
    )

    partner_weight = lax.ppermute(relay(place, out_weight, ring), "c", swap)
    queries = project_queries(gathered, query_weight)
    attended = [attend(part, 2, slot_index, lengths, queries, rows) for part in range(2)]
    partner_attended = [lax.ppermute(part, "c", swap) for part in attended]
    return reduce_ring(place, attended, partner_attended, out_weight, partner_weight, ring)


def solution(mesh):
    grid = Mesh(mesh.devices.reshape(4, 4, 8, 2), ("y", "x", "z", "c"))
    head = ("z", "c")
    placed = (
        P(DB, head),
        P(None, head),
        P(None, head),
        P(None, head),
        P(head, None),
        P(DB, None, None),
        P(DB, None),
        P(DB),
        P(DB, None),
        P(DB, None),
    )
    return jax.shard_map(
        local, mesh=grid, in_specs=placed, out_specs=P(DB, head), check_vma=False
    )
```

```python
import functools
import math

import jax
import jax.numpy as jnp
from jax import lax
from jax.experimental import pallas as pl
from jax.experimental.pallas import tpu as pltpu
from jax.sharding import Mesh
from jax.sharding import PartitionSpec as P

HD = 128
ENC = 896
GROUP = 128
SPAN = 64
NBR_LEN = 128
NBRS = 2
DB = ("y", "x")
F32 = jnp.float32
BF16 = jnp.bfloat16
VMEM = pl.BlockSpec(memory_space=pltpu.VMEM)
SMEM = pl.BlockSpec(memory_space=pltpu.SMEM)
ANY = pl.BlockSpec(memory_space=pl.ANY)


def unit(values):
    return values * lax.rsqrt(jnp.mean(values * values, axis=-1, keepdims=True) + 1e-06)


def project_kernel(scales_ref, codes_ref, key_ref, value_ref, out_ref, enc_ref):
    step = pl.program_id(0)
    blocks = codes_ref.shape[0]
    for b in range(blocks):
        for g in range(ENC // GROUP):
            cols = slice(g * GROUP, (g + 1) * GROUP)
            scaled = codes_ref[b, :, cols].astype(F32) * scales_ref[step * blocks + b, g]
            enc_ref[b * NBR_LEN : (b + 1) * NBR_LEN, cols] = scaled.astype(BF16)
    enc = enc_ref[...]
    keys = jnp.dot(enc, key_ref[...], preferred_element_type=F32)
    values = jnp.dot(enc, value_ref[...], preferred_element_type=F32).astype(BF16)
    width = key_ref.shape[1]
    for b in range(blocks):
        rows = slice(b * NBR_LEN, (b + 1) * NBR_LEN)
        for h in range(width // HD):
            cols = slice(h * HD, (h + 1) * HD)
            out_ref[b, :, cols] = unit(keys[rows, cols]).astype(BF16)
        out_ref[b, :, width : 2 * width] = values[rows]


def project_blocks(codes, scales, key_weight, value_weight):
    count, width, per = codes.shape[0], key_weight.shape[1], 2
    return pl.pallas_call(
        project_kernel,
        grid=(count // per,),
        out_shape=jax.ShapeDtypeStruct((count, NBR_LEN, 2 * width), BF16),
        in_specs=[
            SMEM,
            pl.BlockSpec((per, NBR_LEN, ENC), lambda i: (i, 0, 0)),
            pl.BlockSpec((ENC, width), lambda i: (0, 0)),
            pl.BlockSpec((ENC, width), lambda i: (0, 0)),
        ],
        out_specs=pl.BlockSpec((per, NBR_LEN, 2 * width), lambda i: (i, 0, 0)),
        scratch_shapes=[pltpu.VMEM((per * NBR_LEN, ENC), BF16)],
        cost_estimate=pl.CostEstimate(
            flops=2 * count * NBR_LEN * ENC * 2 * width, bytes_accessed=5 << 20, transcendentals=0
        ),
        name="project_blocks",
    )(scales, codes, key_weight, value_weight)


def select_kernel(place_ref, heard_ref, rows_ref, out_ref, sems):
    shards, spans, blocks = out_ref.shape[0], heard_ref.shape[2], rows_ref.shape[0]
    lowest = place_ref[0] * blocks
    copies = []
    for e in range(shards):
        named = [heard_ref[e, n, c] - lowest for n in range(NBRS) for c in range(spans)]
        first, last = jnp.int32(0), jnp.int32(0)
        for up, down in zip(named, reversed(named)):
            last = jnp.where((up >= 0) & (up < blocks), up, last)
            first = jnp.where((down >= 0) & (down < blocks), down, first)
        for s, block in enumerate((first, last)):
            copy = pltpu.make_async_copy(rows_ref.at[block], out_ref.at[e, s], sems.at[e, s])
            copy.start()
            copies.append(copy)
    for copy in copies:
        copy.wait()


def select_blocks(place, heard, rows):
    shards = heard.shape[0]
    return pl.pallas_call(
        select_kernel,
        out_shape=jax.ShapeDtypeStruct((shards, NBRS) + rows.shape[1:], BF16),
        in_specs=[SMEM, SMEM, VMEM],
        out_specs=ANY,
        scratch_shapes=[pltpu.SemaphoreType.DMA((shards, NBRS))],
        cost_estimate=pl.CostEstimate(flops=0, bytes_accessed=9 << 20, transcendentals=0),
        name="select_blocks",
    )(place, heard, rows)


def query_kernel(place_ref, *refs):
    ring = len(refs) - 4
    weight_ref, partner_ref, own_ref, lent_ref = refs[ring:]
    here, core = place_ref[0], place_ref[1]
    own, lent = None, None
    for k in range(ring):
        chip = lax.rem(here + ring - k, ring)
        part = jnp.dot(refs[k][...], weight_ref[chip, core], preferred_element_type=F32)
        own = part if own is None else own + part
        part = jnp.dot(refs[k][...], partner_ref[chip], preferred_element_type=F32)
        lent = part if lent is None else lent + part
    own_ref[...] = own
    lent_ref[...] = lent


def project_queries(place, pieces, weight, partner_weight):
    rows, depth = pieces[0].shape
    width, tile = weight.shape[-1], 256
    out = jax.ShapeDtypeStruct((rows, width), F32)
    return pl.pallas_call(
        query_kernel,
        grid=(rows // tile,),
        out_shape=(out, out),
        in_specs=[SMEM]
        + [pl.BlockSpec((tile, depth), lambda i: (i, 0)) for _ in pieces]
        + [
            pl.BlockSpec(weight.shape, lambda i: (0, 0, 0, 0)),
            pl.BlockSpec(partner_weight.shape, lambda i: (0, 0, 0)),
        ],
        out_specs=[pl.BlockSpec((tile, width), lambda i: (i, 0))] * 2,
        compiler_params=pltpu.CompilerParams(vmem_limit_bytes=56 << 20),
        cost_estimate=pl.CostEstimate(
            flops=4 * rows * depth * width * len(pieces), bytes_accessed=9 << 20, transcendentals=0
        ),
        name="project_queries",
    )(place, *pieces, weight, partner_weight)


def attend_kernel(
    first, slot_ref, length_ref, own_ref, lent_ref, rows_ref, out_ref, query_ref, held_ref, sems
):
    spans = slot_ref.shape[0] // NBRS
    count = sems.shape[0] // NBRS
    width = out_ref.shape[1]
    keys = NBRS * NBR_LEN
    factor = 2.0 / math.sqrt(HD)
    copies = []
    for c in range(count):
        for n in range(NBRS):
            copy = pltpu.make_async_copy(
                rows_ref.at[slot_ref[n * spans + first + c]],
                held_ref.at[pl.ds((c * NBRS + n) * NBR_LEN, NBR_LEN)],
                sems.at[c * NBRS + n],
            )
            copy.start()
            copies.append(copy)
    for h in range(width // HD):
        cols = slice(h * HD, (h + 1) * HD)
        query_ref[:, cols] = unit(own_ref[:, cols] + lent_ref[:, cols]).astype(BF16)
    places = lax.broadcasted_iota(jnp.int32, (SPAN, keys), 1)
    group = 4
    for start in range(0, count, group):
        members = [(c, h) for c in range(start, start + group) for h in range(width // HD)]
        for copy in copies[start * NBRS : (start + group) * NBRS]:
            copy.wait()
        raised = []
        for c, h in members:
            scores = lax.dot_general(
                query_ref[c * SPAN : (c + 1) * SPAN, h * HD : (h + 1) * HD],
                held_ref[c * keys : (c + 1) * keys, h * HD : (h + 1) * HD],
                (((1,), (1,)), ((), ())),
                preferred_element_type=F32,
            )
            ends = [length_ref[n * spans + first + c] + n * NBR_LEN for n in range(NBRS)]
            valid = (places < ends[0]) | ((places >= NBR_LEN) & (places < ends[1]))
            raised.append(jnp.where(valid, jnp.exp(scores * factor), 0.0))
        weights = [
            (part * (1.0 / jnp.sum(part, axis=-1, keepdims=True))).astype(BF16) for part in raised
        ]
        for (c, h), part in zip(members, weights):
            cols = slice(width + h * HD, width + (h + 1) * HD)
            result = jnp.dot(
                part, held_ref[c * keys : (c + 1) * keys, cols], preferred_element_type=F32
            )
            out_ref[c * SPAN : (c + 1) * SPAN, h * HD : (h + 1) * HD] = result.astype(BF16)


def attend(part, parts, slot_index, lengths, own, lent, rows):
    tokens, width = own.shape[0] // parts, own.shape[1]
    count = tokens // SPAN
    requests = count * NBRS
    return pl.pallas_call(
        functools.partial(attend_kernel, part * count),
        grid=(1,),
        out_shape=jax.ShapeDtypeStruct((tokens, width), BF16),
        in_specs=[SMEM, SMEM] + [pl.BlockSpec((tokens, width), lambda i: (part, 0))] * 2 + [ANY],
        out_specs=pl.BlockSpec((tokens, width), lambda i: (0, 0)),
        scratch_shapes=[
            pltpu.VMEM((tokens, width), BF16),
            pltpu.VMEM((requests * NBR_LEN, rows.shape[2]), BF16),
            pltpu.SemaphoreType.DMA((requests,)),
        ],
        compiler_params=pltpu.CompilerParams(vmem_limit_bytes=56 << 20),
        cost_estimate=pl.CostEstimate(
            flops=4 * tokens * NBRS * NBR_LEN * width, bytes_accessed=3 << 20, transcendentals=0
        ),
        name="attend",
    )(slot_index, lengths, own, lent, rows)


def relay_kernel(place_ref, weight_ref, lent_ref):
    here, core = place_ref[0], place_ref[1]
    ring, _, width = lent_ref.shape
    for k in range(ring):
        chip = lax.rem(here + k, ring)
        cols = pl.ds(pl.multiple_of((chip * 2 + 1 - core) * width, width), width)
        lent_ref[k] = weight_ref[:, cols]


def relay(place, weight, ring):
    depth = weight.shape[0]
    return pl.pallas_call(
        relay_kernel,
        out_shape=jax.ShapeDtypeStruct((ring, depth, weight.shape[1] // (2 * ring)), BF16),
        in_specs=[SMEM, VMEM],
        out_specs=VMEM,
        compiler_params=pltpu.CompilerParams(vmem_limit_bytes=8 << 20),
        cost_estimate=pl.CostEstimate(flops=0, bytes_accessed=3 << 20, transcendentals=0),
        name="relay",
    )(place, weight)


def share_kernel(steps, place_ref, own_ref, partner_ref, weight_ref, partner_w_ref, *out_refs):
    here, core = place_ref[0], place_ref[1]
    ring, _, width = partner_w_ref.shape
    for step, ref in zip(steps, out_refs):
        chip = lax.rem(here + step, ring)
        cols = pl.ds(pl.multiple_of((chip * 2 + core) * width, width), width)
        ref[...] = (
            jnp.dot(own_ref[...], weight_ref[:, cols], preferred_element_type=F32)
            + jnp.dot(partner_ref[...], partner_w_ref[step], preferred_element_type=F32)
        ).astype(ref.dtype)


def shares(place, steps, dtype, own, partner, weight, partner_weight):
    rows, width = own.shape
    return pl.pallas_call(
        functools.partial(share_kernel, steps),
        out_shape=[jax.ShapeDtypeStruct((rows, width), dtype)] * len(steps),
        in_specs=[SMEM] + [VMEM] * 4,
        out_specs=[VMEM] * len(steps),
        compiler_params=pltpu.CompilerParams(vmem_limit_bytes=12 << 20),
        cost_estimate=pl.CostEstimate(
            flops=4 * rows * width * width * len(steps), bytes_accessed=4 << 20, transcendentals=0
        ),
        name="shares",
    )(place, own, partner, weight, partner_weight)


def reduce_ring(place, attended, partner_attended, weight, partner_weight, ring):
    up = [(i, (i + 1) % ring) for i in range(ring)]
    down = [(i, (i - 1) % ring) for i in range(ring)]
    far = ring // 2
    chains = [(0, 1, far), (1, -1, far), (0, -1, far - 1), (1, 1, far - 1)]
    held, part = {}, {}
    for half in range(2):
        mine = [(way, first) for rows, way, first in chains if rows == half]
        starts = [way * first % ring for way, first in mine]
        rest = [k for k in range(ring) if k not in starts]
        operands = (attended[half], partner_attended[half], weight, partner_weight)
        begun = shares(place, starts, BF16, *operands)
        held.update({(half, way): begun[i] for i, (way, _) in enumerate(mine)})
        others = shares(place, rest, F32, *operands)
        part.update({(half, k): others[i] for i, k in enumerate(rest)})
    for distance in range(far, 0, -1):
        for half, way, first in chains:
            if distance > first:
                continue
            if distance < first:
                total = held[half, way].astype(F32) + part[half, way * distance % ring]
                held[half, way] = total.astype(BF16)
            held[half, way] = lax.ppermute(held[half, way], "z", up if way == 1 else down)
    out = [
        (part[half, 0] + held[half, 1].astype(F32) + held[half, -1].astype(F32)).astype(BF16)
        for half in range(2)
    ]
    return jnp.concatenate(out, axis=0)


def local(
    tokens,
    query_weight,
    key_weight,
    value_weight,
    out_weight,
    codes,
    scales,
    block_len,
    nbr_owner,
    nbr_block,
):
    width = query_weight.shape[1]
    ring = lax.axis_size("z")
    cores = lax.axis_size("c")
    shards = lax.axis_size(DB)
    here, core = lax.axis_index("z"), lax.axis_index("c")
    swap = [(i, (i + 1) % cores) for i in range(cores)]

    place = jnp.stack([here, core]).astype(jnp.int32)
    spans, blocks = nbr_owner.shape[0], block_len.shape[0]

    block_ids = nbr_owner.T * blocks + nbr_block.T
    notes = jnp.concatenate([block_ids, jnp.pad(block_len, (0, spans - blocks))[None, :]], axis=0)
    notes = jnp.broadcast_to(notes[None], (shards,) + notes.shape)
    heard = lax.all_to_all(notes, DB, split_axis=0, concat_axis=0, tiled=True)
    projected = project_blocks(codes, scales, key_weight, value_weight)
    sent = select_blocks(lax.axis_index(DB).astype(jnp.int32).reshape(1), heard, projected)
    up = [(i, (i + 1) % ring) for i in range(ring)]
    down = [(i, (i - 1) % ring) for i in range(ring)]
    pieces = {0: tokens, 1: lax.ppermute(tokens, "z", up)}
    pieces[ring - 1] = lax.ppermute(tokens, "z", down)
    sent, pieces[1], pieces[ring - 1] = lax.optimization_barrier(
        (sent, pieces[1], pieces[ring - 1])
    )
    rows = lax.all_to_all(sent, DB, split_axis=0, concat_axis=0, tiled=True)
    rows = rows.reshape(shards * NBRS, NBR_LEN, 2 * width)

    owners = nbr_owner.T.reshape(-1)
    block_ids = block_ids.reshape(-1)
    order = jnp.arange(owners.shape[0], dtype=jnp.int32)
    earlier = jnp.sum(
        ((owners[:, None] == owners[None, :]) & (order[:, None] > order[None, :])).astype(jnp.int32),
        axis=1,
    )
    slot_index = owners * NBRS + earlier
    all_lengths = heard[:, NBRS, :blocks].reshape(-1)
    ids = jnp.arange(all_lengths.shape[0], dtype=jnp.int32)
    lengths = jnp.sum(
        jnp.where(block_ids[:, None] == ids[None, :], all_lengths[None, :], 0), axis=1
    )

    for k in range(2, ring // 2 + 1):
        pieces[k] = lax.ppermute(pieces[k - 1], "z", up)
        if k < ring // 2:
            pieces[ring - k] = lax.ppermute(pieces[ring - k + 1], "z", down)
    by_core = query_weight.reshape(ring, cores, width, width)
    lent_rows = lax.dynamic_index_in_dim(by_core, 1 - core, 1, keepdims=False)
    partner_rows = lax.ppermute(lent_rows, "c", swap)

    partner_weight = lax.ppermute(relay(place, out_weight, ring), "c", swap)

    own, lent = project_queries(place, [pieces[k] for k in range(ring)], by_core, partner_rows)
    lent = lax.ppermute(lent, "c", swap)
    attended = [attend(part, 2, slot_index, lengths, own, lent, rows) for part in range(2)]
    partner_attended = [lax.ppermute(part, "c", swap) for part in attended]
    return reduce_ring(place, attended, partner_attended, out_weight, partner_weight, ring)


def solution(mesh):
    grid = Mesh(mesh.devices.reshape(4, 4, 8, 2), ("y", "x", "z", "c"))
    head = ("z", "c")
    placed = (
        P(DB, head),
        P(None, head),
        P(None, head),
        P(None, head),
        P(head, None),
        P(DB, None, None),
        P(DB, None),
        P(DB),
        P(DB, None),
        P(DB, None),
    )
    return jax.shard_map(
        local, mesh=grid, in_specs=placed, out_specs=P(DB, head), check_vma=False
    )
```

```python
import functools
import math

import jax
import jax.numpy as jnp
from jax import lax
from jax.experimental import pallas as pl
from jax.experimental.pallas import tpu as pltpu
from jax.sharding import Mesh
from jax.sharding import PartitionSpec as P

HD = 128
ENC = 896
GROUP = 128
SPAN = 64
NBR_LEN = 128
NBRS = 2
DB = ("y", "x")
F32 = jnp.float32
BF16 = jnp.bfloat16
VMEM = pl.BlockSpec(memory_space=pltpu.VMEM)
SMEM = pl.BlockSpec(memory_space=pltpu.SMEM)
ANY = pl.BlockSpec(memory_space=pl.ANY)
SMALL = pl.CostEstimate(flops=1024, bytes_accessed=1024, transcendentals=0)


def unit(values):
    return values * lax.rsqrt(jnp.mean(values * values, axis=-1, keepdims=True) + 1e-06)


def project_kernel(scales_ref, codes_ref, key_ref, value_ref, out_ref, enc_ref):
    step = pl.program_id(0)
    blocks = codes_ref.shape[0]
    for b in range(blocks):
        for g in range(ENC // GROUP):
            cols = slice(g * GROUP, (g + 1) * GROUP)
            scaled = codes_ref[b, :, cols].astype(F32) * scales_ref[step * blocks + b, g]
            enc_ref[b * NBR_LEN : (b + 1) * NBR_LEN, cols] = scaled.astype(BF16)
    enc = enc_ref[...]
    keys = jnp.dot(enc, key_ref[...], preferred_element_type=F32)
    values = jnp.dot(enc, value_ref[...], preferred_element_type=F32).astype(BF16)
    width = key_ref.shape[1]
    for b in range(blocks):
        rows = slice(b * NBR_LEN, (b + 1) * NBR_LEN)
        for h in range(width // HD):
            cols = slice(h * HD, (h + 1) * HD)
            out_ref[b, :, cols] = unit(keys[rows, cols]).astype(BF16)
        out_ref[b, :, width : 2 * width] = values[rows]


def project_blocks(codes, scales, key_weight, value_weight):
    count, width, per = codes.shape[0], key_weight.shape[1], 2
    return pl.pallas_call(
        project_kernel,
        grid=(count // per,),
        out_shape=jax.ShapeDtypeStruct((count, NBR_LEN, 2 * width), BF16),
        in_specs=[
            SMEM,
            pl.BlockSpec((per, NBR_LEN, ENC), lambda i: (i, 0, 0)),
            pl.BlockSpec((ENC, width), lambda i: (0, 0)),
            pl.BlockSpec((ENC, width), lambda i: (0, 0)),
        ],
        out_specs=pl.BlockSpec((per, NBR_LEN, 2 * width), lambda i: (i, 0, 0)),
        scratch_shapes=[pltpu.VMEM((per * NBR_LEN, ENC), BF16)],
        cost_estimate=pl.CostEstimate(
            flops=2 * count * NBR_LEN * ENC * 2 * width, bytes_accessed=5 << 20, transcendentals=0
        ),
        name="project_blocks",
    )(scales, codes, key_weight, value_weight)


def select_kernel(place_ref, heard_ref, rows_ref, out_ref, sems):
    shards, spans, blocks = out_ref.shape[0], heard_ref.shape[2], rows_ref.shape[0]
    lowest = place_ref[0] * blocks
    copies = []
    for e in range(shards):
        named = [heard_ref[e, n, c] - lowest for n in range(NBRS) for c in range(spans)]
        first, last = jnp.int32(0), jnp.int32(0)
        for up, down in zip(named, reversed(named)):
            last = jnp.where((up >= 0) & (up < blocks), up, last)
            first = jnp.where((down >= 0) & (down < blocks), down, first)
        for s, block in enumerate((first, last)):
            copy = pltpu.make_async_copy(rows_ref.at[block], out_ref.at[e, s], sems.at[e, s])
            copy.start()
            copies.append(copy)
    for copy in copies:
        copy.wait()


def select_blocks(place, heard, rows):
    shards = heard.shape[0]
    return pl.pallas_call(
        select_kernel,
        out_shape=jax.ShapeDtypeStruct((shards, NBRS) + rows.shape[1:], BF16),
        in_specs=[SMEM, SMEM, VMEM],
        out_specs=ANY,
        scratch_shapes=[pltpu.SemaphoreType.DMA((shards, NBRS))],
        cost_estimate=pl.CostEstimate(flops=0, bytes_accessed=9 << 20, transcendentals=0),
        name="select_blocks",
    )(place, heard, rows)


def query_kernel(place_ref, *refs):
    ring = len(refs) - 4
    weight_ref, partner_ref, own_ref, lent_ref = refs[ring:]
    here, core = place_ref[0], place_ref[1]
    own, lent = None, None
    for k in range(ring):
        chip = lax.rem(here + ring - k, ring)
        part = jnp.dot(refs[k][...], weight_ref[chip, core], preferred_element_type=F32)
        own = part if own is None else own + part
        part = jnp.dot(refs[k][...], partner_ref[chip], preferred_element_type=F32)
        lent = part if lent is None else lent + part
    own_ref[...] = own
    lent_ref[...] = lent


def project_queries(place, pieces, weight, partner_weight):
    rows, depth = pieces[0].shape
    width, tile = weight.shape[-1], 256
    out = jax.ShapeDtypeStruct((rows, width), F32)
    return pl.pallas_call(
        query_kernel,
        grid=(rows // tile,),
        out_shape=(out, out),
        in_specs=[SMEM]
        + [pl.BlockSpec((tile, depth), lambda i: (i, 0)) for _ in pieces]
        + [
            pl.BlockSpec(weight.shape, lambda i: (0, 0, 0, 0)),
            pl.BlockSpec(partner_weight.shape, lambda i: (0, 0, 0)),
        ],
        out_specs=[pl.BlockSpec((tile, width), lambda i: (i, 0))] * 2,
        compiler_params=pltpu.CompilerParams(vmem_limit_bytes=56 << 20),
        cost_estimate=pl.CostEstimate(
            flops=4 * rows * depth * width * len(pieces), bytes_accessed=9 << 20, transcendentals=0
        ),
        name="project_queries",
    )(place, *pieces, weight, partner_weight)


def finish_kernel(own_ref, lent_ref, out_ref):
    for h in range(out_ref.shape[1] // HD):
        cols = slice(h * HD, (h + 1) * HD)
        out_ref[:, cols] = unit(own_ref[:, cols] + lent_ref[:, cols]).astype(BF16)


def finish_queries(own, lent):
    return pl.pallas_call(
        finish_kernel,
        out_shape=jax.ShapeDtypeStruct(own.shape, BF16),
        in_specs=[VMEM, VMEM],
        out_specs=VMEM,
        compiler_params=pltpu.CompilerParams(vmem_limit_bytes=8 << 20),
        cost_estimate=pl.CostEstimate(flops=1 << 20, bytes_accessed=3 << 20, transcendentals=0),
        name="finish_queries",
    )(own, lent)


def attend_kernel(
    part, slot_ref, length_ref, queries_ref, rows_ref, out_ref, query_ref, held_ref, sems, query_sem
):
    spans = slot_ref.shape[0] // NBRS
    count = sems.shape[0] // NBRS
    first = part * count
    query_copy = pltpu.make_async_copy(
        queries_ref.at[pl.ds(first * SPAN, count * SPAN)], query_ref, query_sem
    )
    query_copy.start()
    width = out_ref.shape[1]
    keys = NBRS * NBR_LEN
    factor = 2.0 / math.sqrt(HD)
    copies = []
    for c in range(count):
        for n in range(NBRS):
            copy = pltpu.make_async_copy(
                rows_ref.at[slot_ref[n * spans + first + c]],
                held_ref.at[pl.ds((c * NBRS + n) * NBR_LEN, NBR_LEN)],
                sems.at[c * NBRS + n],
            )
            copy.start()
            copies.append(copy)
    query_copy.wait()
    places = lax.broadcasted_iota(jnp.int32, (SPAN, keys), 1)
    group = 4
    for start in range(0, count, group):
        members = [(c, h) for c in range(start, start + group) for h in range(width // HD)]
        for copy in copies[start * NBRS : (start + group) * NBRS]:
            copy.wait()
        raised = []
        for c, h in members:
            scores = lax.dot_general(
                query_ref[c * SPAN : (c + 1) * SPAN, h * HD : (h + 1) * HD],
                held_ref[c * keys : (c + 1) * keys, h * HD : (h + 1) * HD],
                (((1,), (1,)), ((), ())),
                preferred_element_type=F32,
            )
            ends = [length_ref[n * spans + first + c] + n * NBR_LEN for n in range(NBRS)]
            valid = (places < ends[0]) | ((places >= NBR_LEN) & (places < ends[1]))
            raised.append(jnp.where(valid, jnp.exp(scores * factor), 0.0))
        weights = [
            (part * (1.0 / jnp.sum(part, axis=-1, keepdims=True))).astype(BF16) for part in raised
        ]
        for (c, h), part in zip(members, weights):
            cols = slice(width + h * HD, width + (h + 1) * HD)
            result = jnp.dot(
                part, held_ref[c * keys : (c + 1) * keys, cols], preferred_element_type=F32
            )
            out_ref[c * SPAN : (c + 1) * SPAN, h * HD : (h + 1) * HD] = result.astype(BF16)


def attend(part, parts, slot_index, lengths, queries, rows):
    tokens, width = queries.shape[0] // parts, queries.shape[1]
    requests = tokens // SPAN * NBRS
    return pl.pallas_call(
        functools.partial(attend_kernel, part),
        out_shape=jax.ShapeDtypeStruct((tokens, width), BF16),
        in_specs=[SMEM, SMEM, ANY, ANY],
        out_specs=VMEM,
        scratch_shapes=[
            pltpu.VMEM((tokens, width), BF16),
            pltpu.VMEM((requests * NBR_LEN, rows.shape[2]), BF16),
            pltpu.SemaphoreType.DMA((requests,)),
            pltpu.SemaphoreType.DMA,
        ],
        compiler_params=pltpu.CompilerParams(vmem_limit_bytes=56 << 20),
        cost_estimate=SMALL,
        name="attend",
    )(slot_index, lengths, queries, rows)


def relay_kernel(place_ref, weight_ref, lent_ref):
    here, core = place_ref[0], place_ref[1]
    ring, _, width = lent_ref.shape
    for k in range(ring):
        chip = lax.rem(here + k, ring)
        cols = pl.ds(pl.multiple_of((chip * 2 + 1 - core) * width, width), width)
        lent_ref[k] = weight_ref[:, cols]


def relay(place, weight, ring):
    depth = weight.shape[0]
    return pl.pallas_call(
        relay_kernel,
        out_shape=jax.ShapeDtypeStruct((ring, depth, weight.shape[1] // (2 * ring)), BF16),
        in_specs=[SMEM, VMEM],
        out_specs=VMEM,
        compiler_params=pltpu.CompilerParams(vmem_limit_bytes=8 << 20),
        cost_estimate=pl.CostEstimate(flops=0, bytes_accessed=3 << 20, transcendentals=0),
        name="relay",
    )(place, weight)


def share_kernel(steps, place_ref, own_ref, partner_ref, weight_ref, partner_w_ref, *out_refs):
    here, core = place_ref[0], place_ref[1]
    ring, _, width = partner_w_ref.shape
    for step, ref in zip(steps, out_refs):
        chip = lax.rem(here + step, ring)
        cols = pl.ds(pl.multiple_of((chip * 2 + core) * width, width), width)
        ref[...] = (
            jnp.dot(own_ref[...], weight_ref[:, cols], preferred_element_type=F32)
            + jnp.dot(partner_ref[...], partner_w_ref[step], preferred_element_type=F32)
        ).astype(ref.dtype)


def shares(place, steps, dtype, own, partner, weight, partner_weight):
    rows, width = own.shape
    return pl.pallas_call(
        functools.partial(share_kernel, steps),
        out_shape=[jax.ShapeDtypeStruct((rows, width), dtype)] * len(steps),
        in_specs=[SMEM] + [VMEM] * 4,
        out_specs=[VMEM] * len(steps),
        compiler_params=pltpu.CompilerParams(vmem_limit_bytes=12 << 20),
        cost_estimate=SMALL,
        name="shares",
    )(place, own, partner, weight, partner_weight)


def reduce_ring(place, attended, partner_attended, weight, partner_weight, ring):
    up = [(i, (i + 1) % ring) for i in range(ring)]
    down = [(i, (i - 1) % ring) for i in range(ring)]

    def send(sums, way):
        return lax.ppermute(sums, "z", up if way == 1 else down)

    far = ring // 2
    chains = [(0, 1, far), (1, -1, far), (0, -1, far - 1), (1, 1, far - 1)]
    held, part = {}, {}
    for half in range(2):
        mine = [(way, first) for rows, way, first in chains if rows == half]
        starts = [way * first % ring for way, first in mine]
        rest = [k for k in range(ring) if k not in starts]
        operands = (attended[half], partner_attended[half], weight, partner_weight)
        begun = shares(place, starts, BF16, *operands)
        held.update({(half, way): send(begun[i], way) for i, (way, _) in enumerate(mine)})
        others = shares(place, rest, F32, *operands)
        part.update({(half, k): others[i] for i, k in enumerate(rest)})
    for distance in range(far, 0, -1):
        for half, way, first in chains:
            if distance < first:
                total = held[half, way].astype(F32) + part[half, way * distance % ring]
                held[half, way] = send(total.astype(BF16), way)
    out = [
        (part[half, 0] + held[half, 1].astype(F32) + held[half, -1].astype(F32)).astype(BF16)
        for half in range(2)
    ]
    return jnp.concatenate(out, axis=0)


def local(
    tokens,
    query_weight,
    key_weight,
    value_weight,
    out_weight,
    codes,
    scales,
    block_len,
    nbr_owner,
    nbr_block,
):
    width = query_weight.shape[1]
    ring = lax.axis_size("z")
    cores = lax.axis_size("c")
    shards = lax.axis_size(DB)
    here, core = lax.axis_index("z"), lax.axis_index("c")
    swap = [(i, (i + 1) % cores) for i in range(cores)]

    place = jnp.stack([here, core]).astype(jnp.int32)
    spans, blocks = nbr_owner.shape[0], block_len.shape[0]

    block_ids = nbr_owner.T * blocks + nbr_block.T
    notes = jnp.concatenate([block_ids, jnp.pad(block_len, (0, spans - blocks))[None, :]], axis=0)
    notes = jnp.broadcast_to(notes[None], (shards,) + notes.shape)
    heard = lax.all_to_all(notes, DB, split_axis=0, concat_axis=0, tiled=True)
    projected = project_blocks(codes, scales, key_weight, value_weight)
    sent = select_blocks(lax.axis_index(DB).astype(jnp.int32).reshape(1), heard, projected)
    up = [(i, (i + 1) % ring) for i in range(ring)]
    down = [(i, (i - 1) % ring) for i in range(ring)]
    pieces = {0: tokens, 1: lax.ppermute(tokens, "z", up)}
    pieces[ring - 1] = lax.ppermute(tokens, "z", down)
    sent, pieces[1] = lax.optimization_barrier((sent, pieces[1]))
    _, pieces[ring - 1] = lax.optimization_barrier((sent, pieces[ring - 1]))
    rows = lax.all_to_all(sent, DB, split_axis=0, concat_axis=0, tiled=True)
    rows = rows.reshape(shards * NBRS, NBR_LEN, 2 * width)

    owners = nbr_owner.T.reshape(-1)
    block_ids = block_ids.reshape(-1)
    order = jnp.arange(owners.shape[0], dtype=jnp.int32)
    earlier = jnp.sum(
        ((owners[:, None] == owners[None, :]) & (order[:, None] > order[None, :])).astype(jnp.int32),
        axis=1,
    )
    slot_index = owners * NBRS + earlier
    all_lengths = heard[:, NBRS, :blocks].reshape(-1)
    ids = jnp.arange(all_lengths.shape[0], dtype=jnp.int32)
    lengths = jnp.sum(
        jnp.where(block_ids[:, None] == ids[None, :], all_lengths[None, :], 0), axis=1
    )

    for k in range(2, ring // 2 + 1):
        pieces[k] = lax.ppermute(pieces[k - 1], "z", up)
        if k < ring // 2:
            pieces[ring - k] = lax.ppermute(pieces[ring - k + 1], "z", down)
    by_core = query_weight.reshape(ring, cores, width, width)
    lent_rows = lax.dynamic_index_in_dim(by_core, 1 - core, 1, keepdims=False)
    partner_rows = lax.ppermute(lent_rows, "c", swap)

    partner_weight = lax.ppermute(relay(place, out_weight, ring), "c", swap)

    own, lent = project_queries(place, [pieces[k] for k in range(ring)], by_core, partner_rows)
    lent = lax.ppermute(lent, "c", swap)
    queries = finish_queries(own, lent)

    attended = [attend(part, 2, slot_index, lengths, queries, rows) for part in range(2)]
    partner_attended = [lax.ppermute(part, "c", swap) for part in attended]
    return reduce_ring(place, attended, partner_attended, out_weight, partner_weight, ring)


def solution(mesh):
    grid = Mesh(mesh.devices.reshape(4, 4, 8, 2), ("y", "x", "z", "c"))
    head = ("z", "c")
    placed = (
        P(DB, head),
        P(None, head),
        P(None, head),
        P(None, head),
        P(head, None),
        P(DB, None, None),
        P(DB, None),
        P(DB),
        P(DB, None),
        P(DB, None),
    )
    return jax.shard_map(
        local, mesh=grid, in_specs=placed, out_specs=P(DB, head), check_vma=False
    )
```

```python
import functools
import math

import jax
import jax.numpy as jnp
from jax import lax
from jax.experimental import pallas as pl
from jax.experimental.pallas import tpu as pltpu
from jax.sharding import Mesh
from jax.sharding import PartitionSpec as P

HD = 128
ENC = 896
GROUP = 128
SPAN = 64
NBR_LEN = 128
NBRS = 2
DB = ("y", "x")
F32 = jnp.float32
BF16 = jnp.bfloat16
VMEM = pl.BlockSpec(memory_space=pltpu.VMEM)
SMEM = pl.BlockSpec(memory_space=pltpu.SMEM)
ANY = pl.BlockSpec(memory_space=pl.ANY)
SMALL = pl.CostEstimate(flops=1024, bytes_accessed=1024, transcendentals=0)


def unit(values):
    return values * lax.rsqrt(jnp.mean(values * values, axis=-1, keepdims=True) + 1e-06)


def project_kernel(scales_ref, codes_ref, key_ref, value_ref, out_ref, enc_ref):
    step = pl.program_id(0)
    blocks = codes_ref.shape[0]
    for b in range(blocks):
        for g in range(ENC // GROUP):
            cols = slice(g * GROUP, (g + 1) * GROUP)
            scaled = codes_ref[b, :, cols].astype(F32) * scales_ref[step * blocks + b, g]
            enc_ref[b * NBR_LEN : (b + 1) * NBR_LEN, cols] = scaled.astype(BF16)
    enc = enc_ref[...]
    keys = jnp.dot(enc, key_ref[...], preferred_element_type=F32)
    values = jnp.dot(enc, value_ref[...], preferred_element_type=F32).astype(BF16)
    width = key_ref.shape[1]
    for b in range(blocks):
        rows = slice(b * NBR_LEN, (b + 1) * NBR_LEN)
        for h in range(width // HD):
            cols = slice(h * HD, (h + 1) * HD)
            out_ref[b, :, cols] = unit(keys[rows, cols]).astype(BF16)
        out_ref[b, :, width : 2 * width] = values[rows]


def project_blocks(codes, scales, key_weight, value_weight):
    count, width, per = codes.shape[0], key_weight.shape[1], 2
    return pl.pallas_call(
        project_kernel,
        grid=(count // per,),
        out_shape=jax.ShapeDtypeStruct((count, NBR_LEN, 2 * width), BF16),
        in_specs=[
            SMEM,
            pl.BlockSpec((per, NBR_LEN, ENC), lambda i: (i, 0, 0)),
            pl.BlockSpec((ENC, width), lambda i: (0, 0)),
            pl.BlockSpec((ENC, width), lambda i: (0, 0)),
        ],
        out_specs=pl.BlockSpec((per, NBR_LEN, 2 * width), lambda i: (i, 0, 0)),
        scratch_shapes=[pltpu.VMEM((per * NBR_LEN, ENC), BF16)],
        cost_estimate=pl.CostEstimate(
            flops=2 * count * NBR_LEN * ENC * 2 * width, bytes_accessed=5 << 20, transcendentals=0
        ),
        name="project_blocks",
    )(scales, codes, key_weight, value_weight)


def select_kernel(place_ref, heard_ref, rows_ref, out_ref, sems):
    shards, spans, blocks = out_ref.shape[0], heard_ref.shape[2], rows_ref.shape[0]
    lowest = place_ref[0] * blocks
    copies = []
    for e in range(shards):
        named = [heard_ref[e, n, c] - lowest for n in range(NBRS) for c in range(spans)]
        first, last = jnp.int32(0), jnp.int32(0)
        for up, down in zip(named, reversed(named)):
            last = jnp.where((up >= 0) & (up < blocks), up, last)
            first = jnp.where((down >= 0) & (down < blocks), down, first)
        for s, block in enumerate((first, last)):
            copy = pltpu.make_async_copy(rows_ref.at[block], out_ref.at[e, s], sems.at[e, s])
            copy.start()
            copies.append(copy)
    for copy in copies:
        copy.wait()


def select_blocks(place, heard, rows):
    shards = heard.shape[0]
    return pl.pallas_call(
        select_kernel,
        out_shape=jax.ShapeDtypeStruct((shards, NBRS) + rows.shape[1:], BF16),
        in_specs=[SMEM, SMEM, VMEM],
        out_specs=ANY,
        scratch_shapes=[pltpu.SemaphoreType.DMA((shards, NBRS))],
        cost_estimate=pl.CostEstimate(flops=0, bytes_accessed=9 << 20, transcendentals=0),
        name="select_blocks",
    )(place, heard, rows)


def query_kernel(place_ref, *refs):
    ring = len(refs) - 4
    weight_ref, partner_ref, own_ref, lent_ref = refs[ring:]
    here, core = place_ref[0], place_ref[1]
    own, lent = None, None
    for k in range(ring):
        chip = lax.rem(here + ring - k, ring)
        part = jnp.dot(refs[k][...], weight_ref[chip, core], preferred_element_type=F32)
        own = part if own is None else own + part
        part = jnp.dot(refs[k][...], partner_ref[chip], preferred_element_type=F32)
        lent = part if lent is None else lent + part
    own_ref[...] = own
    lent_ref[...] = lent


def project_queries(place, pieces, weight, partner_weight):
    rows, depth = pieces[0].shape
    width, tile = weight.shape[-1], 256
    out = jax.ShapeDtypeStruct((rows, width), F32)
    return pl.pallas_call(
        query_kernel,
        grid=(rows // tile,),
        out_shape=(out, out),
        in_specs=[SMEM]
        + [pl.BlockSpec((tile, depth), lambda i: (i, 0)) for _ in pieces]
        + [
            pl.BlockSpec(weight.shape, lambda i: (0, 0, 0, 0)),
            pl.BlockSpec(partner_weight.shape, lambda i: (0, 0, 0)),
        ],
        out_specs=[pl.BlockSpec((tile, width), lambda i: (i, 0))] * 2,
        compiler_params=pltpu.CompilerParams(vmem_limit_bytes=56 << 20),
        cost_estimate=pl.CostEstimate(
            flops=4 * rows * depth * width * len(pieces), bytes_accessed=9 << 20, transcendentals=0
        ),
        name="project_queries",
    )(place, *pieces, weight, partner_weight)


def finish_kernel(own_ref, lent_ref, *out_refs):
    for i, out_ref in enumerate(out_refs):
        rows = slice(i * out_ref.shape[0], (i + 1) * out_ref.shape[0])
        for h in range(out_ref.shape[1] // HD):
            cols = slice(h * HD, (h + 1) * HD)
            out_ref[:, cols] = unit(own_ref[rows, cols] + lent_ref[rows, cols]).astype(BF16)


def finish_queries(own, lent, parts):
    rows, width = own.shape
    return pl.pallas_call(
        finish_kernel,
        out_shape=[jax.ShapeDtypeStruct((rows // parts, width), BF16)] * parts,
        in_specs=[VMEM, VMEM],
        out_specs=[VMEM] * parts,
        compiler_params=pltpu.CompilerParams(vmem_limit_bytes=56 << 20),
        cost_estimate=pl.CostEstimate(flops=1 << 20, bytes_accessed=3 << 20, transcendentals=0),
        name="finish_queries",
    )(own, lent)


def attend_kernel(
    part, slot_ref, length_ref, queries_ref, rows_ref, out_ref, query_ref, held_ref, sems, query_sem
):
    spans = slot_ref.shape[0] // NBRS
    count = sems.shape[0] // NBRS
    first = part * count
    query_copy = pltpu.make_async_copy(queries_ref, query_ref, query_sem)
    query_copy.start()
    width = out_ref.shape[1]
    keys = NBRS * NBR_LEN
    factor = 2.0 / math.sqrt(HD)
    copies = []
    for c in range(count):
        for n in range(NBRS):
            copy = pltpu.make_async_copy(
                rows_ref.at[slot_ref[n * spans + first + c]],
                held_ref.at[pl.ds((c * NBRS + n) * NBR_LEN, NBR_LEN)],
                sems.at[c * NBRS + n],
            )
            copy.start()
            copies.append(copy)
    query_copy.wait()
    places = lax.broadcasted_iota(jnp.int32, (SPAN, keys), 1)
    group = 4
    for start in range(0, count, group):
        members = [(c, h) for c in range(start, start + group) for h in range(width // HD)]
        for copy in copies[start * NBRS : (start + group) * NBRS]:
            copy.wait()
        raised = []
        for c, h in members:
            scores = lax.dot_general(
                query_ref[c * SPAN : (c + 1) * SPAN, h * HD : (h + 1) * HD],
                held_ref[c * keys : (c + 1) * keys, h * HD : (h + 1) * HD],
                (((1,), (1,)), ((), ())),
                preferred_element_type=F32,
            )
            ends = [length_ref[n * spans + first + c] + n * NBR_LEN for n in range(NBRS)]
            valid = (places < ends[0]) | ((places >= NBR_LEN) & (places < ends[1]))
            raised.append(jnp.where(valid, jnp.exp(scores * factor), 0.0))
        weights = [
            (part * (1.0 / jnp.sum(part, axis=-1, keepdims=True))).astype(BF16) for part in raised
        ]
        for (c, h), part in zip(members, weights):
            cols = slice(width + h * HD, width + (h + 1) * HD)
            result = jnp.dot(
                part, held_ref[c * keys : (c + 1) * keys, cols], preferred_element_type=F32
            )
            out_ref[c * SPAN : (c + 1) * SPAN, h * HD : (h + 1) * HD] = result.astype(BF16)


def attend(part, slot_index, lengths, queries, rows):
    tokens, width = queries.shape
    requests = tokens // SPAN * NBRS
    return pl.pallas_call(
        functools.partial(attend_kernel, part),
        out_shape=jax.ShapeDtypeStruct((tokens, width), BF16),
        in_specs=[SMEM, SMEM, ANY, ANY],
        out_specs=VMEM,
        scratch_shapes=[
            pltpu.VMEM((tokens, width), BF16),
            pltpu.VMEM((requests * NBR_LEN, rows.shape[2]), BF16),
            pltpu.SemaphoreType.DMA((requests,)),
            pltpu.SemaphoreType.DMA,
        ],
        compiler_params=pltpu.CompilerParams(vmem_limit_bytes=24 << 20),
        cost_estimate=SMALL,
        name="attend",
    )(slot_index, lengths, queries, rows)


def relay_kernel(place_ref, weight_ref, lent_ref):
    here, core = place_ref[0], place_ref[1]
    ring, _, width = lent_ref.shape
    for k in range(ring):
        chip = lax.rem(here + k, ring)
        cols = pl.ds(pl.multiple_of((chip * 2 + 1 - core) * width, width), width)
        lent_ref[k] = weight_ref[:, cols]


def relay(place, weight, ring):
    depth = weight.shape[0]
    return pl.pallas_call(
        relay_kernel,
        out_shape=jax.ShapeDtypeStruct((ring, depth, weight.shape[1] // (2 * ring)), BF16),
        in_specs=[SMEM, VMEM],
        out_specs=VMEM,
        compiler_params=pltpu.CompilerParams(vmem_limit_bytes=8 << 20),
        cost_estimate=pl.CostEstimate(flops=0, bytes_accessed=3 << 20, transcendentals=0),
        name="relay",
    )(place, weight)


def share_kernel(steps, place_ref, own_ref, partner_ref, weight_ref, partner_w_ref, *out_refs):
    here, core = place_ref[0], place_ref[1]
    ring, _, width = partner_w_ref.shape
    for step, ref in zip(steps, out_refs):
        chip = lax.rem(here + step, ring)
        cols = pl.ds(pl.multiple_of((chip * 2 + core) * width, width), width)
        ref[...] = (
            jnp.dot(own_ref[...], weight_ref[:, cols], preferred_element_type=F32)
            + jnp.dot(partner_ref[...], partner_w_ref[step], preferred_element_type=F32)
        ).astype(ref.dtype)


def shares(place, steps, dtype, own, partner, weight, partner_weight):
    rows, width = own.shape
    return pl.pallas_call(
        functools.partial(share_kernel, steps),
        out_shape=[jax.ShapeDtypeStruct((rows, width), dtype)] * len(steps),
        in_specs=[SMEM] + [VMEM] * 4,
        out_specs=[VMEM] * len(steps),
        compiler_params=pltpu.CompilerParams(vmem_limit_bytes=12 << 20),
        cost_estimate=SMALL,
        name="shares",
    )(place, own, partner, weight, partner_weight)


def reduce_ring(place, attended, partner_attended, weight, partner_weight, ring):
    up = [(i, (i + 1) % ring) for i in range(ring)]
    down = [(i, (i - 1) % ring) for i in range(ring)]

    def send(sums, way):
        return lax.ppermute(sums, "z", up if way == 1 else down)

    far = ring // 2
    chains = [(0, 1, far), (1, -1, far), (0, -1, far - 1), (1, 1, far - 1)]
    held, part = {}, {}
    for half in range(2):
        mine = [(way, first) for rows, way, first in chains if rows == half]
        starts = [way * first % ring for way, first in mine]
        rest = [k for k in range(ring) if k not in starts]
        operands = (attended[half], partner_attended[half], weight, partner_weight)
        begun = shares(place, starts, BF16, *operands)
        held.update({(half, way): send(begun[i], way) for i, (way, _) in enumerate(mine)})
        others = shares(place, rest, F32, *operands)
        part.update({(half, k): others[i] for i, k in enumerate(rest)})
    for distance in range(far, 0, -1):
        for half, way, first in chains:
            if distance < first:
                total = held[half, way].astype(F32) + part[half, way * distance % ring]
                held[half, way] = send(total.astype(BF16), way)
    out = [
        (part[half, 0] + held[half, 1].astype(F32) + held[half, -1].astype(F32)).astype(BF16)
        for half in range(2)
    ]
    return jnp.concatenate(out, axis=0)


def local(
    tokens,
    query_weight,
    key_weight,
    value_weight,
    out_weight,
    codes,
    scales,
    block_len,
    nbr_owner,
    nbr_block,
):
    width = query_weight.shape[1]
    ring = lax.axis_size("z")
    cores = lax.axis_size("c")
    shards = lax.axis_size(DB)
    here, core = lax.axis_index("z"), lax.axis_index("c")
    swap = [(i, (i + 1) % cores) for i in range(cores)]

    place = jnp.stack([here, core]).astype(jnp.int32)
    spans, blocks = nbr_owner.shape[0], block_len.shape[0]

    block_ids = nbr_owner.T * blocks + nbr_block.T
    notes = jnp.concatenate([block_ids, jnp.pad(block_len, (0, spans - blocks))[None, :]], axis=0)
    notes = jnp.broadcast_to(notes[None], (shards,) + notes.shape)
    heard = lax.all_to_all(notes, DB, split_axis=0, concat_axis=0, tiled=True)
    projected = project_blocks(codes, scales, key_weight, value_weight)
    sent = select_blocks(lax.axis_index(DB).astype(jnp.int32).reshape(1), heard, projected)
    up = [(i, (i + 1) % ring) for i in range(ring)]
    down = [(i, (i - 1) % ring) for i in range(ring)]
    pieces = {0: tokens, 1: lax.ppermute(tokens, "z", up)}
    pieces[ring - 1] = lax.ppermute(tokens, "z", down)
    sent, pieces[1] = lax.optimization_barrier((sent, pieces[1]))
    _, pieces[ring - 1] = lax.optimization_barrier((sent, pieces[ring - 1]))
    rows = lax.all_to_all(sent, DB, split_axis=0, concat_axis=0, tiled=True)
    rows = rows.reshape(shards * NBRS, NBR_LEN, 2 * width)

    owners = nbr_owner.T.reshape(-1)
    block_ids = block_ids.reshape(-1)
    order = jnp.arange(owners.shape[0], dtype=jnp.int32)
    earlier = jnp.sum(
        ((owners[:, None] == owners[None, :]) & (order[:, None] > order[None, :])).astype(jnp.int32),
        axis=1,
    )
    slot_index = owners * NBRS + earlier
    all_lengths = heard[:, NBRS, :blocks].reshape(-1)
    ids = jnp.arange(all_lengths.shape[0], dtype=jnp.int32)
    lengths = jnp.sum(
        jnp.where(block_ids[:, None] == ids[None, :], all_lengths[None, :], 0), axis=1
    )

    for k in range(2, ring // 2 + 1):
        pieces[k] = lax.ppermute(pieces[k - 1], "z", up)
        if k < ring // 2:
            pieces[ring - k] = lax.ppermute(pieces[ring - k + 1], "z", down)
    by_core = query_weight.reshape(ring, cores, width, width)
    lent_rows = lax.dynamic_index_in_dim(by_core, 1 - core, 1, keepdims=False)
    partner_rows = lax.ppermute(lent_rows, "c", swap)

    partner_weight = lax.ppermute(relay(place, out_weight, ring), "c", swap)

    own, lent = project_queries(place, [pieces[k] for k in range(ring)], by_core, partner_rows)
    lent = lax.ppermute(lent, "c", swap)
    queries = finish_queries(own, lent, 2)
    attended = [attend(part, slot_index, lengths, queries[part], rows) for part in range(2)]
    partner_attended = [lax.ppermute(part, "c", swap) for part in attended]
    return reduce_ring(place, attended, partner_attended, out_weight, partner_weight, ring)


def solution(mesh):
    grid = Mesh(mesh.devices.reshape(4, 4, 8, 2), ("y", "x", "z", "c"))
    head = ("z", "c")
    placed = (
        P(DB, head),
        P(None, head),
        P(None, head),
        P(None, head),
        P(head, None),
        P(DB, None, None),
        P(DB, None),
        P(DB),
        P(DB, None),
        P(DB, None),
    )
    return jax.shard_map(
        local, mesh=grid, in_specs=placed, out_specs=P(DB, head), check_vma=False
    )
```

```python
import functools
import math

import jax
import jax.numpy as jnp
from jax import lax
from jax.experimental import pallas as pl
from jax.experimental.pallas import tpu as pltpu
from jax.sharding import Mesh
from jax.sharding import PartitionSpec as P

HD = 128
ENC = 896
GROUP = 128
SPAN = 64
NBR_LEN = 128
NBRS = 2
DB = ("y", "x")
F32 = jnp.float32
BF16 = jnp.bfloat16
VMEM = pl.BlockSpec(memory_space=pltpu.VMEM)
SMEM = pl.BlockSpec(memory_space=pltpu.SMEM)
ANY = pl.BlockSpec(memory_space=pl.ANY)
SMALL = pl.CostEstimate(flops=1024, bytes_accessed=1024, transcendentals=0)


def unit(values):
    return values * lax.rsqrt(jnp.mean(values * values, axis=-1, keepdims=True) + 1e-06)


def project_kernel(scales_ref, codes_ref, key_ref, value_ref, out_ref, enc_ref):
    step = pl.program_id(0)
    blocks = codes_ref.shape[0]
    for b in range(blocks):
        for g in range(ENC // GROUP):
            cols = slice(g * GROUP, (g + 1) * GROUP)
            scaled = codes_ref[b, :, cols].astype(F32) * scales_ref[step * blocks + b, g]
            enc_ref[b * NBR_LEN : (b + 1) * NBR_LEN, cols] = scaled.astype(BF16)
    enc = enc_ref[...]
    keys = jnp.dot(enc, key_ref[...], preferred_element_type=F32)
    values = jnp.dot(enc, value_ref[...], preferred_element_type=F32).astype(BF16)
    width = key_ref.shape[1]
    for b in range(blocks):
        rows = slice(b * NBR_LEN, (b + 1) * NBR_LEN)
        for h in range(width // HD):
            cols = slice(h * HD, (h + 1) * HD)
            out_ref[b, :, cols] = unit(keys[rows, cols]).astype(BF16)
        out_ref[b, :, width : 2 * width] = values[rows]


def project_blocks(codes, scales, key_weight, value_weight):
    count, width, per = codes.shape[0], key_weight.shape[1], 2
    return pl.pallas_call(
        project_kernel,
        grid=(count // per,),
        out_shape=jax.ShapeDtypeStruct((count, NBR_LEN, 2 * width), BF16),
        in_specs=[
            SMEM,
            pl.BlockSpec((per, NBR_LEN, ENC), lambda i: (i, 0, 0)),
            pl.BlockSpec((ENC, width), lambda i: (0, 0)),
            pl.BlockSpec((ENC, width), lambda i: (0, 0)),
        ],
        out_specs=pl.BlockSpec((per, NBR_LEN, 2 * width), lambda i: (i, 0, 0)),
        scratch_shapes=[pltpu.VMEM((per * NBR_LEN, ENC), BF16)],
        cost_estimate=pl.CostEstimate(
            flops=2 * count * NBR_LEN * ENC * 2 * width, bytes_accessed=5 << 20, transcendentals=0
        ),
        name="project_blocks",
    )(scales, codes, key_weight, value_weight)


def select_kernel(place_ref, heard_ref, rows_ref, out_ref, sems):
    shards, spans, blocks = out_ref.shape[0], heard_ref.shape[2], rows_ref.shape[0]
    lowest = place_ref[0] * blocks
    copies = []
    for e in range(shards):
        named = [heard_ref[e, n, c] - lowest for n in range(NBRS) for c in range(spans)]
        first, last = jnp.int32(0), jnp.int32(0)
        for up, down in zip(named, reversed(named)):
            last = jnp.where((up >= 0) & (up < blocks), up, last)
            first = jnp.where((down >= 0) & (down < blocks), down, first)
        for s, block in enumerate((first, last)):
            copy = pltpu.make_async_copy(rows_ref.at[block], out_ref.at[e, s], sems.at[e, s])
            copy.start()
            copies.append(copy)
    for copy in copies:
        copy.wait()


def select_blocks(place, heard, rows):
    shards = heard.shape[0]
    return pl.pallas_call(
        select_kernel,
        out_shape=jax.ShapeDtypeStruct((shards, NBRS) + rows.shape[1:], BF16),
        in_specs=[SMEM, SMEM, VMEM],
        out_specs=ANY,
        scratch_shapes=[pltpu.SemaphoreType.DMA((shards, NBRS))],
        cost_estimate=pl.CostEstimate(flops=0, bytes_accessed=9 << 20, transcendentals=0),
        name="select_blocks",
    )(place, heard, rows)


def query_kernel(place_ref, *refs):
    ring = len(refs) - 4
    weight_ref, partner_ref, own_ref, lent_ref = refs[ring:]
    here, core = place_ref[0], place_ref[1]
    own, lent = None, None
    for k in range(ring):
        chip = lax.rem(here + ring - k, ring)
        part = jnp.dot(refs[k][...], weight_ref[chip, core], preferred_element_type=F32)
        own = part if own is None else own + part
        part = jnp.dot(refs[k][...], partner_ref[chip], preferred_element_type=F32)
        lent = part if lent is None else lent + part
    own_ref[...] = own
    lent_ref[...] = lent


def project_queries(place, pieces, weight, partner_weight):
    rows, depth = pieces[0].shape
    width, tile = weight.shape[-1], 256
    out = jax.ShapeDtypeStruct((rows, width), F32)
    return pl.pallas_call(
        query_kernel,
        grid=(rows // tile,),
        out_shape=(out, out),
        in_specs=[SMEM]
        + [pl.BlockSpec((tile, depth), lambda i: (i, 0)) for _ in pieces]
        + [
            pl.BlockSpec(weight.shape, lambda i: (0, 0, 0, 0)),
            pl.BlockSpec(partner_weight.shape, lambda i: (0, 0, 0)),
        ],
        out_specs=[pl.BlockSpec((tile, width), lambda i: (i, 0))] * 2,
        compiler_params=pltpu.CompilerParams(vmem_limit_bytes=56 << 20),
        cost_estimate=pl.CostEstimate(
            flops=4 * rows * depth * width * len(pieces), bytes_accessed=9 << 20, transcendentals=0
        ),
        name="project_queries",
    )(place, *pieces, weight, partner_weight)


def finish_kernel(own_ref, lent_ref, out_ref):
    for h in range(out_ref.shape[1] // HD):
        cols = slice(h * HD, (h + 1) * HD)
        out_ref[:, cols] = unit(own_ref[:, cols] + lent_ref[:, cols]).astype(BF16)


def finish_queries(own, lent):
    return pl.pallas_call(
        finish_kernel,
        out_shape=jax.ShapeDtypeStruct(own.shape, BF16),
        in_specs=[VMEM, VMEM],
        out_specs=VMEM,
        compiler_params=pltpu.CompilerParams(vmem_limit_bytes=56 << 20),
        cost_estimate=pl.CostEstimate(flops=1 << 20, bytes_accessed=3 << 20, transcendentals=0),
        name="finish_queries",
    )(own, lent)


def attend_kernel(
    slot_ref, length_ref, queries_ref, rows_ref, out_ref, query_ref, held_ref, sems, query_sem
):
    spans = slot_ref.shape[0] // NBRS
    query_copy = pltpu.make_async_copy(queries_ref, query_ref, query_sem)
    query_copy.start()
    width = out_ref.shape[1]
    keys = NBRS * NBR_LEN
    factor = 2.0 / math.sqrt(HD)
    copies = []
    for c in range(spans):
        for n in range(NBRS):
            copy = pltpu.make_async_copy(
                rows_ref.at[slot_ref[n * spans + c]],
                held_ref.at[pl.ds((c * NBRS + n) * NBR_LEN, NBR_LEN)],
                sems.at[c * NBRS + n],
            )
            copy.start()
            copies.append(copy)
    query_copy.wait()
    places = lax.broadcasted_iota(jnp.int32, (SPAN, keys), 1)
    group = 4
    for start in range(0, spans, group):
        members = [(c, h) for c in range(start, start + group) for h in range(width // HD)]
        for copy in copies[start * NBRS : (start + group) * NBRS]:
            copy.wait()
        raised = []
        for c, h in members:
            scores = lax.dot_general(
                query_ref[c * SPAN : (c + 1) * SPAN, h * HD : (h + 1) * HD],
                held_ref[c * keys : (c + 1) * keys, h * HD : (h + 1) * HD],
                (((1,), (1,)), ((), ())),
                preferred_element_type=F32,
            )
            ends = [length_ref[n * spans + c] + n * NBR_LEN for n in range(NBRS)]
            valid = (places < ends[0]) | ((places >= NBR_LEN) & (places < ends[1]))
            raised.append(jnp.where(valid, jnp.exp(scores * factor), 0.0))
        weights = [
            (part * (1.0 / jnp.sum(part, axis=-1, keepdims=True))).astype(BF16) for part in raised
        ]
        for (c, h), part in zip(members, weights):
            cols = slice(width + h * HD, width + (h + 1) * HD)
            result = jnp.dot(
                part, held_ref[c * keys : (c + 1) * keys, cols], preferred_element_type=F32
            )
            out_ref[c * SPAN : (c + 1) * SPAN, h * HD : (h + 1) * HD] = result.astype(BF16)


def attend(slot_index, lengths, queries, rows):
    tokens, width = queries.shape
    requests = tokens // SPAN * NBRS
    return pl.pallas_call(
        attend_kernel,
        out_shape=jax.ShapeDtypeStruct((tokens, width), BF16),
        in_specs=[SMEM, SMEM, ANY, ANY],
        out_specs=VMEM,
        scratch_shapes=[
            pltpu.VMEM((tokens, width), BF16),
            pltpu.VMEM((requests * NBR_LEN, rows.shape[2]), BF16),
            pltpu.SemaphoreType.DMA((requests,)),
            pltpu.SemaphoreType.DMA,
        ],
        compiler_params=pltpu.CompilerParams(vmem_limit_bytes=24 << 20),
        cost_estimate=SMALL,
        name="attend",
    )(slot_index, lengths, queries, rows)


def relay_kernel(place_ref, weight_ref, lent_ref):
    here, core = place_ref[0], place_ref[1]
    ring, _, width = lent_ref.shape
    for k in range(ring):
        chip = lax.rem(here + k, ring)
        cols = pl.ds(pl.multiple_of((chip * 2 + 1 - core) * width, width), width)
        lent_ref[k] = weight_ref[:, cols]


def relay(place, weight, ring):
    depth = weight.shape[0]
    return pl.pallas_call(
        relay_kernel,
        out_shape=jax.ShapeDtypeStruct((ring, depth, weight.shape[1] // (2 * ring)), BF16),
        in_specs=[SMEM, VMEM],
        out_specs=VMEM,
        compiler_params=pltpu.CompilerParams(vmem_limit_bytes=8 << 20),
        cost_estimate=pl.CostEstimate(flops=0, bytes_accessed=3 << 20, transcendentals=0),
        name="relay",
    )(place, weight)


def share_kernel(parts, place_ref, own_ref, partner_ref, weight_ref, partner_w_ref, *out_refs):
    here, core = place_ref[0], place_ref[1]
    ring, _, width = partner_w_ref.shape
    for (half, step), ref in zip(parts, out_refs):
        chip = lax.rem(here + step, ring)
        cols = pl.ds(pl.multiple_of((chip * 2 + core) * width, width), width)
        rows = slice(half * ref.shape[0], (half + 1) * ref.shape[0])
        ref[...] = (
            jnp.dot(own_ref[rows], weight_ref[:, cols], preferred_element_type=F32)
            + jnp.dot(partner_ref[rows], partner_w_ref[step], preferred_element_type=F32)
        ).astype(ref.dtype)


def shares(place, parts, dtype, own, partner, weight, partner_weight):
    rows, width = own.shape[0] // 2, own.shape[1]
    made = pl.pallas_call(
        functools.partial(share_kernel, parts),
        out_shape=[jax.ShapeDtypeStruct((rows, width), dtype)] * len(parts),
        in_specs=[SMEM] + [VMEM] * 4,
        out_specs=[VMEM] * len(parts),
        compiler_params=pltpu.CompilerParams(vmem_limit_bytes=12 << 20),
        cost_estimate=SMALL,
        name="shares",
    )(place, own, partner, weight, partner_weight)
    return dict(zip(parts, made))


def total_kernel(*refs):
    *in_refs, out_ref = refs
    rows = in_refs[0].shape[0]
    for half in range(2):
        part_ref, one_ref, other_ref = in_refs[half], in_refs[2 + half], in_refs[4 + half]
        total = part_ref[...] + one_ref[...].astype(F32) + other_ref[...].astype(F32)
        out_ref[half * rows : (half + 1) * rows] = total.astype(BF16)


def total_rows(parts, sums):
    rows, width = parts[0].shape
    return pl.pallas_call(
        total_kernel,
        out_shape=jax.ShapeDtypeStruct((2 * rows, width), BF16),
        in_specs=[VMEM] * 6,
        out_specs=VMEM,
        compiler_params=pltpu.CompilerParams(vmem_limit_bytes=8 << 20),
        cost_estimate=SMALL,
        name="total_rows",
    )(*parts, *sums)


def reduce_ring(place, attended, partner_attended, weight, partner_weight, ring):
    up = [(i, (i + 1) % ring) for i in range(ring)]
    down = [(i, (i - 1) % ring) for i in range(ring)]
    operands = (attended, partner_attended, weight, partner_weight)
    far = ring // 2
    chains = [(0, 1, far), (1, -1, far), (0, -1, far - 1), (1, 1, far - 1)]
    begun, held = {}, {}
    for pair in (chains[:2], chains[2:]):
        begun.update(shares(place, [(h, w * d % ring) for h, w, d in pair], BF16, *operands))
        for half, way, first in pair:
            sums = begun[half, way * first % ring]
            held[half, way] = lax.ppermute(sums, "z", up if way == 1 else down)
    part = {}
    for half in range(2):
        rest = [(half, k) for k in range(ring) if (half, k) not in begun]
        part.update(shares(place, rest, F32, *operands))
    for distance in range(far - 1, 0, -1):
        for half, way, first in chains:
            if distance < first:
                total = held[half, way].astype(F32) + part[half, way * distance % ring]
                held[half, way] = lax.ppermute(total.astype(BF16), "z", up if way == 1 else down)
    return total_rows([part[half, 0] for half in range(2)], list(held.values()))


def local(
    tokens,
    query_weight,
    key_weight,
    value_weight,
    out_weight,
    codes,
    scales,
    block_len,
    nbr_owner,
    nbr_block,
):
    width = query_weight.shape[1]
    ring = lax.axis_size("z")
    cores = lax.axis_size("c")
    shards = lax.axis_size(DB)
    here, core = lax.axis_index("z"), lax.axis_index("c")
    swap = [(i, (i + 1) % cores) for i in range(cores)]

    place = jnp.stack([here, core]).astype(jnp.int32)
    spans, blocks = nbr_owner.shape[0], block_len.shape[0]

    block_ids = nbr_owner.T * blocks + nbr_block.T
    notes = jnp.concatenate([block_ids, jnp.pad(block_len, (0, spans - blocks))[None, :]], axis=0)
    notes = jnp.broadcast_to(notes[None], (shards,) + notes.shape)
    heard = lax.all_to_all(notes, DB, split_axis=0, concat_axis=0, tiled=True)
    projected = project_blocks(codes, scales, key_weight, value_weight)
    sent = select_blocks(lax.axis_index(DB).astype(jnp.int32).reshape(1), heard, projected)
    up = [(i, (i + 1) % ring) for i in range(ring)]
    down = [(i, (i - 1) % ring) for i in range(ring)]
    pieces = {0: tokens, 1: lax.ppermute(tokens, "z", up)}
    pieces[ring - 1] = lax.ppermute(tokens, "z", down)
    sent, pieces[1] = lax.optimization_barrier((sent, pieces[1]))
    _, pieces[ring - 1] = lax.optimization_barrier((sent, pieces[ring - 1]))
    rows = lax.all_to_all(sent, DB, split_axis=0, concat_axis=0, tiled=True)
    rows = rows.reshape(shards * NBRS, NBR_LEN, 2 * width)

    owners = nbr_owner.T.reshape(-1)
    block_ids = block_ids.reshape(-1)
    order = jnp.arange(owners.shape[0], dtype=jnp.int32)
    earlier = jnp.sum(
        ((owners[:, None] == owners[None, :]) & (order[:, None] > order[None, :])).astype(jnp.int32),
        axis=1,
    )
    slot_index = owners * NBRS + earlier
    all_lengths = heard[:, NBRS, :blocks].reshape(-1)
    ids = jnp.arange(all_lengths.shape[0], dtype=jnp.int32)
    lengths = jnp.sum(
        jnp.where(block_ids[:, None] == ids[None, :], all_lengths[None, :], 0), axis=1
    )

    for k in range(2, ring // 2 + 1):
        pieces[k] = lax.ppermute(pieces[k - 1], "z", up)
        if k < ring // 2:
            pieces[ring - k] = lax.ppermute(pieces[ring - k + 1], "z", down)
    by_core = query_weight.reshape(ring, cores, width, width)
    lent_rows = lax.dynamic_index_in_dim(by_core, 1 - core, 1, keepdims=False)
    partner_rows = lax.ppermute(lent_rows, "c", swap)

    partner_weight = lax.ppermute(relay(place, out_weight, ring), "c", swap)

    own, lent = project_queries(place, [pieces[k] for k in range(ring)], by_core, partner_rows)
    lent = lax.ppermute(lent, "c", swap)
    attended = attend(slot_index, lengths, finish_queries(own, lent), rows)
    partner_attended = lax.ppermute(attended, "c", swap)
    return reduce_ring(place, attended, partner_attended, out_weight, partner_weight, ring)


def solution(mesh):
    grid = Mesh(mesh.devices.reshape(4, 4, 8, 2), ("y", "x", "z", "c"))
    head = ("z", "c")
    placed = (
        P(DB, head),
        P(None, head),
        P(None, head),
        P(None, head),
        P(head, None),
        P(DB, None, None),
        P(DB, None),
        P(DB),
        P(DB, None),
        P(DB, None),
    )
    return jax.shard_map(
        local, mesh=grid, in_specs=placed, out_specs=P(DB, head), check_vma=False
    )
```

```python
import functools
import math

import jax
import jax.numpy as jnp
from jax import lax
from jax.experimental import pallas as pl
from jax.experimental.pallas import tpu as pltpu
from jax.sharding import Mesh
from jax.sharding import PartitionSpec as P

HD = 128
ENC = 896
GROUP = 128
SPAN = 64
NBR_LEN = 128
NBRS = 2
DB = ("y", "x")
LENGTH = 1024
F32 = jnp.float32
BF16 = jnp.bfloat16
VMEM = pl.BlockSpec(memory_space=pltpu.VMEM)
SMEM = pl.BlockSpec(memory_space=pltpu.SMEM)
ANY = pl.BlockSpec(memory_space=pl.ANY)
SMALL = pl.CostEstimate(flops=1024, bytes_accessed=1024, transcendentals=0)


def unit(values):
    return values * lax.rsqrt(jnp.mean(values * values, axis=-1, keepdims=True) + 1e-06)


def project_kernel(scales_ref, codes_ref, key_ref, value_ref, out_ref, enc_ref):
    step = pl.program_id(0)
    blocks = codes_ref.shape[0]
    for b in range(blocks):
        for g in range(ENC // GROUP):
            cols = slice(g * GROUP, (g + 1) * GROUP)
            scaled = codes_ref[b, :, cols].astype(F32) * scales_ref[step * blocks + b, g]
            enc_ref[b * NBR_LEN : (b + 1) * NBR_LEN, cols] = scaled.astype(BF16)
    enc = enc_ref[...]
    keys = jnp.dot(enc, key_ref[...], preferred_element_type=F32)
    values = jnp.dot(enc, value_ref[...], preferred_element_type=F32).astype(BF16)
    width = key_ref.shape[1]
    for b in range(blocks):
        rows = slice(b * NBR_LEN, (b + 1) * NBR_LEN)
        for h in range(width // HD):
            cols = slice(h * HD, (h + 1) * HD)
            out_ref[b, :, cols] = unit(keys[rows, cols]).astype(BF16)
        out_ref[b, :, width : 2 * width] = values[rows]


def project_blocks(codes, scales, key_weight, value_weight):
    count, width, per = codes.shape[0], key_weight.shape[1], 2
    return pl.pallas_call(
        project_kernel,
        grid=(count // per,),
        out_shape=jax.ShapeDtypeStruct((count, NBR_LEN, 2 * width), BF16),
        in_specs=[
            SMEM,
            pl.BlockSpec((per, NBR_LEN, ENC), lambda i: (i, 0, 0)),
            pl.BlockSpec((ENC, width), lambda i: (0, 0)),
            pl.BlockSpec((ENC, width), lambda i: (0, 0)),
        ],
        out_specs=pl.BlockSpec((per, NBR_LEN, 2 * width), lambda i: (i, 0, 0)),
        scratch_shapes=[pltpu.VMEM((per * NBR_LEN, ENC), BF16)],
        cost_estimate=pl.CostEstimate(
            flops=2 * count * NBR_LEN * ENC * 2 * width, bytes_accessed=5 << 20, transcendentals=0
        ),
        name="project_blocks",
    )(scales, codes, key_weight, value_weight)


def select_kernel(place_ref, heard_ref, rows_ref, out_ref, sems):
    shards, spans, blocks = out_ref.shape[0], heard_ref.shape[2], rows_ref.shape[0]
    lowest = place_ref[0] * blocks
    copies = []
    for e in range(shards):
        named = [
            (heard_ref[e, n, c] & (LENGTH - 1) if n == 0 and c < blocks else heard_ref[e, n, c])
            - lowest
            for n in range(NBRS)
            for c in range(spans)
        ]
        first, last = jnp.int32(0), jnp.int32(0)
        for up, down in zip(named, reversed(named)):
            last = jnp.where((up >= 0) & (up < blocks), up, last)
            first = jnp.where((down >= 0) & (down < blocks), down, first)
        for s, block in enumerate((first, last)):
            copy = pltpu.make_async_copy(rows_ref.at[block], out_ref.at[e, s], sems.at[e, s])
            copy.start()
            copies.append(copy)
    for copy in copies:
        copy.wait()


def select_blocks(place, heard, rows):
    shards = heard.shape[0]
    return pl.pallas_call(
        select_kernel,
        out_shape=jax.ShapeDtypeStruct((shards, NBRS) + rows.shape[1:], BF16),
        in_specs=[SMEM, SMEM, VMEM],
        out_specs=ANY,
        scratch_shapes=[pltpu.SemaphoreType.DMA((shards, NBRS))],
        cost_estimate=pl.CostEstimate(flops=0, bytes_accessed=9 << 20, transcendentals=0),
        name="select_blocks",
    )(place, heard, rows)


def query_kernel(place_ref, *refs):
    ring = len(refs) - 4
    weight_ref, partner_ref, own_ref, lent_ref = refs[ring:]
    here, core = place_ref[0], place_ref[1]
    own, lent = None, None
    for k in range(ring):
        chip = lax.rem(here + ring - k, ring)
        part = jnp.dot(refs[k][...], weight_ref[chip, core], preferred_element_type=F32)
        own = part if own is None else own + part
        part = jnp.dot(refs[k][...], partner_ref[chip], preferred_element_type=F32)
        lent = part if lent is None else lent + part
    own_ref[...] = own
    lent_ref[...] = lent


def project_queries(place, pieces, weight, partner_weight):
    rows, depth = pieces[0].shape
    width, tile = weight.shape[-1], 256
    out = jax.ShapeDtypeStruct((rows, width), F32)
    return pl.pallas_call(
        query_kernel,
        grid=(rows // tile,),
        out_shape=(out, out),
        in_specs=[SMEM]
        + [pl.BlockSpec((tile, depth), lambda i: (i, 0)) for _ in pieces]
        + [
            pl.BlockSpec(weight.shape, lambda i: (0, 0, 0, 0)),
            pl.BlockSpec(partner_weight.shape, lambda i: (0, 0, 0)),
        ],
        out_specs=[pl.BlockSpec((tile, width), lambda i: (i, 0))] * 2,
        compiler_params=pltpu.CompilerParams(vmem_limit_bytes=56 << 20),
        cost_estimate=pl.CostEstimate(
            flops=4 * rows * depth * width * len(pieces), bytes_accessed=9 << 20, transcendentals=0
        ),
        name="project_queries",
    )(place, *pieces, weight, partner_weight)


def finish_kernel(own_ref, lent_ref, out_ref):
    for h in range(out_ref.shape[1] // HD):
        cols = slice(h * HD, (h + 1) * HD)
        out_ref[:, cols] = unit(own_ref[:, cols] + lent_ref[:, cols]).astype(BF16)


def finish_queries(own, lent):
    return pl.pallas_call(
        finish_kernel,
        out_shape=jax.ShapeDtypeStruct(own.shape, BF16),
        in_specs=[VMEM, VMEM],
        out_specs=VMEM,
        compiler_params=pltpu.CompilerParams(vmem_limit_bytes=56 << 20),
        cost_estimate=pl.CostEstimate(flops=1 << 20, bytes_accessed=3 << 20, transcendentals=0),
        name="finish_queries",
    )(own, lent)


def attend_kernel(
    slot_ref, length_ref, queries_ref, rows_ref, out_ref, query_ref, held_ref, sems, query_sem
):
    spans = slot_ref.shape[0] // NBRS
    query_copy = pltpu.make_async_copy(queries_ref, query_ref, query_sem)
    query_copy.start()
    width = out_ref.shape[1]
    keys = NBRS * NBR_LEN
    factor = 2.0 / math.sqrt(HD)
    copies = []
    for c in range(spans):
        for n in range(NBRS):
            copy = pltpu.make_async_copy(
                rows_ref.at[slot_ref[n * spans + c]],
                held_ref.at[pl.ds((c * NBRS + n) * NBR_LEN, NBR_LEN)],
                sems.at[c * NBRS + n],
            )
            copy.start()
            copies.append(copy)
    query_copy.wait()
    places = lax.broadcasted_iota(jnp.int32, (SPAN, keys), 1)
    group = 4
    for start in range(0, spans, group):
        members = [(c, h) for c in range(start, start + group) for h in range(width // HD)]
        for copy in copies[start * NBRS : (start + group) * NBRS]:
            copy.wait()
        raised = []
        for c, h in members:
            scores = lax.dot_general(
                query_ref[c * SPAN : (c + 1) * SPAN, h * HD : (h + 1) * HD],
                held_ref[c * keys : (c + 1) * keys, h * HD : (h + 1) * HD],
                (((1,), (1,)), ((), ())),
                preferred_element_type=F32,
            )
            ends = [length_ref[n * spans + c] + n * NBR_LEN for n in range(NBRS)]
            valid = (places < ends[0]) | ((places >= NBR_LEN) & (places < ends[1]))
            raised.append(jnp.where(valid, jnp.exp(scores * factor), 0.0))
        weights = [
            (part * (1.0 / jnp.sum(part, axis=-1, keepdims=True))).astype(BF16) for part in raised
        ]
        for (c, h), part in zip(members, weights):
            cols = slice(width + h * HD, width + (h + 1) * HD)
            result = jnp.dot(
                part, held_ref[c * keys : (c + 1) * keys, cols], preferred_element_type=F32
            )
            out_ref[c * SPAN : (c + 1) * SPAN, h * HD : (h + 1) * HD] = result.astype(BF16)


def attend(slot_index, lengths, queries, rows):
    tokens, width = queries.shape
    requests = tokens // SPAN * NBRS
    return pl.pallas_call(
        attend_kernel,
        out_shape=jax.ShapeDtypeStruct((tokens, width), BF16),
        in_specs=[SMEM, SMEM, ANY, ANY],
        out_specs=VMEM,
        scratch_shapes=[
            pltpu.VMEM((tokens, width), BF16),
            pltpu.VMEM((requests * NBR_LEN, rows.shape[2]), BF16),
            pltpu.SemaphoreType.DMA((requests,)),
            pltpu.SemaphoreType.DMA,
        ],
        compiler_params=pltpu.CompilerParams(vmem_limit_bytes=24 << 20),
        cost_estimate=SMALL,
        name="attend",
    )(slot_index, lengths, queries, rows)


def relay_kernel(place_ref, weight_ref, lent_ref):
    here, core = place_ref[0], place_ref[1]
    ring, _, width = lent_ref.shape
    for k in range(ring):
        chip = lax.rem(here + k, ring)
        cols = pl.ds(pl.multiple_of((chip * 2 + 1 - core) * width, width), width)
        lent_ref[k] = weight_ref[:, cols]


def relay(place, weight, ring):
    depth = weight.shape[0]
    return pl.pallas_call(
        relay_kernel,
        out_shape=jax.ShapeDtypeStruct((ring, depth, weight.shape[1] // (2 * ring)), BF16),
        in_specs=[SMEM, VMEM],
        out_specs=VMEM,
        compiler_params=pltpu.CompilerParams(vmem_limit_bytes=8 << 20),
        cost_estimate=pl.CostEstimate(flops=0, bytes_accessed=3 << 20, transcendentals=0),
        name="relay",
    )(place, weight)


def share_kernel(parts, place_ref, own_ref, partner_ref, weight_ref, partner_w_ref, *out_refs):
    here, core = place_ref[0], place_ref[1]
    ring, _, width = partner_w_ref.shape
    for (half, step), ref in zip(parts, out_refs):
        chip = lax.rem(here + step, ring)
        cols = pl.ds(pl.multiple_of((chip * 2 + core) * width, width), width)
        rows = slice(half * ref.shape[0], (half + 1) * ref.shape[0])
        ref[...] = (
            jnp.dot(own_ref[rows], weight_ref[:, cols], preferred_element_type=F32)
            + jnp.dot(partner_ref[rows], partner_w_ref[step], preferred_element_type=F32)
        ).astype(ref.dtype)


def shares(place, parts, dtype, own, partner, weight, partner_weight):
    rows, width = own.shape[0] // 2, own.shape[1]
    made = pl.pallas_call(
        functools.partial(share_kernel, parts),
        out_shape=[jax.ShapeDtypeStruct((rows, width), dtype)] * len(parts),
        in_specs=[SMEM] + [VMEM] * 4,
        out_specs=[VMEM] * len(parts),
        compiler_params=pltpu.CompilerParams(vmem_limit_bytes=12 << 20),
        cost_estimate=SMALL,
        name="shares",
    )(place, own, partner, weight, partner_weight)
    return dict(zip(parts, made))


def total_kernel(*refs):
    *in_refs, out_ref = refs
    rows = in_refs[0].shape[0]
    for half in range(2):
        part_ref, one_ref, other_ref = in_refs[half], in_refs[2 + half], in_refs[4 + half]
        total = part_ref[...] + one_ref[...].astype(F32) + other_ref[...].astype(F32)
        out_ref[half * rows : (half + 1) * rows] = total.astype(BF16)


def total_rows(parts, sums):
    rows, width = parts[0].shape
    return pl.pallas_call(
        total_kernel,
        out_shape=jax.ShapeDtypeStruct((2 * rows, width), BF16),
        in_specs=[VMEM] * 6,
        out_specs=VMEM,
        compiler_params=pltpu.CompilerParams(vmem_limit_bytes=8 << 20),
        cost_estimate=SMALL,
        name="total_rows",
    )(*parts, *sums)


def reduce_ring(place, attended, partner_attended, weight, partner_weight, ring):
    up = [(i, (i + 1) % ring) for i in range(ring)]
    down = [(i, (i - 1) % ring) for i in range(ring)]
    operands = (attended, partner_attended, weight, partner_weight)
    far = ring // 2
    chains = [(0, 1, far), (1, -1, far), (0, -1, far - 1), (1, 1, far - 1)]
    begun, held = {}, {}
    for pair in (chains[:2], chains[2:]):
        begun.update(shares(place, [(h, w * d % ring) for h, w, d in pair], BF16, *operands))
        for half, way, first in pair:
            sums = begun[half, way * first % ring]
            held[half, way] = lax.ppermute(sums, "z", up if way == 1 else down)
    part = {}
    for distance in range(far - 1, 0, -1):
        rest = [(h, w * distance % ring) for h, w, first in chains if distance < first]
        rest += [(0, 0), (1, 0)] if distance == 1 else []
        part.update(shares(place, rest, F32, *operands))
        own, _ = lax.optimization_barrier((attended, held[0, 1]))
        operands = (own, *operands[1:])
        for half, way, first in chains:
            if distance < first:
                total = held[half, way].astype(F32) + part[half, way * distance % ring]
                held[half, way] = lax.ppermute(total.astype(BF16), "z", up if way == 1 else down)
    return total_rows([part[half, 0] for half in range(2)], list(held.values()))


def local(
    tokens,
    query_weight,
    key_weight,
    value_weight,
    out_weight,
    codes,
    scales,
    block_len,
    nbr_owner,
    nbr_block,
):
    width = query_weight.shape[1]
    ring = lax.axis_size("z")
    cores = lax.axis_size("c")
    shards = lax.axis_size(DB)
    here, core = lax.axis_index("z"), lax.axis_index("c")
    swap = [(i, (i + 1) % cores) for i in range(cores)]

    place = jnp.stack([here, core]).astype(jnp.int32)
    spans, blocks = nbr_owner.shape[0], block_len.shape[0]

    block_ids = nbr_owner.T * blocks + nbr_block.T
    assert shards * blocks <= LENGTH and blocks <= spans
    lengths_here = jnp.pad(block_len[None, :] * LENGTH, ((0, NBRS - 1), (0, spans - blocks)))
    notes = jnp.broadcast_to((block_ids + lengths_here)[None], (shards, NBRS, spans))
    heard = lax.all_to_all(notes, DB, split_axis=0, concat_axis=0, tiled=True)
    projected = project_blocks(codes, scales, key_weight, value_weight)
    sent = select_blocks(lax.axis_index(DB).astype(jnp.int32).reshape(1), heard, projected)
    up = [(i, (i + 1) % ring) for i in range(ring)]
    down = [(i, (i - 1) % ring) for i in range(ring)]
    pieces = {0: tokens, 1: lax.ppermute(tokens, "z", up)}
    pieces[ring - 1] = lax.ppermute(tokens, "z", down)
    sent, pieces[1] = lax.optimization_barrier((sent, pieces[1]))
    _, pieces[ring - 1] = lax.optimization_barrier((sent, pieces[ring - 1]))
    rows = lax.all_to_all(sent, DB, split_axis=0, concat_axis=0, tiled=True)
    rows = rows.reshape(shards * NBRS, NBR_LEN, 2 * width)

    owners = nbr_owner.T.reshape(-1)
    block_ids = block_ids.reshape(-1)
    order = jnp.arange(owners.shape[0], dtype=jnp.int32)
    earlier = jnp.sum(
        ((owners[:, None] == owners[None, :]) & (order[:, None] > order[None, :])).astype(jnp.int32),
        axis=1,
    )
    slot_index = owners * NBRS + earlier
    all_lengths = (heard[:, 0, :blocks] // LENGTH).reshape(-1)
    ids = jnp.arange(all_lengths.shape[0], dtype=jnp.int32)
    lengths = jnp.sum(
        jnp.where(block_ids[:, None] == ids[None, :], all_lengths[None, :], 0), axis=1
    )

    for k in range(2, ring // 2 + 1):
        pieces[k] = lax.ppermute(pieces[k - 1], "z", up)
        if k < ring // 2:
            pieces[ring - k] = lax.ppermute(pieces[ring - k + 1], "z", down)
    by_core = query_weight.reshape(ring, cores, width, width)
    lent_rows = lax.dynamic_index_in_dim(by_core, 1 - core, 1, keepdims=False)
    partner_rows = lax.ppermute(lent_rows, "c", swap)

    partner_weight = lax.ppermute(relay(place, out_weight, ring), "c", swap)

    own, lent = project_queries(place, [pieces[k] for k in range(ring)], by_core, partner_rows)
    lent = lax.ppermute(lent, "c", swap)
    attended = attend(slot_index, lengths, finish_queries(own, lent), rows)
    partner_attended = lax.ppermute(attended, "c", swap)
    return reduce_ring(place, attended, partner_attended, out_weight, partner_weight, ring)


def solution(mesh):
    grid = Mesh(mesh.devices.reshape(4, 4, 8, 2), ("y", "x", "z", "c"))
    head = ("z", "c")
    placed = (
        P(DB, head),
        P(None, head),
        P(None, head),
        P(None, head),
        P(head, None),
        P(DB, None, None),
        P(DB, None),
        P(DB),
        P(DB, None),
        P(DB, None),
    )
    return jax.shard_map(
        local, mesh=grid, in_specs=placed, out_specs=P(DB, head), check_vma=False
    )
```

```python
import functools
import math

import jax
import jax.numpy as jnp
from jax import lax
from jax.experimental import pallas as pl
from jax.experimental.pallas import tpu as pltpu
from jax.sharding import Mesh
from jax.sharding import PartitionSpec as P

HD = 128
ENC = 896
GROUP = 128
SPAN = 64
NBR_LEN = 128
NBRS = 2
DB = ("y", "x")
F32 = jnp.float32
BF16 = jnp.bfloat16
VMEM = pl.BlockSpec(memory_space=pltpu.VMEM)
SMEM = pl.BlockSpec(memory_space=pltpu.SMEM)
ANY = pl.BlockSpec(memory_space=pl.ANY)
SMALL = pl.CostEstimate(flops=1024, bytes_accessed=1024, transcendentals=0)


def unit(values):
    return values * lax.rsqrt(jnp.mean(values * values, axis=-1, keepdims=True) + 1e-06)


def project_kernel(scales_ref, codes_ref, key_ref, value_ref, out_ref, enc_ref):
    step = pl.program_id(0)
    blocks = codes_ref.shape[0]
    for b in range(blocks):
        for g in range(ENC // GROUP):
            cols = slice(g * GROUP, (g + 1) * GROUP)
            scaled = codes_ref[b, :, cols].astype(F32) * scales_ref[step * blocks + b, g]
            enc_ref[b * NBR_LEN : (b + 1) * NBR_LEN, cols] = scaled.astype(BF16)
    enc = enc_ref[...]
    keys = jnp.dot(enc, key_ref[...], preferred_element_type=F32)
    values = jnp.dot(enc, value_ref[...], preferred_element_type=F32).astype(BF16)
    width = key_ref.shape[1]
    for b in range(blocks):
        rows = slice(b * NBR_LEN, (b + 1) * NBR_LEN)
        for h in range(width // HD):
            cols = slice(h * HD, (h + 1) * HD)
            out_ref[b, :, cols] = unit(keys[rows, cols]).astype(BF16)
        out_ref[b, :, width : 2 * width] = values[rows]


def project_blocks(codes, scales, key_weight, value_weight):
    count, width, per = codes.shape[0], key_weight.shape[1], 2
    return pl.pallas_call(
        project_kernel,
        grid=(count // per,),
        out_shape=jax.ShapeDtypeStruct((count, NBR_LEN, 2 * width), BF16),
        in_specs=[
            SMEM,
            pl.BlockSpec((per, NBR_LEN, ENC), lambda i: (i, 0, 0)),
            pl.BlockSpec((ENC, width), lambda i: (0, 0)),
            pl.BlockSpec((ENC, width), lambda i: (0, 0)),
        ],
        out_specs=pl.BlockSpec((per, NBR_LEN, 2 * width), lambda i: (i, 0, 0)),
        scratch_shapes=[pltpu.VMEM((per * NBR_LEN, ENC), BF16)],
        cost_estimate=pl.CostEstimate(
            flops=2 * count * NBR_LEN * ENC * 2 * width, bytes_accessed=5 << 20, transcendentals=0
        ),
        name="project_blocks",
    )(scales, codes, key_weight, value_weight)


def select_kernel(place_ref, heard_ref, rows_ref, out_ref, sems):
    shards, spans, blocks = out_ref.shape[0], heard_ref.shape[2], rows_ref.shape[0]
    lowest = place_ref[0] * blocks
    copies = []
    for e in range(shards):
        named = [heard_ref[e, n, c] - lowest for n in range(NBRS) for c in range(spans)]
        first, last = jnp.int32(0), jnp.int32(0)
        for up, down in zip(named, reversed(named)):
            last = jnp.where((up >= 0) & (up < blocks), up, last)
            first = jnp.where((down >= 0) & (down < blocks), down, first)
        for s, block in enumerate((first, last)):
            copy = pltpu.make_async_copy(rows_ref.at[block], out_ref.at[e, s], sems.at[e, s])
            copy.start()
            copies.append(copy)
    for copy in copies:
        copy.wait()


def select_blocks(place, heard, rows):
    shards = heard.shape[0]
    return pl.pallas_call(
        select_kernel,
        out_shape=jax.ShapeDtypeStruct((shards, NBRS) + rows.shape[1:], BF16),
        in_specs=[SMEM, SMEM, VMEM],
        out_specs=ANY,
        scratch_shapes=[pltpu.SemaphoreType.DMA((shards, NBRS))],
        cost_estimate=pl.CostEstimate(flops=0, bytes_accessed=9 << 20, transcendentals=0),
        name="select_blocks",
    )(place, heard, rows)


def query_kernel(place_ref, *refs):
    ring = len(refs) - 4
    weight_ref, partner_ref, own_ref, lent_ref = refs[ring:]
    here, core = place_ref[0], place_ref[1]
    own, lent = None, None
    for k in range(ring):
        chip = lax.rem(here + ring - k, ring)
        part = jnp.dot(refs[k][...], weight_ref[chip, core], preferred_element_type=F32)
        own = part if own is None else own + part
        part = jnp.dot(refs[k][...], partner_ref[chip], preferred_element_type=F32)
        lent = part if lent is None else lent + part
    own_ref[...] = own
    lent_ref[...] = lent


def project_queries(place, pieces, weight, partner_weight):
    rows, depth = pieces[0].shape
    width, tile = weight.shape[-1], 256
    out = jax.ShapeDtypeStruct((rows, width), F32)
    return pl.pallas_call(
        query_kernel,
        grid=(rows // tile,),
        out_shape=(out, out),
        in_specs=[SMEM]
        + [pl.BlockSpec((tile, depth), lambda i: (i, 0)) for _ in pieces]
        + [
            pl.BlockSpec(weight.shape, lambda i: (0, 0, 0, 0)),
            pl.BlockSpec(partner_weight.shape, lambda i: (0, 0, 0)),
        ],
        out_specs=[pl.BlockSpec((tile, width), lambda i: (i, 0))] * 2,
        compiler_params=pltpu.CompilerParams(vmem_limit_bytes=56 << 20),
        cost_estimate=pl.CostEstimate(
            flops=4 * rows * depth * width * len(pieces), bytes_accessed=9 << 20, transcendentals=0
        ),
        name="project_queries",
    )(place, *pieces, weight, partner_weight)


def finish_kernel(own_ref, lent_ref, out_ref):
    for h in range(out_ref.shape[1] // HD):
        cols = slice(h * HD, (h + 1) * HD)
        out_ref[:, cols] = unit(own_ref[:, cols] + lent_ref[:, cols]).astype(BF16)


def finish_queries(own, lent):
    return pl.pallas_call(
        finish_kernel,
        out_shape=jax.ShapeDtypeStruct(own.shape, BF16),
        in_specs=[VMEM, VMEM],
        out_specs=VMEM,
        compiler_params=pltpu.CompilerParams(vmem_limit_bytes=56 << 20),
        cost_estimate=pl.CostEstimate(flops=1 << 20, bytes_accessed=3 << 20, transcendentals=0),
        name="finish_queries",
    )(own, lent)


def attend_kernel(
    slot_ref, length_ref, queries_ref, rows_ref, out_ref, query_ref, held_ref, sems, query_sem
):
    spans = slot_ref.shape[0] // NBRS
    query_copy = pltpu.make_async_copy(queries_ref, query_ref, query_sem)
    query_copy.start()
    width = out_ref.shape[1]
    keys = NBRS * NBR_LEN
    factor = 2.0 / math.sqrt(HD)
    copies = []
    for c in range(spans):
        for n in range(NBRS):
            copy = pltpu.make_async_copy(
                rows_ref.at[slot_ref[n * spans + c]],
                held_ref.at[pl.ds((c * NBRS + n) * NBR_LEN, NBR_LEN)],
                sems.at[c * NBRS + n],
            )
            copy.start()
            copies.append(copy)
    query_copy.wait()
    places = lax.broadcasted_iota(jnp.int32, (SPAN, keys), 1)
    group = 8
    for start in range(0, spans, group):
        members = [(c, h) for c in range(start, start + group) for h in range(width // HD)]
        for copy in copies[start * NBRS : (start + group) * NBRS]:
            copy.wait()
        raised = []
        for c, h in members:
            scores = lax.dot_general(
                query_ref[c * SPAN : (c + 1) * SPAN, h * HD : (h + 1) * HD],
                held_ref[c * keys : (c + 1) * keys, h * HD : (h + 1) * HD],
                (((1,), (1,)), ((), ())),
                preferred_element_type=F32,
            )
            ends = [length_ref[n * spans + c] + n * NBR_LEN for n in range(NBRS)]
            valid = (places < ends[0]) | ((places >= NBR_LEN) & (places < ends[1]))
            raised.append(jnp.where(valid, jnp.exp(scores * factor), 0.0))
        weights = [
            (part * (1.0 / jnp.sum(part, axis=-1, keepdims=True))).astype(BF16) for part in raised
        ]
        for (c, h), part in zip(members, weights):
            cols = slice(width + h * HD, width + (h + 1) * HD)
            result = jnp.dot(
                part, held_ref[c * keys : (c + 1) * keys, cols], preferred_element_type=F32
            )
            out_ref[c * SPAN : (c + 1) * SPAN, h * HD : (h + 1) * HD] = result.astype(BF16)


def attend(slot_index, lengths, queries, rows):
    tokens, width = queries.shape
    requests = tokens // SPAN * NBRS
    return pl.pallas_call(
        attend_kernel,
        out_shape=jax.ShapeDtypeStruct((tokens, width), BF16),
        in_specs=[SMEM, SMEM, ANY, ANY],
        out_specs=VMEM,
        scratch_shapes=[
            pltpu.VMEM((tokens, width), BF16),
            pltpu.VMEM((requests * NBR_LEN, rows.shape[2]), BF16),
            pltpu.SemaphoreType.DMA((requests,)),
            pltpu.SemaphoreType.DMA,
        ],
        compiler_params=pltpu.CompilerParams(vmem_limit_bytes=24 << 20),
        cost_estimate=SMALL,
        name="attend",
    )(slot_index, lengths, queries, rows)


def relay_kernel(place_ref, weight_ref, lent_ref):
    here, core = place_ref[0], place_ref[1]
    ring, _, width = lent_ref.shape
    for k in range(ring):
        chip = lax.rem(here + k, ring)
        cols = pl.ds(pl.multiple_of((chip * 2 + 1 - core) * width, width), width)
        lent_ref[k] = weight_ref[:, cols]


def relay(place, weight, ring):
    depth = weight.shape[0]
    return pl.pallas_call(
        relay_kernel,
        out_shape=jax.ShapeDtypeStruct((ring, depth, weight.shape[1] // (2 * ring)), BF16),
        in_specs=[SMEM, VMEM],
        out_specs=VMEM,
        compiler_params=pltpu.CompilerParams(vmem_limit_bytes=8 << 20),
        cost_estimate=pl.CostEstimate(flops=0, bytes_accessed=3 << 20, transcendentals=0),
        name="relay",
    )(place, weight)


def share_kernel(parts, place_ref, own_ref, partner_ref, weight_ref, partner_w_ref, *out_refs):
    here, core = place_ref[0], place_ref[1]
    ring, _, width = partner_w_ref.shape
    for (half, step), ref in zip(parts, out_refs):
        chip = lax.rem(here + step, ring)
        cols = pl.ds(pl.multiple_of((chip * 2 + core) * width, width), width)
        rows = slice(half * ref.shape[0], (half + 1) * ref.shape[0])
        ref[...] = (
            jnp.dot(own_ref[rows], weight_ref[:, cols], preferred_element_type=F32)
            + jnp.dot(partner_ref[rows], partner_w_ref[step], preferred_element_type=F32)
        ).astype(ref.dtype)


def shares(place, parts, dtype, own, partner, weight, partner_weight):
    rows, width = own.shape[0] // 2, own.shape[1]
    made = pl.pallas_call(
        functools.partial(share_kernel, parts),
        out_shape=[jax.ShapeDtypeStruct((rows, width), dtype)] * len(parts),
        in_specs=[SMEM] + [VMEM] * 4,
        out_specs=[VMEM] * len(parts),
        compiler_params=pltpu.CompilerParams(vmem_limit_bytes=12 << 20),
        cost_estimate=SMALL,
        name="shares",
    )(place, own, partner, weight, partner_weight)
    return dict(zip(parts, made))


def total_kernel(*refs):
    *in_refs, out_ref = refs
    rows = in_refs[0].shape[0]
    for half in range(2):
        part_ref, one_ref, other_ref = in_refs[half], in_refs[2 + half], in_refs[4 + half]
        total = part_ref[...] + one_ref[...].astype(F32) + other_ref[...].astype(F32)
        out_ref[half * rows : (half + 1) * rows] = total.astype(BF16)


def total_rows(parts, sums):
    rows, width = parts[0].shape
    return pl.pallas_call(
        total_kernel,
        out_shape=jax.ShapeDtypeStruct((2 * rows, width), BF16),
        in_specs=[VMEM] * 6,
        out_specs=VMEM,
        compiler_params=pltpu.CompilerParams(vmem_limit_bytes=8 << 20),
        cost_estimate=SMALL,
        name="total_rows",
    )(*parts, *sums)


def reduce_ring(place, attended, partner_attended, weight, partner_weight, ring):
    up = [(i, (i + 1) % ring) for i in range(ring)]
    down = [(i, (i - 1) % ring) for i in range(ring)]
    operands = (attended, partner_attended, weight, partner_weight)
    far = ring // 2
    chains = [(0, 1, far), (1, -1, far), (0, -1, far - 1), (1, 1, far - 1)]
    begun, held = {}, {}
    for pair in (chains[:2], chains[2:]):
        begun.update(shares(place, [(h, w * d % ring) for h, w, d in pair], BF16, *operands))
        for half, way, first in pair:
            sums = begun[half, way * first % ring]
            held[half, way] = lax.ppermute(sums, "z", up if way == 1 else down)
    part = {}
    for half in range(2):
        rest = [(half, k) for k in range(ring) if (half, k) not in begun]
        part.update(shares(place, rest, F32, *operands))
    for distance in range(far - 1, 0, -1):
        for half, way, first in chains:
            if distance < first:
                total = held[half, way].astype(F32) + part[half, way * distance % ring]
                held[half, way] = lax.ppermute(total.astype(BF16), "z", up if way == 1 else down)
    return total_rows([part[half, 0] for half in range(2)], list(held.values()))


def local(
    tokens,
    query_weight,
    key_weight,
    value_weight,
    out_weight,
    codes,
    scales,
    block_len,
    nbr_owner,
    nbr_block,
):
    width = query_weight.shape[1]
    ring = lax.axis_size("z")
    cores = lax.axis_size("c")
    shards = lax.axis_size(DB)
    here, core = lax.axis_index("z"), lax.axis_index("c")
    swap = [(i, (i + 1) % cores) for i in range(cores)]

    place = jnp.stack([here, core]).astype(jnp.int32)
    spans, blocks = nbr_owner.shape[0], block_len.shape[0]

    block_ids = nbr_owner.T * blocks + nbr_block.T
    notes = jnp.concatenate([block_ids, jnp.pad(block_len, (0, spans - blocks))[None, :]], axis=0)
    notes = jnp.broadcast_to(notes[None], (shards,) + notes.shape)
    heard = lax.all_to_all(notes, DB, split_axis=0, concat_axis=0, tiled=True)
    projected = project_blocks(codes, scales, key_weight, value_weight)
    sent = select_blocks(lax.axis_index(DB).astype(jnp.int32).reshape(1), heard, projected)
    up = [(i, (i + 1) % ring) for i in range(ring)]
    down = [(i, (i - 1) % ring) for i in range(ring)]
    pieces = {0: tokens, 1: lax.ppermute(tokens, "z", up)}
    pieces[ring - 1] = lax.ppermute(tokens, "z", down)
    sent, pieces[1] = lax.optimization_barrier((sent, pieces[1]))
    _, pieces[ring - 1] = lax.optimization_barrier((sent, pieces[ring - 1]))
    rows = lax.all_to_all(sent, DB, split_axis=0, concat_axis=0, tiled=True)
    rows = rows.reshape(shards * NBRS, NBR_LEN, 2 * width)

    owners = nbr_owner.T.reshape(-1)
    block_ids = block_ids.reshape(-1)
    order = jnp.arange(owners.shape[0], dtype=jnp.int32)
    earlier = jnp.sum(
        ((owners[:, None] == owners[None, :]) & (order[:, None] > order[None, :])).astype(jnp.int32),
        axis=1,
    )
    slot_index = owners * NBRS + earlier
    all_lengths = heard[:, NBRS, :blocks].reshape(-1)
    ids = jnp.arange(all_lengths.shape[0], dtype=jnp.int32)
    lengths = jnp.sum(
        jnp.where(block_ids[:, None] == ids[None, :], all_lengths[None, :], 0), axis=1
    )

    for k in range(2, ring // 2 + 1):
        pieces[k] = lax.ppermute(pieces[k - 1], "z", up)
        if k < ring // 2:
            pieces[ring - k] = lax.ppermute(pieces[ring - k + 1], "z", down)
    by_core = query_weight.reshape(ring, cores, width, width)
    lent_rows = lax.dynamic_index_in_dim(by_core, 1 - core, 1, keepdims=False)
    partner_rows = lax.ppermute(lent_rows, "c", swap)

    partner_weight = lax.ppermute(relay(place, out_weight, ring), "c", swap)

    own, lent = project_queries(place, [pieces[k] for k in range(ring)], by_core, partner_rows)
    lent = lax.ppermute(lent, "c", swap)
    attended = attend(slot_index, lengths, finish_queries(own, lent), rows)
    partner_attended = lax.ppermute(attended, "c", swap)
    return reduce_ring(place, attended, partner_attended, out_weight, partner_weight, ring)


def solution(mesh):
    grid = Mesh(mesh.devices.reshape(4, 4, 8, 2), ("y", "x", "z", "c"))
    head = ("z", "c")
    placed = (
        P(DB, head),
        P(None, head),
        P(None, head),
        P(None, head),
        P(head, None),
        P(DB, None, None),
        P(DB, None),
        P(DB),
        P(DB, None),
        P(DB, None),
    )
    return jax.shard_map(
        local, mesh=grid, in_specs=placed, out_specs=P(DB, head), check_vma=False
    )
```

```python
import functools
import math

import jax
import jax.numpy as jnp
from jax import lax
from jax.experimental import pallas as pl
from jax.experimental.pallas import tpu as pltpu
from jax.sharding import Mesh
from jax.sharding import PartitionSpec as P

HD = 128
ENC = 896
GROUP = 128
SPAN = 64
NBR_LEN = 128
NBRS = 2
DB = ("y", "x")
LENGTH = 1024
F32 = jnp.float32
BF16 = jnp.bfloat16
VMEM = pl.BlockSpec(memory_space=pltpu.VMEM)
SMEM = pl.BlockSpec(memory_space=pltpu.SMEM)
ANY = pl.BlockSpec(memory_space=pl.ANY)
SMALL = pl.CostEstimate(flops=1024, bytes_accessed=1024, transcendentals=0)


def unit(values):
    return values * lax.rsqrt(jnp.mean(values * values, axis=-1, keepdims=True) + 1e-06)


def project_kernel(scales_ref, codes_ref, key_ref, value_ref, out_ref, enc_ref):
    step = pl.program_id(0)
    blocks = codes_ref.shape[0]
    for b in range(blocks):
        for g in range(ENC // GROUP):
            cols = slice(g * GROUP, (g + 1) * GROUP)
            scaled = codes_ref[b, :, cols].astype(F32) * scales_ref[step * blocks + b, g]
            enc_ref[b * NBR_LEN : (b + 1) * NBR_LEN, cols] = scaled.astype(BF16)
    enc = enc_ref[...]
    keys = jnp.dot(enc, key_ref[...], preferred_element_type=F32)
    values = jnp.dot(enc, value_ref[...], preferred_element_type=F32).astype(BF16)
    width = key_ref.shape[1]
    for b in range(blocks):
        rows = slice(b * NBR_LEN, (b + 1) * NBR_LEN)
        for h in range(width // HD):
            cols = slice(h * HD, (h + 1) * HD)
            out_ref[b, :, cols] = unit(keys[rows, cols]).astype(BF16)
        out_ref[b, :, width : 2 * width] = values[rows]


def project_blocks(codes, scales, key_weight, value_weight):
    count, width, per = codes.shape[0], key_weight.shape[1], 2
    return pl.pallas_call(
        project_kernel,
        grid=(count // per,),
        out_shape=jax.ShapeDtypeStruct((count, NBR_LEN, 2 * width), BF16),
        in_specs=[
            SMEM,
            pl.BlockSpec((per, NBR_LEN, ENC), lambda i: (i, 0, 0)),
            pl.BlockSpec((ENC, width), lambda i: (0, 0)),
            pl.BlockSpec((ENC, width), lambda i: (0, 0)),
        ],
        out_specs=pl.BlockSpec((per, NBR_LEN, 2 * width), lambda i: (i, 0, 0)),
        scratch_shapes=[pltpu.VMEM((per * NBR_LEN, ENC), BF16)],
        cost_estimate=pl.CostEstimate(
            flops=2 * count * NBR_LEN * ENC * 2 * width, bytes_accessed=5 << 20, transcendentals=0
        ),
        name="project_blocks",
    )(scales, codes, key_weight, value_weight)


def select_kernel(place_ref, heard_ref, rows_ref, out_ref, sems):
    shards, spans, blocks = out_ref.shape[0], heard_ref.shape[2], rows_ref.shape[0]
    lowest = place_ref[0] * blocks
    copies = []
    for e in range(shards):
        named = [
            (heard_ref[e, n, c] & (LENGTH - 1) if n == 0 and c < blocks else heard_ref[e, n, c])
            - lowest
            for n in range(NBRS)
            for c in range(spans)
        ]
        first, last = jnp.int32(0), jnp.int32(0)
        for up, down in zip(named, reversed(named)):
            last = jnp.where((up >= 0) & (up < blocks), up, last)
            first = jnp.where((down >= 0) & (down < blocks), down, first)
        for s, block in enumerate((first, last)):
            copy = pltpu.make_async_copy(rows_ref.at[block], out_ref.at[e, s], sems.at[e, s])
            copy.start()
            copies.append(copy)
    for copy in copies:
        copy.wait()


def select_blocks(place, heard, rows):
    shards = heard.shape[0]
    return pl.pallas_call(
        select_kernel,
        out_shape=jax.ShapeDtypeStruct((shards, NBRS) + rows.shape[1:], BF16),
        in_specs=[SMEM, SMEM, VMEM],
        out_specs=ANY,
        scratch_shapes=[pltpu.SemaphoreType.DMA((shards, NBRS))],
        cost_estimate=pl.CostEstimate(flops=0, bytes_accessed=9 << 20, transcendentals=0),
        name="select_blocks",
    )(place, heard, rows)


def query_kernel(place_ref, *refs):
    ring = len(refs) - 4
    weight_ref, partner_ref, own_ref, lent_ref = refs[ring:]
    here, core = place_ref[0], place_ref[1]
    own, lent = None, None
    for k in range(ring):
        chip = lax.rem(here + ring - k, ring)
        part = jnp.dot(refs[k][...], weight_ref[chip, core], preferred_element_type=F32)
        own = part if own is None else own + part
        part = jnp.dot(refs[k][...], partner_ref[chip], preferred_element_type=F32)
        lent = part if lent is None else lent + part
    own_ref[...] = own
    lent_ref[...] = lent


def project_queries(place, pieces, weight, partner_weight):
    rows, depth = pieces[0].shape
    width, tile = weight.shape[-1], 256
    out = jax.ShapeDtypeStruct((rows, width), F32)
    return pl.pallas_call(
        query_kernel,
        grid=(rows // tile,),
        out_shape=(out, out),
        in_specs=[SMEM]
        + [pl.BlockSpec((tile, depth), lambda i: (i, 0)) for _ in pieces]
        + [
            pl.BlockSpec(weight.shape, lambda i: (0, 0, 0, 0)),
            pl.BlockSpec(partner_weight.shape, lambda i: (0, 0, 0)),
        ],
        out_specs=[pl.BlockSpec((tile, width), lambda i: (i, 0))] * 2,
        compiler_params=pltpu.CompilerParams(vmem_limit_bytes=56 << 20),
        cost_estimate=pl.CostEstimate(
            flops=4 * rows * depth * width * len(pieces), bytes_accessed=9 << 20, transcendentals=0
        ),
        name="project_queries",
    )(place, *pieces, weight, partner_weight)


def finish_kernel(own_ref, lent_ref, out_ref):
    for h in range(out_ref.shape[1] // HD):
        cols = slice(h * HD, (h + 1) * HD)
        out_ref[:, cols] = unit(own_ref[:, cols] + lent_ref[:, cols]).astype(BF16)


def finish_queries(own, lent):
    return pl.pallas_call(
        finish_kernel,
        out_shape=jax.ShapeDtypeStruct(own.shape, BF16),
        in_specs=[VMEM, VMEM],
        out_specs=VMEM,
        compiler_params=pltpu.CompilerParams(vmem_limit_bytes=56 << 20),
        cost_estimate=pl.CostEstimate(flops=1 << 20, bytes_accessed=3 << 20, transcendentals=0),
        name="finish_queries",
    )(own, lent)


def attend_kernel(
    slot_ref, length_ref, queries_ref, rows_ref, out_ref, query_ref, held_ref, sems, query_sem
):
    spans = slot_ref.shape[0] // NBRS
    query_copy = pltpu.make_async_copy(queries_ref, query_ref, query_sem)
    query_copy.start()
    width = out_ref.shape[1]
    keys = NBRS * NBR_LEN
    factor = 2.0 / math.sqrt(HD)
    copies = []
    for c in range(spans):
        for n in range(NBRS):
            copy = pltpu.make_async_copy(
                rows_ref.at[slot_ref[n * spans + c]],
                held_ref.at[pl.ds((c * NBRS + n) * NBR_LEN, NBR_LEN)],
                sems.at[c * NBRS + n],
            )
            copy.start()
            copies.append(copy)
    query_copy.wait()
    places = lax.broadcasted_iota(jnp.int32, (SPAN, keys), 1)
    group = 8
    for start in range(0, spans, group):
        members = [(c, h) for c in range(start, start + group) for h in range(width // HD)]
        for copy in copies[start * NBRS : (start + group) * NBRS]:
            copy.wait()
        raised = []
        for c, h in members:
            scores = lax.dot_general(
                query_ref[c * SPAN : (c + 1) * SPAN, h * HD : (h + 1) * HD],
                held_ref[c * keys : (c + 1) * keys, h * HD : (h + 1) * HD],
                (((1,), (1,)), ((), ())),
                preferred_element_type=F32,
            )
            ends = [length_ref[n * spans + c] + n * NBR_LEN for n in range(NBRS)]
            valid = (places < ends[0]) | ((places >= NBR_LEN) & (places < ends[1]))
            raised.append(jnp.where(valid, jnp.exp(scores * factor), 0.0))
        weights = [
            (part * (1.0 / jnp.sum(part, axis=-1, keepdims=True))).astype(BF16) for part in raised
        ]
        for (c, h), part in zip(members, weights):
            cols = slice(width + h * HD, width + (h + 1) * HD)
            result = jnp.dot(
                part, held_ref[c * keys : (c + 1) * keys, cols], preferred_element_type=F32
            )
            out_ref[c * SPAN : (c + 1) * SPAN, h * HD : (h + 1) * HD] = result.astype(BF16)


def attend(slot_index, lengths, queries, rows):
    tokens, width = queries.shape
    requests = tokens // SPAN * NBRS
    return pl.pallas_call(
        attend_kernel,
        out_shape=jax.ShapeDtypeStruct((tokens, width), BF16),
        in_specs=[SMEM, SMEM, ANY, ANY],
        out_specs=VMEM,
        scratch_shapes=[
            pltpu.VMEM((tokens, width), BF16),
            pltpu.VMEM((requests * NBR_LEN, rows.shape[2]), BF16),
            pltpu.SemaphoreType.DMA((requests,)),
            pltpu.SemaphoreType.DMA,
        ],
        compiler_params=pltpu.CompilerParams(vmem_limit_bytes=24 << 20),
        cost_estimate=SMALL,
        name="attend",
    )(slot_index, lengths, queries, rows)


def relay_kernel(place_ref, weight_ref, lent_ref):
    here, core = place_ref[0], place_ref[1]
    ring, _, width = lent_ref.shape
    for k in range(ring):
        chip = lax.rem(here + k, ring)
        cols = pl.ds(pl.multiple_of((chip * 2 + 1 - core) * width, width), width)
        lent_ref[k] = weight_ref[:, cols]


def relay(place, weight, ring):
    depth = weight.shape[0]
    return pl.pallas_call(
        relay_kernel,
        out_shape=jax.ShapeDtypeStruct((ring, depth, weight.shape[1] // (2 * ring)), BF16),
        in_specs=[SMEM, VMEM],
        out_specs=VMEM,
        compiler_params=pltpu.CompilerParams(vmem_limit_bytes=8 << 20),
        cost_estimate=pl.CostEstimate(flops=0, bytes_accessed=3 << 20, transcendentals=0),
        name="relay",
    )(place, weight)


def share_kernel(parts, place_ref, own_ref, partner_ref, weight_ref, partner_w_ref, *out_refs):
    here, core = place_ref[0], place_ref[1]
    ring, _, width = partner_w_ref.shape
    for (half, step), ref in zip(parts, out_refs):
        chip = lax.rem(here + step, ring)
        cols = pl.ds(pl.multiple_of((chip * 2 + core) * width, width), width)
        rows = slice(half * ref.shape[0], (half + 1) * ref.shape[0])
        ref[...] = (
            jnp.dot(own_ref[rows], weight_ref[:, cols], preferred_element_type=F32)
            + jnp.dot(partner_ref[rows], partner_w_ref[step], preferred_element_type=F32)
        ).astype(ref.dtype)


def shares(place, parts, dtype, own, partner, weight, partner_weight):
    rows, width = own.shape[0] // 2, own.shape[1]
    made = pl.pallas_call(
        functools.partial(share_kernel, parts),
        out_shape=[jax.ShapeDtypeStruct((rows, width), dtype)] * len(parts),
        in_specs=[SMEM] + [VMEM] * 4,
        out_specs=[VMEM] * len(parts),
        compiler_params=pltpu.CompilerParams(vmem_limit_bytes=12 << 20),
        cost_estimate=SMALL,
        name="shares",
    )(place, own, partner, weight, partner_weight)
    return dict(zip(parts, made))


def total_kernel(*refs):
    *in_refs, out_ref = refs
    rows = in_refs[0].shape[0]
    for half in range(2):
        part_ref, one_ref, other_ref = in_refs[half], in_refs[2 + half], in_refs[4 + half]
        total = part_ref[...] + one_ref[...].astype(F32) + other_ref[...].astype(F32)
        out_ref[half * rows : (half + 1) * rows] = total.astype(BF16)


def total_rows(parts, sums):
    rows, width = parts[0].shape
    return pl.pallas_call(
        total_kernel,
        out_shape=jax.ShapeDtypeStruct((2 * rows, width), BF16),
        in_specs=[VMEM] * 6,
        out_specs=VMEM,
        compiler_params=pltpu.CompilerParams(vmem_limit_bytes=8 << 20),
        cost_estimate=SMALL,
        name="total_rows",
    )(*parts, *sums)


def reduce_ring(place, attended, partner_attended, weight, partner_weight, ring):
    up = [(i, (i + 1) % ring) for i in range(ring)]
    down = [(i, (i - 1) % ring) for i in range(ring)]
    operands = (attended, partner_attended, weight, partner_weight)
    far = ring // 2
    chains = [(0, 1, far), (1, -1, far), (0, -1, far - 1), (1, 1, far - 1)]
    begun, held = {}, {}
    for pair in (chains[:2], chains[2:]):
        begun.update(shares(place, [(h, w * d % ring) for h, w, d in pair], BF16, *operands))
        for half, way, first in pair:
            sums = begun[half, way * first % ring]
            held[half, way] = lax.ppermute(sums, "z", up if way == 1 else down)
    part = {}
    for distance in range(far - 1, 0, -1):
        rest = [(h, w * distance % ring) for h, w, first in chains if distance < first]
        rest += [(0, 0), (1, 0)] if distance == 1 else []
        part.update(shares(place, rest, F32, *operands))
        own, _ = lax.optimization_barrier((attended, held[0, 1]))
        operands = (own, *operands[1:])
        for half, way, first in chains:
            if distance < first:
                total = held[half, way].astype(F32) + part[half, way * distance % ring]
                held[half, way] = lax.ppermute(total.astype(BF16), "z", up if way == 1 else down)
    return total_rows([part[half, 0] for half in range(2)], list(held.values()))


def local(
    tokens,
    query_weight,
    key_weight,
    value_weight,
    out_weight,
    codes,
    scales,
    block_len,
    nbr_owner,
    nbr_block,
):
    width = query_weight.shape[1]
    ring = lax.axis_size("z")
    cores = lax.axis_size("c")
    shards = lax.axis_size(DB)
    here, core = lax.axis_index("z"), lax.axis_index("c")
    swap = [(i, (i + 1) % cores) for i in range(cores)]

    place = jnp.stack([here, core]).astype(jnp.int32)
    spans, blocks = nbr_owner.shape[0], block_len.shape[0]

    block_ids = nbr_owner.T * blocks + nbr_block.T
    assert shards * blocks <= LENGTH and blocks <= spans
    lengths_here = jnp.pad(block_len[None, :] * LENGTH, ((0, NBRS - 1), (0, spans - blocks)))
    notes = jnp.broadcast_to((block_ids + lengths_here)[None], (shards, NBRS, spans))
    heard = lax.all_to_all(notes, DB, split_axis=0, concat_axis=0, tiled=True)
    projected = project_blocks(codes, scales, key_weight, value_weight)
    sent = select_blocks(lax.axis_index(DB).astype(jnp.int32).reshape(1), heard, projected)
    up = [(i, (i + 1) % ring) for i in range(ring)]
    down = [(i, (i - 1) % ring) for i in range(ring)]
    pieces = {0: tokens, 1: lax.ppermute(tokens, "z", up)}
    pieces[ring - 1] = lax.ppermute(tokens, "z", down)
    sent, pieces[1] = lax.optimization_barrier((sent, pieces[1]))
    _, pieces[ring - 1] = lax.optimization_barrier((sent, pieces[ring - 1]))
    rows = lax.all_to_all(sent, DB, split_axis=0, concat_axis=0, tiled=True)
    rows = rows.reshape(shards * NBRS, NBR_LEN, 2 * width)

    owners = nbr_owner.T.reshape(-1)
    block_ids = block_ids.reshape(-1)
    order = jnp.arange(owners.shape[0], dtype=jnp.int32)
    earlier = jnp.sum(
        ((owners[:, None] == owners[None, :]) & (order[:, None] > order[None, :])).astype(jnp.int32),
        axis=1,
    )
    slot_index = owners * NBRS + earlier
    all_lengths = (heard[:, 0, :blocks] // LENGTH).reshape(-1)
    ids = jnp.arange(all_lengths.shape[0], dtype=jnp.int32)
    lengths = jnp.sum(
        jnp.where(block_ids[:, None] == ids[None, :], all_lengths[None, :], 0), axis=1
    )

    for k in range(2, ring // 2 + 1):
        pieces[k] = lax.ppermute(pieces[k - 1], "z", up)
        if k < ring // 2:
            pieces[ring - k] = lax.ppermute(pieces[ring - k + 1], "z", down)
    by_core = query_weight.reshape(ring, cores, width, width)
    lent_rows = lax.dynamic_index_in_dim(by_core, 1 - core, 1, keepdims=False)
    partner_rows = lax.ppermute(lent_rows, "c", swap)

    partner_weight = lax.ppermute(relay(place, out_weight, ring), "c", swap)

    own, lent = project_queries(place, [pieces[k] for k in range(ring)], by_core, partner_rows)
    lent = lax.ppermute(lent, "c", swap)
    attended = attend(slot_index, lengths, finish_queries(own, lent), rows)
    partner_attended = lax.ppermute(attended, "c", swap)
    return reduce_ring(place, attended, partner_attended, out_weight, partner_weight, ring)


def solution(mesh):
    grid = Mesh(mesh.devices.reshape(4, 4, 8, 2), ("y", "x", "z", "c"))
    head = ("z", "c")
    placed = (
        P(DB, head),
        P(None, head),
        P(None, head),
        P(None, head),
        P(head, None),
        P(DB, None, None),
        P(DB, None),
        P(DB),
        P(DB, None),
        P(DB, None),
    )
    return jax.shard_map(
        local, mesh=grid, in_specs=placed, out_specs=P(DB, head), check_vma=False
    )
```
